32 devices in a mesh: dp: 8 (over y, x, core), ctx: 4 (over z).
Axes of the slice: x: 2, y: 2, z: 4, core: 2. Of those that a mesh axis runs over, the one named last changes fastest.
Arguments:
- tokens: bfloat16 [8, 1024, 8192], P('dp', 'ctx'), may hold values from -16 to 16
- positions: int32 [1024], replicated, may hold values from 0 to 1023, as said below
- query_weight: float32 [8192, 512], P(('dp', 'ctx')), may hold values from -0.5 to 0.5
- key_weight: float32 [8192, 128], P(('dp', 'ctx')), may hold values from -0.5 to 0.5
- value_weight: float32 [8192, 128], P(('dp', 'ctx')), may hold values from -0.0625 to 0.0625
- grad_output: bfloat16 [8, 1024, 512], P('dp', 'ctx'), may hold values from -6 to 6
Outputs:
- attention: bfloat16 [8, 1024, 512], P('dp', 'ctx')
- grad_tokens: bfloat16 [8, 1024, 8192], P('dp', 'ctx')
- query_grad: float32 [8192, 512], P(('dp', 'ctx'))
- key_grad: float32 [8192, 128], P(('dp', 'ctx'))
- value_grad: float32 [8192, 128], P(('dp', 'ctx'))
The draws below stay inside these ranges and needn't reach their ends.
Inputs may be any that keep to these rules, and one draw needn't show every extreme that they name: Stored rows come in runs of 128; each run holds consecutive increasing positions starting at a multiple of 128; together the runs hold every position of the sequence once.
All inputs are finite; a program needn't handle non-finite values.
Results may differ from the reference program's by a relative error of at most 0.034.
Values may be sent and summed in bfloat16 or wider, within the bound.
No kernel may reach another device: no remote copies, remote signals or barrier semaphores. Data moves between devices by JAX's collectives and lax.ppermute only.
A program may use at most 192 MiB of HBM per device.

```python
import jax
import jax.numpy as jnp
from jax import lax

D = 8192
HD = 128
HQ = 4
BATCH = 8
SEQ = 1024
RUN = 128


def draw_tokens(key, part):
    values_drawn = jax.random.normal(jax.random.fold_in(key, 1), (BATCH, SEQ, D), jnp.float32)
    values_drawn = jnp.clip(values_drawn, -5.0, 5.0)
    return values_drawn.astype(jnp.bfloat16)


def draw_positions(key, part):
    order_runs = jax.random.permutation(jax.random.fold_in(key, 3), SEQ // RUN)
    return (order_runs[:, None] * RUN + jnp.arange(RUN)[None, :]).reshape(SEQ).astype(jnp.int32)


def query_columns(key):
    drawn = jax.random.normal(jax.random.fold_in(key, 7), (D, HQ * HD), jnp.float32)
    return jnp.clip(drawn, -5.0, 5.0) * D ** (-0.5)


def draw_query_weight(key, part):
    return query_columns(key)


def draw_key_weight(key, part):
    fresh = jnp.clip(jax.random.normal(jax.random.fold_in(key, 8), (D, HD), jnp.float32), -5.0, 5.0) * D ** (-0.5)
    return fresh


def block_scale(key, dims, shards, least, largest):
    loudness = 1.0
    for axis_at, shards_of in shards:
        steps = jax.random.uniform(jax.random.fold_in(jax.random.fold_in(key, 6), axis_at), (shards_of,), jnp.float32, least / len(shards), largest / len(shards))
        loudness = loudness * jnp.repeat(jnp.exp(steps), dims[axis_at] // shards_of).reshape((-1,) + (1,) * (len(dims) - 1 - axis_at))
    return loudness


def bell_draw(stream_key, extent, scale, most, split=(), dtype=jnp.bfloat16):
    values = scale * jax.random.normal(stream_key, extent, jnp.float32)
    if split:
        values = values * block_scale(stream_key, extent, split, -0.22, 0.18)
    return jnp.clip(values, -most, most).astype(dtype)


def setup_inputs(seed: int = 0) -> dict:
    splits = jax.random.split(jax.random.key(seed), 7)
    return {
        "tokens": draw_tokens(jax.random.fold_in(splits[6], 71), 0),
        "positions": draw_positions(jax.random.fold_in(splits[6], 71), 0),
        "query_weight": draw_query_weight(jax.random.fold_in(splits[6], 71), 0),
        "key_weight": draw_key_weight(jax.random.fold_in(splits[6], 71), 0),
        "value_weight": bell_draw(splits[4], (D, HD), D ** -0.5, 0.0625, ((0, 32),), jnp.float32),
        "grad_output": bell_draw(splits[5], (BATCH, SEQ, HQ * HD), 1.0, 6.0, ((0, 8), (1, 4))),
    }


ROPE_BASE = 1000000.0
MASKED = -1.0e30


def rope_tables(positions_in, head_dim):
    half_width = head_dim // 2
    exponent = jnp.arange(half_width).astype(jnp.float32) * (2.0 / head_dim)
    frequency = jnp.power(ROPE_BASE, -exponent)
    angles = positions_in.astype(jnp.float32)[:, None] * frequency[None, :]
    angles = jnp.concatenate([angles, angles], axis=1)
    return jnp.cos(angles), jnp.sin(angles)


def rotate(field, cos_table, sin_table):
    half_width = field.shape[-1] // 2
    turned = jnp.concatenate([-field[..., half_width:], field[..., :half_width]], axis=-1)
    return field * cos_table + turned * sin_table


def unrotate(field, cos_table, sin_table):
    half_width = field.shape[-1] // 2
    turned = jnp.concatenate([field[..., half_width:], -field[..., :half_width]], axis=-1)
    return field * cos_table + turned * sin_table


def one_sequence(token_rows, weights_all, grad_rows, row_positions):
    score_scale = HD ** -0.5
    projected = jnp.dot(token_rows, weights_all, preferred_element_type=jnp.float32)
    cos_table, sin_table = rope_tables(row_positions, HD)
    query = projected[:, :HQ * HD].reshape(SEQ, HQ, HD)
    key_part = projected[:, HQ * HD:HQ * HD + HD]
    value_part = projected[:, HQ * HD + HD:]
    query_rot = rotate(query, cos_table[:, None, :], sin_table[:, None, :]).astype(jnp.bfloat16)
    key_rot = rotate(key_part, cos_table, sin_table).astype(jnp.bfloat16)
    value_b = value_part.astype(jnp.bfloat16)
    allowed = row_positions[None, :] <= row_positions[:, None]
    scores = jnp.einsum("qhd,kd->qhk", query_rot.astype(jnp.float32), key_rot.astype(jnp.float32)) * score_scale
    scores = jnp.where(allowed[:, None, :], scores, MASKED)
    row_max = jnp.max(scores, axis=-1)
    weight = jnp.where(allowed[:, None, :], jnp.exp(scores - row_max[..., None]), 0.0)
    denominator = jnp.sum(weight, axis=-1)
    log_total = row_max + jnp.log(denominator)
    weighted = jnp.einsum("qhk,kd->qhd", weight.astype(jnp.bfloat16).astype(jnp.float32), value_b.astype(jnp.float32))
    attention = (weighted / denominator[..., None]).astype(jnp.bfloat16)
    grad_heads = grad_rows.reshape(SEQ, HQ, HD).astype(jnp.float32)
    row_delta = jnp.sum(grad_heads * attention.astype(jnp.float32), axis=-1)
    probs = jnp.where(allowed[:, None, :], jnp.exp(scores - log_total[..., None]), 0.0)
    grad_probs = jnp.einsum("qhd,kd->qhk", grad_heads, value_b.astype(jnp.float32))
    dscore = (probs * (grad_probs - row_delta[..., None])).astype(jnp.bfloat16).astype(jnp.float32)
    probs_b = probs.astype(jnp.bfloat16).astype(jnp.float32)
    grad_query_rot = jnp.einsum("qhk,kd->qhd", dscore, key_rot.astype(jnp.float32)) * score_scale
    grad_key_rot = jnp.einsum("qhk,qhd->kd", dscore, query_rot.astype(jnp.float32)) * score_scale
    grad_value = jnp.einsum("qhk,qhd->kd", probs_b, grad_heads)
    grad_query = unrotate(grad_query_rot, cos_table[:, None, :], sin_table[:, None, :]).reshape(SEQ, HQ * HD)
    grad_key = unrotate(grad_key_rot, cos_table, sin_table)
    grad_proj = jnp.concatenate([grad_query, grad_key, grad_value], axis=1).astype(jnp.bfloat16)
    grad_input = jnp.dot(grad_proj, weights_all.T, preferred_element_type=jnp.float32).astype(jnp.bfloat16)
    grad_term = jnp.dot(token_rows.T, grad_proj, preferred_element_type=jnp.float32)
    return attention.reshape(SEQ, HQ * HD), grad_input, grad_term


def reference(tokens, positions, query_weight, key_weight, value_weight, grad_output):
    weights_all = jnp.concatenate([query_weight, key_weight, value_weight], axis=1).astype(jnp.bfloat16)

    def advance(grad_sum, inputs):
        attention, grad_input, grad_term = one_sequence(inputs[0], weights_all, inputs[1], positions)
        return grad_sum + grad_term, (attention, grad_input)

    initial = jnp.zeros((D, (HQ + 2) * HD), jnp.float32)
    weight_grads, (attention, grad_tokens) = lax.scan(advance, initial, (tokens, grad_output))
    query_grad = weight_grads[:, :HQ * HD]
    key_grad = weight_grads[:, HQ * HD:HQ * HD + HD]
    value_grad = weight_grads[:, HQ * HD + HD:]
    return attention, grad_tokens, query_grad, key_grad, value_grad
```

```python
import functools

import jax
import jax.numpy as jnp
from jax import lax
from jax.experimental import pallas as pl
from jax.experimental.pallas import tpu as pltpu
from jax.sharding import Mesh, PartitionSpec as P

ROPE_BASE = 1000000.0
MASKED = -1e30


def rope_tables(positions_in, head_dim):
    half_width = head_dim // 2
    exponent = jnp.arange(half_width).astype(jnp.float32) * (2.0 / head_dim)
    frequency = jnp.power(ROPE_BASE, -exponent)
    angles = positions_in.astype(jnp.float32)[:, None] * frequency[None, :]
    angles = jnp.concatenate([angles, angles], axis=1)
    return (jnp.cos(angles), jnp.sin(angles))


def mm(a, b, dims):
    return lax.dot_general(a, b, (dims, ((), ())), preferred_element_type=jnp.float32)


def shift(block, axis, step):
    size = lax.axis_size(axis)
    return lax.ppermute(block, axis, [(i, (i + step) % size) for i in range(size)])


def after(block, *others):
    return lax.optimization_barrier((block, *others))[0]


def swap(block):
    return shift(block, "core", 1)


def gather_line(block):
    return [block] + [shift(block, "ctx", k) for k in range(1, lax.axis_size("ctx"))]


def along(block, axis):
    return [shift(block, axis, step) for step in range(1, lax.axis_size(axis))]


def gather_corners(sides_a, sides_b, way, *deps):
    corners = {}
    for da, side_a in enumerate(sides_a, 1):
        for db, side_b in enumerate(sides_b, 1):
            mid = side_a.shape[0] // 2
            if way == "b":
                corners[da, db] = [shift(after(side_a, *deps), "b", db)]
            elif way == "a":
                corners[da, db] = [shift(after(side_b, *deps), "a", da)]
            else:
                corners[da, db] = [
                    shift(after(side_a[:mid], *deps), "b", db),
                    shift(after(side_b[mid:], *deps), "a", da),
                ]
    return corners


def in_order(block, sides_a, sides_b, corners):
    slabs = [[block]] + [[side] for side in sides_b]
    for da, side in enumerate(sides_a, 1):
        slabs.append([side])
        slabs += [corners[da, db] for db in range(1, len(sides_b) + 1)]
    return slabs


def reduce_corners(make, way, split, *deps):
    size_b = lax.axis_size("b")
    whole, top, low = slice(None), slice(0, split), slice(split, None)
    came_a, came_b = {}, {}
    for da in range(1, lax.axis_size("a")):
        for db in range(1, size_b):
            i = da * size_b + db
            if way == "b":
                came_a[da, db] = shift(make(i, whole, deps), "b", -db)
            elif way == "a":
                came_b[da, db] = shift(make(i, whole, deps), "a", -da)
            else:
                came_a[da, db] = shift(make(i, top, deps), "b", -db)
                came_b[da, db] = shift(make(i, low, deps), "a", -da)
    return came_a, came_b


def reduce_sides(make, came, way, split, *deps):
    size_a, size_b = lax.axis_size("a"), lax.axis_size("b")
    whole, top, low = slice(None), slice(0, split), slice(split, None)

    def side(i, extra, part):
        if not extra:
            return make(i, whole, deps)
        if way != "both":
            return make(i, whole, deps, extra)
        halves = [make(i, rows, deps, extra if rows == part else []) for rows in (top, low)]
        return jnp.concatenate(halves, axis=0)

    arrived = []
    for da in range(1, size_a):
        extra = [piece for (at, _), piece in came[0].items() if at == da]
        arrived.append(shift(side(da * size_b, extra, top), "a", -da))
    for db in range(1, size_b):
        extra = [piece for (_, at), piece in came[1].items() if at == db]
        arrived.append(shift(side(db, extra, low), "b", -db))
    return arrived


def reduce_line(term, last=()):
    size = lax.axis_size("ctx")
    rows = term.shape[0] // size
    total = after(term[:rows], *last).astype(jnp.float32)
    for k in range(1, size):
        total = total + shift(term[k * rows : (k + 1) * rows], "ctx", -k).astype(jnp.float32)
    return total


def pick_kernel(slab_ref, piece_ref, source_ref, mine_ref, theirs_ref, *, block):
    for k in range(mine_ref.shape[1] // block):
        to = slice(k * block, (k + 1) * block)
        start = pl.multiple_of(piece_ref[0, k] * block, block)
        mine_ref[:, to] = source_ref[:, pl.ds(start, block)]
        start = pl.multiple_of(piece_ref[1, k] * block, block)
        theirs_ref[:, to] = source_ref[:, pl.ds(start, block)]


def slab_terms(grads, slabs, i):
    cuts = {0}
    for part in slabs:
        at = 0
        for piece in part[i]:
            at += piece.shape[0]
            cuts.add(at)
    cuts = sorted(cuts)
    for low, high in zip(cuts[:-1], cuts[1:]):
        total = None
        for grad, part in zip(grads, slabs):
            at = 0
            for piece in part[i]:
                if at <= low and high <= at + piece.shape[0]:
                    term = dot(grad, piece[low - at : high - at, :], 1, 1)
                    total = term if total is None else total + term
                at += piece.shape[0]
        yield low, total


def nest(refs, shape):
    refs = iter(refs)
    return [[[next(refs) for _ in range(count)] for count in part] for part in shape]


def grad_kernel(*refs, shape, plane):
    parts = len(shape)
    grads = [ref[...] for ref in refs[:parts]]
    slabs = nest(refs[parts:-1], shape)
    for i in range(len(shape[0])):
        for low, total in slab_terms(grads, slabs, i):
            start = i * plane + low
            refs[-1][:, start : start + total.shape[1]] = total.astype(jnp.bfloat16)


def grad_place_kernel(*refs, shape, plane, block):
    slab_ref, piece_ref, *refs = refs
    parts = len(shape)
    grads = [ref[...] for ref in refs[:parts]]
    slabs = nest(refs[parts:-2], shape)
    theirs_ref, target_ref = refs[-2:]
    for i in range(len(shape[0])):
        base = slab_ref[i] * (2 * plane)
        for k in range(plane // block):
            start = pl.multiple_of(base + piece_ref[1, k] * block, block)
            at = i * plane + k * block
            target_ref[:, pl.ds(start, block)] = theirs_ref[:, at : at + block]
        for low, total in slab_terms(grads, slabs, i):
            total = total.astype(jnp.bfloat16)
            for j in range(total.shape[1] // block):
                k = low // block + j
                start = pl.multiple_of(base + piece_ref[0, k] * block, block)
                target_ref[:, pl.ds(start, block)] = total[:, j * block : (j + 1) * block]


VMEM = pl.BlockSpec(memory_space=pltpu.VMEM)


def pieces_of(slabs, pieces, block):
    at = slabs[None, :, None] * pieces.size + pieces[:, None, :]
    return at[..., None] * block + jnp.arange(block)


def pick_columns(source, slabs, pieces, block):
    rows, width = source.shape
    count, depth = slabs.shape[0], pieces.shape[1]
    half = depth * block
    if block % 128:
        at = pieces_of(slabs, pieces, block).reshape(2, -1)
        return source[:, at[0]], source[:, at[1]]
    part = jax.ShapeDtypeStruct((rows, width // 2), source.dtype)
    return pl.pallas_call(
        functools.partial(pick_kernel, block=block),
        grid_spec=pltpu.PrefetchScalarGridSpec(
            num_scalar_prefetch=2,
            grid=(count,),
            in_specs=[pl.BlockSpec((rows, 2 * half), lambda i, slab, piece: (0, slab[i]))],
            out_specs=[pl.BlockSpec((rows, half), lambda i, slab, piece: (0, i))] * 2,
        ),
        out_shape=[part, part],
        cost_estimate=pl.CostEstimate(
            flops=0, bytes_accessed=4 * rows * width, transcendentals=0
        ),
        name="pick_columns",
    )(slabs, pieces, source)


def grad_columns(grads, slabs):
    rows = grads[0].shape[0]
    shape = [[len(slab) for slab in part] for part in slabs]
    flat = [piece for part in slabs for slab in part for piece in slab]
    plane = sum(piece.shape[0] for piece in slabs[0][0])
    width = plane * len(shape[0])
    return pl.pallas_call(
        functools.partial(grad_kernel, shape=shape, plane=plane),
        in_specs=[VMEM] * (len(grads) + len(flat)),
        out_specs=VMEM,
        out_shape=jax.ShapeDtypeStruct((rows, width), jnp.bfloat16),
        compiler_params=pltpu.CompilerParams(vmem_limit_bytes=40 * 1024 * 1024),
        cost_estimate=pl.CostEstimate(
            flops=2 * rows * sum(piece.size for piece in flat),
            bytes_accessed=2 * sum(piece.size for piece in flat) + 2 * rows * width,
            transcendentals=0,
        ),
        name="grad_columns",
    )(*grads, *flat)


def grad_place(grads, slabs, theirs, places, pieces, block):
    rows, width = theirs.shape[0], 2 * theirs.shape[1]
    shape = [[len(slab) for slab in part] for part in slabs]
    flat = [piece for part in slabs for slab in part for piece in slab]
    plane = sum(piece.shape[0] for piece in slabs[0][0])
    if block % 128:
        at = pieces_of(places, pieces, block).reshape(2, -1)
        target = jnp.zeros((rows, width), theirs.dtype)
        return target.at[:, at[0]].set(grad_columns(grads, slabs)).at[:, at[1]].set(theirs)
    return pl.pallas_call(
        functools.partial(grad_place_kernel, shape=shape, plane=plane, block=block),
        grid_spec=pltpu.PrefetchScalarGridSpec(
            num_scalar_prefetch=2,
            grid=(),
            in_specs=[VMEM] * (len(grads) + len(flat) + 1),
            out_specs=VMEM,
        ),
        out_shape=jax.ShapeDtypeStruct((rows, width), jnp.bfloat16),
        compiler_params=pltpu.CompilerParams(vmem_limit_bytes=40 * 1024 * 1024),
        cost_estimate=pl.CostEstimate(
            flops=2 * rows * sum(piece.size for piece in flat),
            bytes_accessed=2 * sum(piece.size for piece in flat) + 3 * rows * width,
            transcendentals=0,
        ),
        name="grad_place",
    )(places, pieces, *grads, *flat, theirs)


def dot(a, b, left, right):
    return lax.dot_general(
        a, b, (((left,), (right,)), ((), ())), preferred_element_type=jnp.float32
    )


def attend_kernel(*refs, group, parts, head_dim, scale, last):
    q_own, q_other, grads, cos_ref, sin_ref, row_pos, key_pos = refs[:7]
    pieces = refs[7 : 7 + parts]
    rest = refs[7 + parts :]
    if last:
        before, rest = rest[0], rest[1:]
    attention_ref, grad_ref = rest[:2]
    terms = rest[2:-1]
    held = rest[-1]
    rows = q_own.shape[0]
    for j in range(parts):
        held[j * rows : (j + 1) * rows, :] = pieces[j][...]
    keys, values = held[:, :head_dim], held[:, head_dim:]
    cos, sin = cos_ref[...], sin_ref[...]
    allowed = key_pos[...] <= row_pos[...]
    key_term = value_term = None
    for h in range(group):
        at = slice(h * head_dim, (h + 1) * head_dim)
        q = q_own[:, at] + q_other[:, at]
        q = (q * cos + pltpu.roll(q, head_dim // 2, 1) * sin).astype(jnp.bfloat16)
        scores = jnp.where(allowed, dot(q, keys, 1, 1) * scale, MASKED)
        weight = jnp.exp(scores - jnp.max(scores, axis=1, keepdims=True))
        inverse = 1.0 / jnp.sum(weight, axis=1, keepdims=True)
        attention = (dot(weight.astype(jnp.bfloat16), values, 1, 0) * inverse).astype(jnp.bfloat16)
        attention_ref[:, at] = attention
        grad = grads[:, at]
        delta = jnp.sum(
            grad.astype(jnp.float32) * attention.astype(jnp.float32), axis=1, keepdims=True
        )
        probs = weight * inverse
        dscore = (probs * (dot(grad, values, 1, 1) - delta)).astype(jnp.bfloat16)
        grad_q = dot(dscore, keys, 1, 0) * scale
        grad_q = grad_q * cos - pltpu.roll(grad_q, head_dim // 2, 1) * sin
        grad_ref[:, at] = grad_q.astype(jnp.bfloat16)
        key_new = dot(dscore, q, 0, 0) * scale
        value_new = dot(probs.astype(jnp.bfloat16), grad, 0, 0)
        key_term = key_new if h == 0 else key_term + key_new
        value_term = value_new if h == 0 else value_term + value_new
    if last:
        key_term = key_term + before[:, :head_dim]
        value_term = value_term + before[:, head_dim:]
        for j in range(parts):
            span = slice(j * rows, (j + 1) * rows)
            terms[j][:, :head_dim] = key_term[span].astype(terms[j].dtype)
            terms[j][:, head_dim:] = value_term[span].astype(terms[j].dtype)
    else:
        terms[0][:, :head_dim] = key_term
        terms[0][:, head_dim:] = value_term


def attend(q_own, q_other, grads, cos, sin, row_pos, key_pos, pieces, before, scale):
    rows, columns = q_own.shape
    head_dim = cos.shape[1]
    parts = len(pieces)
    last = before is not None
    keys = parts * rows
    group = columns // head_dim
    if last:
        terms = [jax.ShapeDtypeStruct((rows, 2 * head_dim), jnp.float32)]
        terms += [jax.ShapeDtypeStruct((rows, 2 * head_dim), jnp.bfloat16)] * (parts - 1)
    else:
        terms = [jax.ShapeDtypeStruct((keys, 2 * head_dim), jnp.float32)]
    out_shape = [jax.ShapeDtypeStruct((rows, columns), jnp.bfloat16)] * 2 + terms
    operands = [q_own, q_other, grads, cos, sin, row_pos, key_pos, *pieces]
    operands += [before] if last else []
    out = pl.pallas_call(
        functools.partial(
            attend_kernel, group=group, parts=parts, head_dim=head_dim, scale=scale, last=last
        ),
        in_specs=[VMEM] * len(operands),
        out_specs=[VMEM] * len(out_shape),
        out_shape=out_shape,
        scratch_shapes=[pltpu.VMEM((keys, 2 * head_dim), jnp.bfloat16)],
        compiler_params=pltpu.CompilerParams(vmem_limit_bytes=48 * 1024 * 1024),
        cost_estimate=pl.CostEstimate(
            flops=14 * rows * keys * columns,
            bytes_accessed=8 * keys * 2 * head_dim,
            transcendentals=rows * keys * group,
        ),
        name="attend",
    )(*operands)
    return out[0], out[1], out[2:]


def finish_kernel(own, other, cos_ref, sin_ref, out):
    head_dim = cos_ref.shape[1]
    total = own[...] + other[...]
    key = total[:, :head_dim]
    key = key * cos_ref[...] + pltpu.roll(key, head_dim // 2, 1) * sin_ref[...]
    out[:, :head_dim] = key.astype(jnp.bfloat16)
    out[:, head_dim:] = total[:, head_dim:].astype(jnp.bfloat16)


def finish_keys(own, other, cos, sin):
    return pl.pallas_call(
        finish_kernel,
        in_specs=[VMEM] * 4,
        out_specs=VMEM,
        out_shape=jax.ShapeDtypeStruct(own.shape, jnp.bfloat16),
        name="finish_keys",
    )(own, other, cos, sin)


def undo_kernel(*refs):
    pieces, (cos_ref, sin_ref, out) = refs[:-3], refs[-3:]
    head_dim = cos_ref.shape[1]
    total = pieces[0][...]
    for piece in pieces[1:]:
        total = total + piece[...].astype(jnp.float32)
    key = total[:, :head_dim]
    key = key * cos_ref[...] - pltpu.roll(key, head_dim // 2, 1) * sin_ref[...]
    out[:, :head_dim] = key.astype(jnp.bfloat16)
    out[:, head_dim:] = total[:, head_dim:].astype(jnp.bfloat16)


def undo_keys(pieces, cos, sin):
    return pl.pallas_call(
        undo_kernel,
        in_specs=[VMEM] * (len(pieces) + 2),
        out_specs=VMEM,
        out_shape=jax.ShapeDtypeStruct(pieces[0].shape, jnp.bfloat16),
        name="undo_keys",
    )(*pieces, cos, sin)


def body(tokens, positions, query_weight, key_weight, value_weight, grad_output):
    token_rows = tokens[0]
    rows, width = token_rows.shape
    head_dim = key_weight.shape[1]
    query_width = query_weight.shape[1]
    heads = query_width // head_dim
    group = heads // 2
    scale = head_dim ** (-0.5)
    size_a, size_b, ctx = lax.axis_size("a"), lax.axis_size("b"), lax.axis_size("ctx")
    at_a, at_b = lax.axis_index("a"), lax.axis_index("b")
    core, place = lax.axis_index("core"), lax.axis_index("ctx")
    block = query_weight.shape[0]
    plane = ctx * block

    kv_local = jnp.concatenate([key_weight, value_weight], axis=1).astype(jnp.bfloat16)
    q_local = [
        query_weight[:, g * group * head_dim : (g + 1) * group * head_dim].astype(jnp.bfloat16)
        for g in range(2)
    ]
    kv_line = jnp.concatenate(gather_line(kv_local), axis=0)
    q_line = [jnp.concatenate(gather_line(q_local[0]), axis=0)]
    kv_sides = along(kv_line, "a"), along(kv_line, "b")
    q_line.append(jnp.concatenate(gather_line(after(q_local[1], kv_line)), axis=0))
    stage = kv_sides[0] + kv_sides[1]
    kv_corners = gather_corners(*kv_sides, "b", *stage)
    q0_a = along(after(q_line[0], *stage), "a")
    stage = q0_a + [piece for corner in kv_corners.values() for piece in corner]
    q1_a = along(after(q_line[1], *stage), "a")
    q0_b = along(after(q_line[0], *stage), "b")
    kv_slabs = in_order(kv_line, *kv_sides, kv_corners)

    da, db = jnp.meshgrid(jnp.arange(size_a), jnp.arange(size_b), indexing="ij")
    slabs = ((at_a + size_a - da) % size_a) * size_b + (at_b + size_b - db) % size_b
    slabs = slabs.reshape(-1).astype(jnp.int32)
    line = (place + ctx - jnp.arange(ctx)) % ctx
    pieces = jnp.stack([core * ctx + line, (1 - core) * ctx + line]).astype(jnp.int32)
    mine, theirs = pick_columns(token_rows, slabs, pieces, block)
    theirs = swap(theirs)

    positions = after(positions, kv_line)
    own_positions = lax.dynamic_slice_in_dim(positions, place * rows, rows)
    cos_table, sin_table = rope_tables(own_positions, head_dim)
    sin_table = jnp.where(jnp.arange(head_dim) < head_dim // 2, -sin_table, sin_table)
    key_positions = jnp.concatenate(
        [
            lax.dynamic_slice_in_dim(positions, ((place + ctx - k) % ctx) * rows, rows)
            for k in range(ctx)
        ]
    )

    def product(columns, slabs):
        at, total = 0, None
        for piece in [piece for slab in slabs for piece in slab]:
            end = at + piece.shape[0]
            term = mm(columns[:, at:end], piece, ((1,), (0,)))
            total = term if total is None else total + term
            at = end
        return total

    def project(slabs):
        other = swap(product(theirs, slabs))
        return product(mine, slabs), other

    columns = jnp.concatenate([mine, theirs], axis=0)

    def terms_of(own, other):
        both = jnp.concatenate([own, other], axis=0)

        def make(i, part, deps=(), extra=()):
            start, stop, _ = part.indices(plane)
            at = slice(i * plane + start, i * plane + stop)
            term = mm(columns[:, at], after(both, *deps) if deps else both, ((0,), (0,)))
            for piece in extra:
                term = term + piece.astype(jnp.float32)
            return term.astype(jnp.bfloat16)

        return make

    key_value = finish_keys(*project(kv_slabs), cos_table, sin_table)
    stage = q1_a + q0_b + [key_value]
    q0_corners = gather_corners(q0_a, q0_b, "a", *stage)
    q1_b = along(after(q_line[1], *stage), "b")
    key_values = gather_line(key_value)
    stage = q1_b + [piece for corner in q0_corners.values() for piece in corner]
    q1_corners = gather_corners(q1_a, q1_b, "both", *stage)
    q_slabs = [
        in_order(q_line[0], q0_a, q0_b, q0_corners),
        in_order(q_line[1], q1_a, q1_b, q1_corners),
    ]
    attentions, gradients, made, came = [], [], [], []
    mid = plane // 2
    term = None
    for g in range(2):
        span = slice(g * group * head_dim, (g + 1) * group * head_dim)
        attention, grad_q, terms = attend(
            *project(q_slabs[g]),
            grad_output[0][:, span],
            cos_table,
            sin_table,
            own_positions[:, None],
            key_positions[None, :],
            key_values,
            term,
            scale,
        )
        term = terms[0]
        attentions.append(attention)
        grads = (grad_q, swap(grad_q))
        gradients.append(grads)
        made.append(terms_of(*grads))
        came.append(reduce_corners(made[g], "ba"[g], mid))
    summed = [terms[0]] + [shift(terms[k], "ctx", -k) for k in range(1, ctx)]
    first = [*came[0][0].values(), *came[0][1].values()]
    sides = [reduce_sides(made[0], came[0], "b", mid, *first)]
    grad_kv = undo_keys([after(summed[0], *first), *summed[1:]], cos_table, sin_table)
    gradients.append((grad_kv, swap(grad_kv)))
    made.append(terms_of(*gradients[2]))
    came.append(reduce_corners(made[2], "both", mid))
    line0 = made[0](0, slice(None), (), sides[0])
    q_sum = reduce_line(line0)
    sides.append(reduce_sides(made[1], came[1], "a", mid, *sides[0]))
    kv_sides = reduce_sides(made[2], came[2], "both", mid)
    kv_sum = reduce_line(made[2](0, slice(None), (), kv_sides))

    weights = [*q_slabs, kv_slabs]
    grad_theirs = grad_columns(
        [gradients[0][1], gradients[1][1], after(gradients[2][1], q_sum, *kv_sides)], weights
    )
    grad_theirs = swap(grad_theirs)
    line1 = made[1](0, slice(None), (), sides[1])
    grad_input = grad_place(
        [gradients[0][0], gradients[1][0], gradients[2][0]], weights, grad_theirs, slabs, pieces, block
    )
    q_grads = [q_sum, reduce_line(line1, (grad_input,))]
    kv_wgrad = kv_sum

    query_grad = jnp.concatenate(q_grads, axis=1)
    key_grad = kv_wgrad[:, :head_dim]
    value_grad = kv_wgrad[:, head_dim:]
    attention_rows = jnp.concatenate(attentions, axis=1)
    return (attention_rows[None], grad_input[None], query_grad, key_grad, value_grad)


def solution(mesh):
    dp, ctx = mesh.devices.shape
    fine = Mesh(mesh.devices.reshape(dp // 4, 2, 2, ctx), ("a", "b", "core", "ctx"))
    batch = P(("a", "b", "core"), "ctx", None)
    master = P(("a", "b", "core", "ctx"), None)
    in_specs = (batch, P(), master, master, master, batch)
    out_specs = (batch, batch, master, master, master)
    return jax.shard_map(body, mesh=fine, in_specs=in_specs, out_specs=out_specs, check_vma=False)
```

```python
import functools

import jax
import jax.numpy as jnp
from jax import lax
from jax.experimental import pallas as pl
from jax.experimental.pallas import tpu as pltpu
from jax.sharding import Mesh, PartitionSpec as P

ROPE_BASE = 1000000.0
MASKED = -1e30


def rope_tables(positions_in, head_dim):
    half_width = head_dim // 2
    exponent = jnp.arange(half_width).astype(jnp.float32) * (2.0 / head_dim)
    frequency = jnp.power(ROPE_BASE, -exponent)
    angles = positions_in.astype(jnp.float32)[:, None] * frequency[None, :]
    angles = jnp.concatenate([angles, angles], axis=1)
    return (jnp.cos(angles), jnp.sin(angles))


def mm(a, b, dims):
    return lax.dot_general(a, b, (dims, ((), ())), preferred_element_type=jnp.float32)


def shift(block, axis, step):
    size = lax.axis_size(axis)
    return lax.ppermute(block, axis, [(i, (i + step) % size) for i in range(size)])


def after(block, *others):
    return lax.optimization_barrier((block, *others))[0]


def swap(block):
    return shift(block, "core", 1)


def gather_line(block):
    return [block] + [shift(block, "ctx", k) for k in range(1, lax.axis_size("ctx"))]


def along(block, axis):
    return [shift(block, axis, step) for step in range(1, lax.axis_size(axis))]


def gather_corners(sides_a, sides_b, way, *deps):
    corners = {}
    for da, side_a in enumerate(sides_a, 1):
        for db, side_b in enumerate(sides_b, 1):
            mid = side_a.shape[0] // 2
            if way == "b":
                corners[da, db] = [shift(after(side_a, *deps), "b", db)]
            elif way == "a":
                corners[da, db] = [shift(after(side_b, *deps), "a", da)]
            else:
                corners[da, db] = [
                    shift(after(side_a[:mid], *deps), "b", db),
                    shift(after(side_b[mid:], *deps), "a", da),
                ]
    return corners


def in_order(block, sides_a, sides_b, corners):
    slabs = [[block]] + [[side] for side in sides_b]
    for da, side in enumerate(sides_a, 1):
        slabs.append([side])
        slabs += [corners[da, db] for db in range(1, len(sides_b) + 1)]
    return slabs


def reduce_corners(make, way, split, *deps):
    size_b = lax.axis_size("b")
    whole, top, low = slice(None), slice(0, split), slice(split, None)
    came_a, came_b = {}, {}
    for da in range(1, lax.axis_size("a")):
        for db in range(1, size_b):
            i = da * size_b + db
            if way == "b":
                came_a[da, db] = shift(make(i, whole, deps), "b", -db)
            elif way == "a":
                came_b[da, db] = shift(make(i, whole, deps), "a", -da)
            else:
                came_a[da, db] = shift(make(i, top, deps), "b", -db)
                came_b[da, db] = shift(make(i, low, deps), "a", -da)
    return came_a, came_b


def reduce_sides(make, came, way, split, *deps):
    size_a, size_b = lax.axis_size("a"), lax.axis_size("b")
    whole, top, low = slice(None), slice(0, split), slice(split, None)

    def side(i, extra, part):
        if not extra:
            return make(i, whole, deps)
        if way != "both":
            return make(i, whole, deps, extra)
        halves = [make(i, rows, deps, extra if rows == part else []) for rows in (top, low)]
        return jnp.concatenate(halves, axis=0)

    went, arrived = [], []
    for da in range(1, size_a):
        extra = [piece for (at, _), piece in came[0].items() if at == da]
        went.append(side(da * size_b, extra, top))
        arrived.append(shift(went[-1], "a", -da))
    for db in range(1, size_b):
        extra = [piece for (_, at), piece in came[1].items() if at == db]
        went.append(side(db, extra, low))
        arrived.append(shift(went[-1], "b", -db))
    return arrived, went


def reduce_line(term, last=()):
    size = lax.axis_size("ctx")
    rows = term.shape[0] // size
    total = after(term[:rows], *last).astype(jnp.float32)
    for k in range(1, size):
        total = total + shift(term[k * rows : (k + 1) * rows], "ctx", -k).astype(jnp.float32)
    return total


def pick_kernel(slab_ref, piece_ref, source_ref, mine_ref, theirs_ref, *, block):
    for k in range(mine_ref.shape[1] // block):
        to = slice(k * block, (k + 1) * block)
        start = pl.multiple_of(piece_ref[0, k] * block, block)
        mine_ref[:, to] = source_ref[:, pl.ds(start, block)]
        start = pl.multiple_of(piece_ref[1, k] * block, block)
        theirs_ref[:, to] = source_ref[:, pl.ds(start, block)]


def slab_terms(grads, slabs, i):
    cuts = {0}
    for part in slabs:
        at = 0
        for piece in part[i]:
            at += piece.shape[0]
            cuts.add(at)
    cuts = sorted(cuts)
    for low, high in zip(cuts[:-1], cuts[1:]):
        total = None
        for grad, part in zip(grads, slabs):
            at = 0
            for piece in part[i]:
                if at <= low and high <= at + piece.shape[0]:
                    term = dot(grad, piece[low - at : high - at, :], 1, 1)
                    total = term if total is None else total + term
                at += piece.shape[0]
        yield low, total


def nest(refs, shape):
    refs = iter(refs)
    return [[[next(refs) for _ in range(count)] for count in part] for part in shape]


def grad_kernel(*refs, shape, plane):
    parts = len(shape)
    grads = [ref[...] for ref in refs[:parts]]
    slabs = nest(refs[parts:-1], shape)
    for i in range(len(shape[0])):
        for low, total in slab_terms(grads, slabs, i):
            start = i * plane + low
            refs[-1][:, start : start + total.shape[1]] = total.astype(jnp.bfloat16)


def grad_place_kernel(*refs, shape, plane, block):
    slab_ref, piece_ref, *refs = refs
    parts = len(shape)
    grads = [ref[...] for ref in refs[:parts]]
    slabs = nest(refs[parts:-2], shape)
    theirs_ref, target_ref = refs[-2:]
    for i in range(len(shape[0])):
        base = slab_ref[i] * (2 * plane)
        for k in range(plane // block):
            start = pl.multiple_of(base + piece_ref[1, k] * block, block)
            at = i * plane + k * block
            target_ref[:, pl.ds(start, block)] = theirs_ref[:, at : at + block]
        for low, total in slab_terms(grads, slabs, i):
            total = total.astype(jnp.bfloat16)
            for j in range(total.shape[1] // block):
                k = low // block + j
                start = pl.multiple_of(base + piece_ref[0, k] * block, block)
                target_ref[:, pl.ds(start, block)] = total[:, j * block : (j + 1) * block]


VMEM = pl.BlockSpec(memory_space=pltpu.VMEM)


def pieces_of(slabs, pieces, block):
    at = slabs[None, :, None] * pieces.size + pieces[:, None, :]
    return at[..., None] * block + jnp.arange(block)


def pick_columns(source, slabs, pieces, block):
    rows, width = source.shape
    count, depth = slabs.shape[0], pieces.shape[1]
    half = depth * block
    if block % 128:
        at = pieces_of(slabs, pieces, block).reshape(2, -1)
        return source[:, at[0]], source[:, at[1]]
    part = jax.ShapeDtypeStruct((rows, width // 2), source.dtype)
    return pl.pallas_call(
        functools.partial(pick_kernel, block=block),
        grid_spec=pltpu.PrefetchScalarGridSpec(
            num_scalar_prefetch=2,
            grid=(count,),
            in_specs=[pl.BlockSpec((rows, 2 * half), lambda i, slab, piece: (0, slab[i]))],
            out_specs=[pl.BlockSpec((rows, half), lambda i, slab, piece: (0, i))] * 2,
        ),
        out_shape=[part, part],
        cost_estimate=pl.CostEstimate(
            flops=0, bytes_accessed=4 * rows * width, transcendentals=0
        ),
        name="pick_columns",
    )(slabs, pieces, source)


def grad_columns(grads, slabs):
    rows = grads[0].shape[0]
    shape = [[len(slab) for slab in part] for part in slabs]
    flat = [piece for part in slabs for slab in part for piece in slab]
    plane = sum(piece.shape[0] for piece in slabs[0][0])
    width = plane * len(shape[0])
    return pl.pallas_call(
        functools.partial(grad_kernel, shape=shape, plane=plane),
        in_specs=[VMEM] * (len(grads) + len(flat)),
        out_specs=VMEM,
        out_shape=jax.ShapeDtypeStruct((rows, width), jnp.bfloat16),
        compiler_params=pltpu.CompilerParams(vmem_limit_bytes=20 * 1024 * 1024),
        cost_estimate=pl.CostEstimate(
            flops=2 * rows * sum(piece.size for piece in flat),
            bytes_accessed=2 * sum(piece.size for piece in flat) + 2 * rows * width,
            transcendentals=0,
        ),
        name="grad_columns",
    )(*grads, *flat)


def grad_place(grads, slabs, theirs, places, pieces, block):
    rows, width = theirs.shape[0], 2 * theirs.shape[1]
    shape = [[len(slab) for slab in part] for part in slabs]
    flat = [piece for part in slabs for slab in part for piece in slab]
    plane = sum(piece.shape[0] for piece in slabs[0][0])
    if block % 128:
        at = pieces_of(places, pieces, block).reshape(2, -1)
        target = jnp.zeros((rows, width), theirs.dtype)
        return target.at[:, at[0]].set(grad_columns(grads, slabs)).at[:, at[1]].set(theirs)
    return pl.pallas_call(
        functools.partial(grad_place_kernel, shape=shape, plane=plane, block=block),
        grid_spec=pltpu.PrefetchScalarGridSpec(
            num_scalar_prefetch=2,
            grid=(),
            in_specs=[VMEM] * (len(grads) + len(flat) + 1),
            out_specs=VMEM,
        ),
        out_shape=jax.ShapeDtypeStruct((rows, width), jnp.bfloat16),
        compiler_params=pltpu.CompilerParams(vmem_limit_bytes=20 * 1024 * 1024),
        cost_estimate=pl.CostEstimate(
            flops=2 * rows * sum(piece.size for piece in flat),
            bytes_accessed=2 * sum(piece.size for piece in flat) + 3 * rows * width,
            transcendentals=0,
        ),
        name="grad_place",
    )(places, pieces, *grads, *flat, theirs)


def dot(a, b, left, right):
    return lax.dot_general(
        a, b, (((left,), (right,)), ((), ())), preferred_element_type=jnp.float32
    )


def project_kernel(mine_ref, theirs_ref, *refs):
    pieces, (own_ref, other_ref) = refs[:-2], refs[-2:]
    for source, target in ((theirs_ref, other_ref), (mine_ref, own_ref)):
        at, total = 0, None
        for piece in pieces:
            end = at + piece.shape[0]
            term = dot(source[:, at:end], piece[...], 1, 0)
            total = term if total is None else total + term
            at = end
        target[...] = total


def project_rows(mine, theirs, pieces):
    rows, columns = mine.shape[0], pieces[0].shape[1]
    return pl.pallas_call(
        project_kernel,
        in_specs=[VMEM] * (len(pieces) + 2),
        out_specs=[VMEM] * 2,
        out_shape=[jax.ShapeDtypeStruct((rows, columns), jnp.float32)] * 2,
        compiler_params=pltpu.CompilerParams(vmem_limit_bytes=20 * 1024 * 1024),
        cost_estimate=pl.CostEstimate(
            flops=4 * mine.size * columns,
            bytes_accessed=4 * mine.size + 2 * mine.shape[1] * columns,
            transcendentals=0,
        ),
        name="project_rows",
    )(mine, theirs, *pieces)


def attend_kernel(*refs, group, parts, head_dim, scale, last):
    q_own, q_other, grads, cos_ref, sin_ref, row_pos, key_pos = refs[:7]
    pieces = refs[7 : 7 + parts]
    rest = refs[7 + parts :]
    if last:
        before, rest = rest[0], rest[1:]
    attention_ref, grad_ref = rest[:2]
    terms = rest[2:-1]
    held = rest[-1]
    rows = q_own.shape[0]
    for j in range(parts):
        held[j * rows : (j + 1) * rows, :] = pieces[j][...]
    keys, values = held[:, :head_dim], held[:, head_dim:]
    cos, sin = cos_ref[...], sin_ref[...]
    allowed = key_pos[...] <= row_pos[...]
    key_term = value_term = None
    for h in range(group):
        at = slice(h * head_dim, (h + 1) * head_dim)
        q = q_own[:, at] + q_other[:, at]
        q = (q * cos + pltpu.roll(q, head_dim // 2, 1) * sin).astype(jnp.bfloat16)
        scores = jnp.where(allowed, dot(q, keys, 1, 1) * scale, MASKED)
        weight = jnp.exp(scores - jnp.max(scores, axis=1, keepdims=True))
        inverse = 1.0 / jnp.sum(weight, axis=1, keepdims=True)
        attention = (dot(weight.astype(jnp.bfloat16), values, 1, 0) * inverse).astype(jnp.bfloat16)
        attention_ref[:, at] = attention
        grad = grads[:, at]
        delta = jnp.sum(
            grad.astype(jnp.float32) * attention.astype(jnp.float32), axis=1, keepdims=True
        )
        probs = weight * inverse
        dscore = (probs * (dot(grad, values, 1, 1) - delta)).astype(jnp.bfloat16)
        grad_q = dot(dscore, keys, 1, 0) * scale
        grad_q = grad_q * cos - pltpu.roll(grad_q, head_dim // 2, 1) * sin
        grad_ref[:, at] = grad_q.astype(jnp.bfloat16)
        key_new = dot(dscore, q, 0, 0) * scale
        value_new = dot(probs.astype(jnp.bfloat16), grad, 0, 0)
        key_term = key_new if h == 0 else key_term + key_new
        value_term = value_new if h == 0 else value_term + value_new
    if last:
        key_term = key_term + before[:, :head_dim]
        value_term = value_term + before[:, head_dim:]
        for j in range(parts):
            span = slice(j * rows, (j + 1) * rows)
            terms[j][:, :head_dim] = key_term[span].astype(terms[j].dtype)
            terms[j][:, head_dim:] = value_term[span].astype(terms[j].dtype)
    else:
        terms[0][:, :head_dim] = key_term
        terms[0][:, head_dim:] = value_term


def attend(q_own, q_other, grads, cos, sin, row_pos, key_pos, pieces, before, scale):
    rows, columns = q_own.shape
    head_dim = cos.shape[1]
    parts = len(pieces)
    last = before is not None
    keys = parts * rows
    group = columns // head_dim
    if last:
        terms = [jax.ShapeDtypeStruct((rows, 2 * head_dim), jnp.float32)]
        terms += [jax.ShapeDtypeStruct((rows, 2 * head_dim), jnp.bfloat16)] * (parts - 1)
    else:
        terms = [jax.ShapeDtypeStruct((keys, 2 * head_dim), jnp.float32)]
    out_shape = [jax.ShapeDtypeStruct((rows, columns), jnp.bfloat16)] * 2 + terms
    operands = [q_own, q_other, grads, cos, sin, row_pos, key_pos, *pieces]
    operands += [before] if last else []
    out = pl.pallas_call(
        functools.partial(
            attend_kernel, group=group, parts=parts, head_dim=head_dim, scale=scale, last=last
        ),
        in_specs=[VMEM] * len(operands),
        out_specs=[VMEM] * len(out_shape),
        out_shape=out_shape,
        scratch_shapes=[pltpu.VMEM((keys, 2 * head_dim), jnp.bfloat16)],
        compiler_params=pltpu.CompilerParams(vmem_limit_bytes=20 * 1024 * 1024),
        cost_estimate=pl.CostEstimate(
            flops=14 * rows * keys * columns,
            bytes_accessed=8 * keys * 2 * head_dim,
            transcendentals=rows * keys * group,
        ),
        name="attend",
    )(*operands)
    return out[0], out[1], out[2:]


def finish_kernel(own, other, cos_ref, sin_ref, out):
    head_dim = cos_ref.shape[1]
    total = own[...] + other[...]
    key = total[:, :head_dim]
    key = key * cos_ref[...] + pltpu.roll(key, head_dim // 2, 1) * sin_ref[...]
    out[:, :head_dim] = key.astype(jnp.bfloat16)
    out[:, head_dim:] = total[:, head_dim:].astype(jnp.bfloat16)


def finish_keys(own, other, cos, sin):
    return pl.pallas_call(
        finish_kernel,
        in_specs=[VMEM] * 4,
        out_specs=VMEM,
        out_shape=jax.ShapeDtypeStruct(own.shape, jnp.bfloat16),
        name="finish_keys",
    )(own, other, cos, sin)


def undo_kernel(*refs):
    pieces, (cos_ref, sin_ref, out) = refs[:-3], refs[-3:]
    head_dim = cos_ref.shape[1]
    total = pieces[0][...]
    for piece in pieces[1:]:
        total = total + piece[...].astype(jnp.float32)
    key = total[:, :head_dim]
    key = key * cos_ref[...] - pltpu.roll(key, head_dim // 2, 1) * sin_ref[...]
    out[:, :head_dim] = key.astype(jnp.bfloat16)
    out[:, head_dim:] = total[:, head_dim:].astype(jnp.bfloat16)


def undo_keys(pieces, cos, sin):
    return pl.pallas_call(
        undo_kernel,
        in_specs=[VMEM] * (len(pieces) + 2),
        out_specs=VMEM,
        out_shape=jax.ShapeDtypeStruct(pieces[0].shape, jnp.bfloat16),
        name="undo_keys",
    )(*pieces, cos, sin)


def body(tokens, positions, query_weight, key_weight, value_weight, grad_output):
    token_rows = tokens[0]
    rows, width = token_rows.shape
    head_dim = key_weight.shape[1]
    query_width = query_weight.shape[1]
    heads = query_width // head_dim
    group = heads // 2
    scale = head_dim ** (-0.5)
    size_a, size_b, ctx = lax.axis_size("a"), lax.axis_size("b"), lax.axis_size("ctx")
    at_a, at_b = lax.axis_index("a"), lax.axis_index("b")
    core, place = lax.axis_index("core"), lax.axis_index("ctx")
    block = query_weight.shape[0]
    plane = ctx * block

    kv_local = jnp.concatenate([key_weight, value_weight], axis=1).astype(jnp.bfloat16)
    da, db = jnp.meshgrid(jnp.arange(size_a), jnp.arange(size_b), indexing="ij")
    slabs = ((at_a + size_a - da) % size_a) * size_b + (at_b + size_b - db) % size_b
    slabs = slabs.reshape(-1).astype(jnp.int32)
    line = (place + ctx - jnp.arange(ctx)) % ctx
    pieces = jnp.stack([core * ctx + line, (1 - core) * ctx + line]).astype(jnp.int32)
    mine, theirs = pick_columns(token_rows, slabs, pieces, block)
    pieces_kv = gather_line(kv_local)
    kv_line = jnp.concatenate([after(pieces_kv[0], mine), *pieces_kv[1:]], axis=0)
    theirs = swap(after(theirs, kv_line))

    pieces_q = gather_line(after(query_weight, kv_line).astype(jnp.bfloat16))
    half = query_width // 2
    q_line = [
        jnp.concatenate([piece[:, g * half : (g + 1) * half] for piece in pieces_q], axis=0)
        for g in range(2)
    ]
    kv_sides = along(kv_line, "a"), along(kv_line, "b")
    stage = kv_sides[0] + kv_sides[1] + q_line
    kv_corners = gather_corners(*kv_sides, "b", *stage)
    q0_a = along(after(q_line[0], *stage), "a")
    stage = q0_a + [piece for corner in kv_corners.values() for piece in corner]
    q1_a = along(after(q_line[1], *stage), "a")
    q0_b = along(after(q_line[0], *stage), "b")
    kv_slabs = in_order(kv_line, *kv_sides, kv_corners)

    positions = after(positions, kv_line)
    own_positions = lax.dynamic_slice_in_dim(positions, place * rows, rows)
    cos_table, sin_table = rope_tables(own_positions, head_dim)
    sin_table = jnp.where(jnp.arange(head_dim) < head_dim // 2, -sin_table, sin_table)
    key_positions = jnp.concatenate(
        [
            lax.dynamic_slice_in_dim(positions, ((place + ctx - k) % ctx) * rows, rows)
            for k in range(ctx)
        ]
    )

    def project(slabs):
        own, other = project_rows(mine, theirs, [piece for slab in slabs for piece in slab])
        return own, swap(other)

    columns = jnp.concatenate([after(mine, *q0_a), theirs], axis=0)

    def terms_of(own, other):
        both = jnp.concatenate([own, other], axis=0)

        def make(i, part, deps=(), extra=()):
            start, stop, _ = part.indices(plane)
            at = slice(i * plane + start, i * plane + stop)
            term = mm(columns[:, at], after(both, *deps) if deps else both, ((0,), (0,)))
            for piece in extra:
                term = term + piece.astype(jnp.float32)
            return term.astype(jnp.bfloat16)

        return make

    key_value = finish_keys(*project(kv_slabs), cos_table, sin_table)
    stage = q1_a + q0_b + [key_value]
    q0_corners = gather_corners(q0_a, q0_b, "a", *stage)
    q1_b = along(after(q_line[1], *stage), "b")
    key_values = gather_line(key_value)
    stage = q1_b + key_values + [piece for corner in q0_corners.values() for piece in corner]
    q1_corners = gather_corners(q1_a, q1_b, "both", *stage)
    q_slabs = [
        in_order(q_line[0], q0_a, q0_b, q0_corners),
        in_order(q_line[1], q1_a, q1_b, q1_corners),
    ]
    attentions, gradients, made, came = [], [], [], []
    mid = plane // 2
    term = None
    for g in range(2):
        span = slice(g * group * head_dim, (g + 1) * group * head_dim)
        attention, grad_q, terms = attend(
            *project(q_slabs[g]),
            grad_output[0][:, span],
            cos_table,
            sin_table,
            own_positions[:, None],
            key_positions[None, :],
            key_values,
            term,
            scale,
        )
        term = terms[0]
        attentions.append(attention)
        grads = (grad_q, swap(grad_q))
        gradients.append(grads)
        made.append(terms_of(*grads))
        came.append(reduce_corners(made[g], "ba"[g], mid))
    summed = [terms[0]] + [shift(terms[k], "ctx", -k) for k in range(1, ctx)]
    first = [*came[0][0].values(), *came[0][1].values()]
    second = [*came[1][0].values(), *came[1][1].values()]
    sides0, went0 = reduce_sides(made[0], came[0], "b", mid, *first, *summed[1:])
    grad_kv = undo_keys(
        [after(summed[0], *first, *second, *went0), *summed[1:]], cos_table, sin_table
    )
    gradients.append((grad_kv, swap(grad_kv)))
    made.append(terms_of(*gradients[2]))
    came.append(reduce_corners(made[2], "both", mid))
    sides1, went1 = reduce_sides(made[1], came[1], "a", mid, *sides0)
    q_sum = reduce_line(made[0](0, slice(None), went1, sides0))
    line1 = made[1](0, slice(None), (), sides1)
    kv_sides, _ = reduce_sides(made[2], came[2], "both", mid, *sides1)

    weights = [*q_slabs, kv_slabs]
    grad_theirs = grad_columns(
        [gradients[0][1], gradients[1][1], after(gradients[2][1], q_sum, *sides1)], weights
    )
    grad_theirs = swap(grad_theirs)
    grad_input = grad_place(
        [gradients[0][0], gradients[1][0], gradients[2][0]], weights, grad_theirs, slabs, pieces, block
    )
    q_grads = [q_sum, reduce_line(line1)]
    kv_wgrad = reduce_line(made[2](0, slice(None), (), kv_sides), (grad_input,))

    query_grad = jnp.concatenate(q_grads, axis=1)
    key_grad = kv_wgrad[:, :head_dim]
    value_grad = kv_wgrad[:, head_dim:]
    attention_rows = jnp.concatenate(attentions, axis=1)
    return (attention_rows[None], grad_input[None], query_grad, key_grad, value_grad)


def solution(mesh):
    dp, ctx = mesh.devices.shape
    fine = Mesh(mesh.devices.reshape(dp // 4, 2, 2, ctx), ("a", "b", "core", "ctx"))
    batch = P(("a", "b", "core"), "ctx", None)
    master = P(("a", "b", "core", "ctx"), None)
    in_specs = (batch, P(), master, master, master, batch)
    out_specs = (batch, batch, master, master, master)
    return jax.shard_map(body, mesh=fine, in_specs=in_specs, out_specs=out_specs, check_vma=False)
```

```python
import functools

import jax
import jax.numpy as jnp
from jax import lax
from jax.experimental import pallas as pl
from jax.experimental.pallas import tpu as pltpu
from jax.sharding import Mesh, PartitionSpec as P

ROPE_BASE = 1000000.0
MASKED = -1e30


def rope_tables(positions_in, head_dim):
    half_width = head_dim // 2
    exponent = jnp.arange(half_width).astype(jnp.float32) * (2.0 / head_dim)
    frequency = jnp.power(ROPE_BASE, -exponent)
    angles = positions_in.astype(jnp.float32)[:, None] * frequency[None, :]
    angles = jnp.concatenate([angles, angles], axis=1)
    return (jnp.cos(angles), jnp.sin(angles))


def mm(a, b, dims):
    return lax.dot_general(a, b, (dims, ((), ())), preferred_element_type=jnp.float32)


def shift(block, axis, step):
    size = lax.axis_size(axis)
    return lax.ppermute(block, axis, [(i, (i + step) % size) for i in range(size)])


def after(block, *others):
    return lax.optimization_barrier((block, *others))[0]


def stage(*arrays):
    return list(lax.optimization_barrier(arrays))


def after_all(blocks, *others):
    return [after(block, *others) for block in blocks]


def swap(block):
    return shift(block, "core", 1)


def gather_line(block):
    copies = jnp.broadcast_to(block[None], (lax.axis_size("ctx"), *block.shape))
    return lax.all_to_all(copies, "ctx", 0, 0).reshape(-1, block.shape[1])


def scatter_line(term):
    size = lax.axis_size("ctx")
    blocks = term.reshape(size, term.shape[0] // size, term.shape[1])
    return lax.all_to_all(blocks, "ctx", 0, 0)


def along(block, axis):
    return [shift(block, axis, step) for step in range(1, lax.axis_size(axis))]


def gather_corners(sides_a, sides_b, way, *deps):
    corners = {}
    for da, side_a in enumerate(sides_a, 1):
        for db, side_b in enumerate(sides_b, 1):
            mid = side_a.shape[0] // 2
            if way == "b":
                corners[da, db] = [shift(after(side_a, *deps), "b", db)]
            elif way == "a":
                corners[da, db] = [shift(after(side_b, *deps), "a", da)]
            else:
                corners[da, db] = [
                    shift(after(side_a[:mid], *deps), "b", db),
                    shift(after(side_b[mid:], *deps), "a", da),
                ]
    return corners


def in_order(block, sides_a, sides_b, corners):
    slabs = [[block]] + [[side] for side in sides_b]
    for da, side in enumerate(sides_a, 1):
        slabs.append([side])
        slabs += [corners[da, db] for db in range(1, len(sides_b) + 1)]
    return slabs


def reduce_corners(make, way, split):
    size_b = lax.axis_size("b")
    whole, top, low = slice(None), slice(0, split), slice(split, None)
    came_a, came_b, went = {}, {}, []
    for da in range(1, lax.axis_size("a")):
        for db in range(1, size_b):
            i = da * size_b + db
            went += [make(i, rows) for rows in ((top, low) if way == "both" else (whole,))]
            if way != "a":
                came_a[da, db] = shift(went[-2 if way == "both" else -1], "b", -db)
            if way != "b":
                came_b[da, db] = shift(went[-1], "a", -da)
    return came_a, came_b, went


def reduce_sides(make, came, way, split, *deps):
    size_a, size_b = lax.axis_size("a"), lax.axis_size("b")
    whole, top, low = slice(None), slice(0, split), slice(split, None)

    def side(i, extra, part):
        if not extra or way != "both":
            term = make(i, whole, extra)
        else:
            halves = [make(i, rows, extra if rows == part else []) for rows in (top, low)]
            term = jnp.concatenate(halves, axis=0)
        return after(term, *deps) if deps else term

    went, arrived = [], []
    for da in range(1, size_a):
        extra = [piece for (at, _), piece in came[0].items() if at == da]
        went.append(side(da * size_b, extra, top))
        arrived.append(shift(went[-1], "a", -da))
    for db in range(1, size_b):
        extra = [piece for (_, at), piece in came[1].items() if at == db]
        went.append(side(db, extra, low))
        arrived.append(shift(went[-1], "b", -db))
    return arrived, went


def reduce_line(term, last=()):
    return jnp.sum(after(scatter_line(term), *last).astype(jnp.float32), axis=0)


def pick_kernel(slab_ref, piece_ref, source_ref, mine_ref, theirs_ref, *, block):
    for k in range(mine_ref.shape[1] // block):
        to = slice(k * block, (k + 1) * block)
        start = pl.multiple_of(piece_ref[0, k] * block, block)
        mine_ref[:, to] = source_ref[:, pl.ds(start, block)]
        start = pl.multiple_of(piece_ref[1, k] * block, block)
        theirs_ref[:, to] = source_ref[:, pl.ds(start, block)]


def slab_terms(grads, slabs, i):
    cuts = {0}
    for part in slabs:
        at = 0
        for piece in part[i]:
            at += piece.shape[0]
            cuts.add(at)
    cuts = sorted(cuts)
    for low, high in zip(cuts[:-1], cuts[1:]):
        total = None
        for grad, part in zip(grads, slabs):
            at = 0
            for piece in part[i]:
                if at <= low and high <= at + piece.shape[0]:
                    term = dot(grad, piece[low - at : high - at, :], 1, 1)
                    total = term if total is None else total + term
                at += piece.shape[0]
        yield low, total


def nest(refs, shape):
    refs = iter(refs)
    return [[[next(refs) for _ in range(count)] for count in part] for part in shape]


def grad_kernel(*refs, shape, plane):
    parts = len(shape)
    grads = [ref[...] for ref in refs[:parts]]
    slabs = nest(refs[parts:-1], shape)
    for i in range(len(shape[0])):
        for low, total in slab_terms(grads, slabs, i):
            start = i * plane + low
            refs[-1][:, start : start + total.shape[1]] = total.astype(jnp.bfloat16)


def grad_place_kernel(*refs, shape, plane, block):
    slab_ref, piece_ref, *refs = refs
    parts = len(shape)
    grads = [ref[...] for ref in refs[:parts]]
    slabs = nest(refs[parts:-2], shape)
    theirs_ref, target_ref = refs[-2:]
    for i in range(len(shape[0])):
        base = slab_ref[i] * (2 * plane)
        for k in range(plane // block):
            start = pl.multiple_of(base + piece_ref[1, k] * block, block)
            at = i * plane + k * block
            target_ref[:, pl.ds(start, block)] = theirs_ref[:, at : at + block]
        for low, total in slab_terms(grads, slabs, i):
            total = total.astype(jnp.bfloat16)
            for j in range(total.shape[1] // block):
                k = low // block + j
                start = pl.multiple_of(base + piece_ref[0, k] * block, block)
                target_ref[:, pl.ds(start, block)] = total[:, j * block : (j + 1) * block]


VMEM = pl.BlockSpec(memory_space=pltpu.VMEM)


def pieces_of(slabs, pieces, block):
    at = slabs[None, :, None] * pieces.size + pieces[:, None, :]
    return at[..., None] * block + jnp.arange(block)


def pick_columns(source, slabs, pieces, block):
    rows, width = source.shape
    count, depth = slabs.shape[0], pieces.shape[1]
    half = depth * block
    if block % 128:
        at = pieces_of(slabs, pieces, block).reshape(2, -1)
        return source[:, at[0]], source[:, at[1]]
    part = jax.ShapeDtypeStruct((rows, width // 2), source.dtype)
    return pl.pallas_call(
        functools.partial(pick_kernel, block=block),
        grid_spec=pltpu.PrefetchScalarGridSpec(
            num_scalar_prefetch=2,
            grid=(count,),
            in_specs=[pl.BlockSpec((rows, 2 * half), lambda i, slab, piece: (0, slab[i]))],
            out_specs=[pl.BlockSpec((rows, half), lambda i, slab, piece: (0, i))] * 2,
        ),
        out_shape=[part, part],
        cost_estimate=pl.CostEstimate(
            flops=0, bytes_accessed=4 * rows * width, transcendentals=0
        ),
        name="pick_columns",
    )(slabs, pieces, source)


def grad_columns(grads, slabs):
    rows = grads[0].shape[0]
    shape = [[len(slab) for slab in part] for part in slabs]
    flat = [piece for part in slabs for slab in part for piece in slab]
    plane = sum(piece.shape[0] for piece in slabs[0][0])
    width = plane * len(shape[0])
    return pl.pallas_call(
        functools.partial(grad_kernel, shape=shape, plane=plane),
        in_specs=[VMEM] * (len(grads) + len(flat)),
        out_specs=VMEM,
        out_shape=jax.ShapeDtypeStruct((rows, width), jnp.bfloat16),
        compiler_params=pltpu.CompilerParams(vmem_limit_bytes=20 * 1024 * 1024),
        cost_estimate=pl.CostEstimate(
            flops=2 * rows * sum(piece.size for piece in flat),
            bytes_accessed=2 * sum(piece.size for piece in flat) + 2 * rows * width,
            transcendentals=0,
        ),
        name="grad_columns",
    )(*grads, *flat)


def grad_place(grads, slabs, theirs, places, pieces, block):
    rows, width = theirs.shape[0], 2 * theirs.shape[1]
    shape = [[len(slab) for slab in part] for part in slabs]
    flat = [piece for part in slabs for slab in part for piece in slab]
    plane = sum(piece.shape[0] for piece in slabs[0][0])
    if block % 128:
        at = pieces_of(places, pieces, block).reshape(2, -1)
        target = jnp.zeros((rows, width), theirs.dtype)
        return target.at[:, at[0]].set(grad_columns(grads, slabs)).at[:, at[1]].set(theirs)
    return pl.pallas_call(
        functools.partial(grad_place_kernel, shape=shape, plane=plane, block=block),
        grid_spec=pltpu.PrefetchScalarGridSpec(
            num_scalar_prefetch=2,
            grid=(),
            in_specs=[VMEM] * (len(grads) + len(flat) + 1),
            out_specs=VMEM,
        ),
        out_shape=jax.ShapeDtypeStruct((rows, width), jnp.bfloat16),
        compiler_params=pltpu.CompilerParams(vmem_limit_bytes=20 * 1024 * 1024),
        cost_estimate=pl.CostEstimate(
            flops=2 * rows * sum(piece.size for piece in flat),
            bytes_accessed=2 * sum(piece.size for piece in flat) + 3 * rows * width,
            transcendentals=0,
        ),
        name="grad_place",
    )(places, pieces, *grads, *flat, theirs)


def dot(a, b, left, right):
    return lax.dot_general(
        a, b, (((left,), (right,)), ((), ())), preferred_element_type=jnp.float32
    )


def project_kernel(*refs, counts, more):
    count = 2 * len(counts)
    sources, refs = refs[:count], refs[count:]
    pieces, (own_ref, other_ref) = refs[: sum(counts)], refs[-2:]
    for half, target in ((1, other_ref), (0, own_ref)):
        total = refs[sum(counts) + half][...] if more else None
        left = iter(pieces)
        for i, number in enumerate(counts):
            source, at = sources[2 * i + half], 0
            for _ in range(number):
                piece = next(left)
                end = at + piece.shape[0]
                term = dot(source[:, at:end], piece[...], 1, 0)
                total = term if total is None else total + term
                at = end
        target[...] = total


def project_rows(mine, theirs, slabs, before=()):
    rows = mine.shape[0]
    flat = [piece for slab in slabs.values() for piece in slab]
    columns = flat[0].shape[1]
    operands, in_specs = [], []
    for i, slab in slabs.items():
        plane = sum(piece.shape[0] for piece in slab)
        operands += [mine, theirs]
        in_specs += [pl.BlockSpec((rows, plane), lambda _, i=i: (0, i))] * 2
    whole = [*flat, *before]
    in_specs += [pl.BlockSpec(array.shape, lambda _: (0, 0)) for array in whole]
    area = sum(piece.size for piece in flat)
    return pl.pallas_call(
        functools.partial(
            project_kernel, counts=[len(slab) for slab in slabs.values()], more=bool(before)
        ),
        grid=(1,),
        in_specs=in_specs,
        out_specs=[pl.BlockSpec((rows, columns), lambda _: (0, 0))] * 2,
        out_shape=[jax.ShapeDtypeStruct((rows, columns), jnp.float32)] * 2,
        compiler_params=pltpu.CompilerParams(vmem_limit_bytes=24 * 1024 * 1024),
        cost_estimate=pl.CostEstimate(
            flops=4 * rows * area,
            bytes_accessed=2 * area + 4 * rows * area // columns,
            transcendentals=0,
        ),
        name="project_rows",
    )(*operands, *whole)


def attend_kernel(*refs, group, head_dim, scale, last):
    q_own, q_other, grads, cos_ref, sin_ref, row_pos, key_pos, held = refs[:8]
    before = refs[8]
    attention_ref, grad_ref, term_ref = refs[-3:]
    keys, values = held[:, :head_dim], held[:, head_dim:]
    cos, sin = cos_ref[...], sin_ref[...]
    allowed = key_pos[...] <= row_pos[...]
    key_term = value_term = None
    for h in range(group):
        at = slice(h * head_dim, (h + 1) * head_dim)
        q = q_own[:, at] + q_other[:, at]
        q = (q * cos + pltpu.roll(q, head_dim // 2, 1) * sin).astype(jnp.bfloat16)
        scores = jnp.where(allowed, dot(q, keys, 1, 1) * scale, MASKED)
        weight = jnp.exp(scores - jnp.max(scores, axis=1, keepdims=True))
        inverse = 1.0 / jnp.sum(weight, axis=1, keepdims=True)
        attention = (dot(weight.astype(jnp.bfloat16), values, 1, 0) * inverse).astype(jnp.bfloat16)
        attention_ref[:, at] = attention
        grad = grads[:, at]
        delta = jnp.sum(
            grad.astype(jnp.float32) * attention.astype(jnp.float32), axis=1, keepdims=True
        )
        probs = weight * inverse
        dscore = (probs * (dot(grad, values, 1, 1) - delta)).astype(jnp.bfloat16)
        grad_q = dot(dscore, keys, 1, 0) * scale
        grad_q = grad_q * cos - pltpu.roll(grad_q, head_dim // 2, 1) * sin
        grad_ref[:, at] = grad_q.astype(jnp.bfloat16)
        key_new = dot(dscore, q, 0, 0) * scale
        value_new = dot(probs.astype(jnp.bfloat16), grad, 0, 0)
        key_term = key_new if h == 0 else key_term + key_new
        value_term = value_new if h == 0 else value_term + value_new
    if last:
        key_term = key_term + before[:, :head_dim]
        value_term = value_term + before[:, head_dim:]
    term_ref[:, :head_dim] = key_term.astype(term_ref.dtype)
    term_ref[:, head_dim:] = value_term.astype(term_ref.dtype)


def attend(q_own, q_other, grads, cos, sin, row_pos, key_pos, key_values, before, scale):
    rows, columns = q_own.shape
    head_dim = cos.shape[1]
    keys = key_values.shape[0]
    group = columns // head_dim
    last = before is not None
    operands = [q_own, q_other, grads, cos, sin, row_pos, key_pos, key_values]
    operands += [before] if last else []
    return pl.pallas_call(
        functools.partial(attend_kernel, group=group, head_dim=head_dim, scale=scale, last=last),
        in_specs=[VMEM] * len(operands),
        out_specs=[VMEM] * 3,
        out_shape=[
            jax.ShapeDtypeStruct((rows, columns), jnp.bfloat16),
            jax.ShapeDtypeStruct((rows, columns), jnp.bfloat16),
            jax.ShapeDtypeStruct(key_values.shape, jnp.bfloat16 if last else jnp.float32),
        ],
        compiler_params=pltpu.CompilerParams(vmem_limit_bytes=20 * 1024 * 1024),
        cost_estimate=pl.CostEstimate(
            flops=14 * rows * keys * columns,
            bytes_accessed=8 * keys * 2 * head_dim,
            transcendentals=rows * keys * group,
        ),
        name="attend",
    )(*operands)


def finish_kernel(own, other, cos_ref, sin_ref, out):
    head_dim = cos_ref.shape[1]
    total = own[...] + other[...]
    key = total[:, :head_dim]
    key = key * cos_ref[...] + pltpu.roll(key, head_dim // 2, 1) * sin_ref[...]
    out[:, :head_dim] = key.astype(jnp.bfloat16)
    out[:, head_dim:] = total[:, head_dim:].astype(jnp.bfloat16)


def finish_keys(own, other, cos, sin):
    return pl.pallas_call(
        finish_kernel,
        in_specs=[VMEM] * 4,
        out_specs=VMEM,
        out_shape=jax.ShapeDtypeStruct(own.shape, jnp.bfloat16),
        name="finish_keys",
    )(own, other, cos, sin)


def undo_kernel(pieces, cos_ref, sin_ref, out):
    head_dim = cos_ref.shape[1]
    total = pieces[0].astype(jnp.float32)
    for k in range(1, pieces.shape[0]):
        total = total + pieces[k].astype(jnp.float32)
    key = total[:, :head_dim]
    key = key * cos_ref[...] - pltpu.roll(key, head_dim // 2, 1) * sin_ref[...]
    out[:, :head_dim] = key.astype(jnp.bfloat16)
    out[:, head_dim:] = total[:, head_dim:].astype(jnp.bfloat16)


def undo_keys(pieces, cos, sin):
    return pl.pallas_call(
        undo_kernel,
        in_specs=[VMEM] * 3,
        out_specs=VMEM,
        out_shape=jax.ShapeDtypeStruct(pieces.shape[1:], jnp.bfloat16),
        name="undo_keys",
    )(pieces, cos, sin)


def body(tokens, positions, query_weight, key_weight, value_weight, grad_output):
    token_rows = tokens[0]
    rows, width = token_rows.shape
    head_dim = key_weight.shape[1]
    query_width = query_weight.shape[1]
    heads = query_width // head_dim
    group = heads // 2
    scale = head_dim ** (-0.5)
    size_a, size_b, ctx = lax.axis_size("a"), lax.axis_size("b"), lax.axis_size("ctx")
    at_a, at_b = lax.axis_index("a"), lax.axis_index("b")
    core, place = lax.axis_index("core"), lax.axis_index("ctx")
    block = query_weight.shape[0]
    plane = ctx * block

    kv_local = jnp.concatenate([key_weight, value_weight], axis=1).astype(jnp.bfloat16)
    da, db = jnp.meshgrid(jnp.arange(size_a), jnp.arange(size_b), indexing="ij")
    slabs = ((at_a + size_a - da) % size_a) * size_b + (at_b + size_b - db) % size_b
    slabs = slabs.reshape(-1).astype(jnp.int32)
    line = jnp.arange(ctx)
    pieces = jnp.stack([core * ctx + line, (1 - core) * ctx + line]).astype(jnp.int32)
    mine, theirs = pick_columns(token_rows, slabs, pieces, block)
    kv_line, _ = stage(gather_line(kv_local), mine)
    theirs = swap(after(theirs, kv_line))
    half = query_width // 2
    q_local = [query_weight[:, g * half : (g + 1) * half].astype(jnp.bfloat16) for g in range(2)]

    count_a, count_b = size_a - 1, size_b - 1
    kv_sides = along(kv_line, "a") + along(kv_line, "b")
    there = stage(*kv_sides, gather_line(after(q_local[0], kv_line)))
    kv_a, kv_b, q_line = there[:count_a], there[count_a:-1], there[-1:]
    kv_corners = gather_corners(kv_a, kv_b, "b")
    q0_a = along(q_line[0], "a")
    corners = [piece for corner in kv_corners.values() for piece in corner]
    there = stage(*q0_a, *corners, gather_line(after(q_local[1], *kv_a)))
    q0_a = there[:count_a]
    q_line.append(there[-1])
    q1_a = along(q_line[1], "a")
    q0_b = along(after(q_line[0], *q0_a), "b")
    kv_slabs = in_order(kv_line, kv_a, kv_b, kv_corners)

    positions = after(positions, kv_line)
    own_positions = lax.dynamic_slice_in_dim(positions, place * rows, rows)
    cos_table, sin_table = rope_tables(own_positions, head_dim)
    sin_table = jnp.where(jnp.arange(head_dim) < head_dim // 2, -sin_table, sin_table)
    def project(slabs):
        early = {i: slab for i, slab in enumerate(slabs) if (i // size_b) * (i % size_b) == 0}
        late = {i: slab for i, slab in enumerate(slabs) if i not in early}
        part = project_rows(mine, theirs, early)
        own, other = project_rows(mine, theirs, late, part)
        return own, swap(other)

    columns = jnp.concatenate([after(mine, *q0_a), theirs], axis=0)

    def terms_of(own, other):
        both = jnp.concatenate([own, other], axis=0)

        def make(i, part, extra=()):
            start, stop, _ = part.indices(plane)
            at = slice(i * plane + start, i * plane + stop)
            term = mm(columns[:, at], both, ((0,), (0,)))
            for piece in extra:
                term = term + piece.astype(jnp.float32)
            return term.astype(jnp.bfloat16)

        return make

    own, other = project_rows(mine, theirs, dict(enumerate(kv_slabs)))
    key_value = finish_keys(own, swap(other), cos_table, sin_table)
    key_value, *there = stage(key_value, *q1_a, *q0_b)
    q1_a, q0_b = there[:count_a], there[count_a:]
    q0_corners = gather_corners(q0_a, q0_b, "a")
    q1_b = along(after(q_line[1], key_value), "b")
    key_values = gather_line(key_value)
    corners = [piece for corner in q0_corners.values() for piece in corner]
    there = stage(*q1_b, *corners, key_values)
    q1_b, key_values = there[:count_b], there[-1]
    q1_corners = gather_corners(after_all(q1_a, *there), q1_b, "both")
    q_slabs = [
        in_order(q_line[0], q0_a, q0_b, q0_corners),
        in_order(q_line[1], q1_a, q1_b, q1_corners),
    ]
    attentions, gradients, made, came = [], [], [], []
    mid = plane // 2
    term = None
    for g in range(2):
        span = slice(g * group * head_dim, (g + 1) * group * head_dim)
        attention, grad_q, term = attend(
            *project(q_slabs[g]),
            grad_output[0][:, span],
            cos_table,
            sin_table,
            own_positions[:, None],
            positions[None, :],
            key_values,
            term,
            scale,
        )
        attentions.append(attention)
        grads = (grad_q, swap(grad_q))
        gradients.append(grads)
        made.append(terms_of(*grads))
        came.append(reduce_corners(made[g], "ba"[g], mid))
    summed = scatter_line(after(term, *came[1][2]))
    first = [*came[0][0].values(), *came[0][1].values()]
    second = [*came[1][0].values(), *came[1][1].values()]
    sides0, went0 = reduce_sides(made[0], came[0], "b", mid, *first, summed)
    grad_kv = undo_keys(after(summed, *first, *second, *went0), cos_table, sin_table)
    gradients.append((grad_kv, swap(grad_kv)))
    made.append(terms_of(*gradients[2]))
    came.append(reduce_corners(made[2], "both", mid))
    third = [*came[2][0].values(), *came[2][1].values()]
    sides1, went1 = reduce_sides(made[1], came[1], "a", mid, *sides0, *third)
    line0 = after(made[0](0, slice(None), sides0), *went1)
    q_grads = [reduce_line(line0, sides1)]
    line1 = made[1](0, slice(None), sides1)
    kv_sides, _ = reduce_sides(made[2], came[2], "both", mid, *sides1, q_grads[0])
    q_grads.append(reduce_line(line1, kv_sides))

    weights = [*q_slabs, kv_slabs]
    grad_theirs = grad_columns(
        [gradients[0][1], gradients[1][1], after(gradients[2][1], *third)], weights
    )
    grad_theirs = swap(grad_theirs)
    grad_input = grad_place(
        [gradients[0][0], gradients[1][0], gradients[2][0]], weights, grad_theirs, slabs, pieces, block
    )
    kv_line = after(made[2](0, slice(None), kv_sides), q_grads[1])
    kv_wgrad = reduce_line(kv_line, (grad_input,))

    query_grad = jnp.concatenate(q_grads, axis=1)
    key_grad = kv_wgrad[:, :head_dim]
    value_grad = kv_wgrad[:, head_dim:]
    attention_rows = jnp.concatenate(attentions, axis=1)
    return (attention_rows[None], grad_input[None], query_grad, key_grad, value_grad)


def solution(mesh):
    dp, ctx = mesh.devices.shape
    fine = Mesh(mesh.devices.reshape(dp // 4, 2, 2, ctx), ("a", "b", "core", "ctx"))
    batch = P(("a", "b", "core"), "ctx", None)
    master = P(("a", "b", "core", "ctx"), None)
    in_specs = (batch, P(), master, master, master, batch)
    out_specs = (batch, batch, master, master, master)
    return jax.shard_map(body, mesh=fine, in_specs=in_specs, out_specs=out_specs, check_vma=False)
```

```python
import functools

import jax
import jax.numpy as jnp
from jax import lax
from jax.experimental import pallas as pl
from jax.experimental.pallas import tpu as pltpu
from jax.sharding import Mesh, PartitionSpec as P

ROPE_BASE = 1000000.0
MASKED = -1e30


def rope_tables(positions_in, head_dim):
    half_width = head_dim // 2
    exponent = jnp.arange(half_width).astype(jnp.float32) * (2.0 / head_dim)
    frequency = jnp.power(ROPE_BASE, -exponent)
    angles = positions_in.astype(jnp.float32)[:, None] * frequency[None, :]
    angles = jnp.concatenate([angles, angles], axis=1)
    return (jnp.cos(angles), jnp.sin(angles))


def mm(a, b, dims):
    return lax.dot_general(a, b, (dims, ((), ())), preferred_element_type=jnp.float32)


def shift(block, axis, step):
    size = lax.axis_size(axis)
    return lax.ppermute(block, axis, [(i, (i + step) % size) for i in range(size)])


def after(block, *others):
    return lax.optimization_barrier((block, *others))[0]


def after_all(blocks, *others):
    return [after(block, *others) for block in blocks]


def swap(block):
    return shift(block, "core", 1)


def gather_line(block):
    return [block] + [shift(block, "ctx", k) for k in range(1, lax.axis_size("ctx"))]


def along(block, axis):
    return [shift(block, axis, step) for step in range(1, lax.axis_size(axis))]


def gather_corners(sides_a, sides_b, way, *deps):
    corners = {}
    for da, side_a in enumerate(sides_a, 1):
        for db, side_b in enumerate(sides_b, 1):
            mid = side_a.shape[0] // 2
            if way == "b":
                corners[da, db] = [shift(after(side_a, *deps), "b", db)]
            elif way == "a":
                corners[da, db] = [shift(after(side_b, *deps), "a", da)]
            else:
                corners[da, db] = [
                    shift(after(side_a[:mid], *deps), "b", db),
                    shift(after(side_b[mid:], *deps), "a", da),
                ]
    return corners


def in_order(block, sides_a, sides_b, corners):
    slabs = [[block]] + [[side] for side in sides_b]
    for da, side in enumerate(sides_a, 1):
        slabs.append([side])
        slabs += [corners[da, db] for db in range(1, len(sides_b) + 1)]
    return slabs


def reduce_corners(make, way, split):
    size_b = lax.axis_size("b")
    whole, top, low = slice(None), slice(0, split), slice(split, None)
    came_a, came_b, went = {}, {}, []
    for da in range(1, lax.axis_size("a")):
        for db in range(1, size_b):
            i = da * size_b + db
            went += [make(i, rows) for rows in ((top, low) if way == "both" else (whole,))]
            if way != "a":
                came_a[da, db] = shift(went[-2 if way == "both" else -1], "b", -db)
            if way != "b":
                came_b[da, db] = shift(went[-1], "a", -da)
    return came_a, came_b, went


def reduce_sides(make, came, way, split, *deps):
    size_a, size_b = lax.axis_size("a"), lax.axis_size("b")
    whole, top, low = slice(None), slice(0, split), slice(split, None)

    def side(i, extra, part):
        if not extra or way != "both":
            term = make(i, whole, extra)
        else:
            halves = [make(i, rows, extra if rows == part else []) for rows in (top, low)]
            term = jnp.concatenate(halves, axis=0)
        return after(term, *deps) if deps else term

    went, arrived = [], []
    for da in range(1, size_a):
        extra = [piece for (at, _), piece in came[0].items() if at == da]
        went.append(side(da * size_b, extra, top))
        arrived.append(shift(went[-1], "a", -da))
    for db in range(1, size_b):
        extra = [piece for (_, at), piece in came[1].items() if at == db]
        went.append(side(db, extra, low))
        arrived.append(shift(went[-1], "b", -db))
    return arrived, went


def reduce_line(term, last=()):
    size = lax.axis_size("ctx")
    rows = term.shape[0] // size
    total = after(term[:rows], *last).astype(jnp.float32)
    for k in range(1, size):
        total = total + shift(term[k * rows : (k + 1) * rows], "ctx", -k).astype(jnp.float32)
    return total


def pick_kernel(slab_ref, piece_ref, source_ref, mine_ref, theirs_ref, *, block):
    for k in range(mine_ref.shape[1] // block):
        to = slice(k * block, (k + 1) * block)
        start = pl.multiple_of(piece_ref[0, k] * block, block)
        mine_ref[:, to] = source_ref[:, pl.ds(start, block)]
        start = pl.multiple_of(piece_ref[1, k] * block, block)
        theirs_ref[:, to] = source_ref[:, pl.ds(start, block)]


def slab_terms(grads, slabs, i):
    cuts = {0}
    for part in slabs:
        at = 0
        for piece in part[i]:
            at += piece.shape[0]
            cuts.add(at)
    cuts = sorted(cuts)
    for low, high in zip(cuts[:-1], cuts[1:]):
        total = None
        for grad, part in zip(grads, slabs):
            at = 0
            for piece in part[i]:
                if at <= low and high <= at + piece.shape[0]:
                    term = dot(grad, piece[low - at : high - at, :], 1, 1)
                    total = term if total is None else total + term
                at += piece.shape[0]
        yield low, total


def nest(refs, shape):
    refs = iter(refs)
    return [[[next(refs) for _ in range(count)] for count in part] for part in shape]


def grad_kernel(*refs, shape, plane):
    parts = len(shape)
    grads = [ref[...] for ref in refs[:parts]]
    slabs = nest(refs[parts:-1], shape)
    for i in range(len(shape[0])):
        for low, total in slab_terms(grads, slabs, i):
            start = i * plane + low
            refs[-1][:, start : start + total.shape[1]] = total.astype(jnp.bfloat16)


def grad_place_kernel(*refs, shape, plane, block):
    slab_ref, piece_ref, *refs = refs
    parts = len(shape)
    grads = [ref[...] for ref in refs[:parts]]
    slabs = nest(refs[parts:-2], shape)
    theirs_ref, target_ref = refs[-2:]
    for i in range(len(shape[0])):
        base = slab_ref[i] * (2 * plane)
        for k in range(plane // block):
            start = pl.multiple_of(base + piece_ref[1, k] * block, block)
            at = i * plane + k * block
            target_ref[:, pl.ds(start, block)] = theirs_ref[:, at : at + block]
        for low, total in slab_terms(grads, slabs, i):
            total = total.astype(jnp.bfloat16)
            for j in range(total.shape[1] // block):
                k = low // block + j
                start = pl.multiple_of(base + piece_ref[0, k] * block, block)
                target_ref[:, pl.ds(start, block)] = total[:, j * block : (j + 1) * block]


VMEM = pl.BlockSpec(memory_space=pltpu.VMEM)


def pieces_of(slabs, pieces, block):
    at = slabs[None, :, None] * pieces.size + pieces[:, None, :]
    return at[..., None] * block + jnp.arange(block)


def pick_columns(source, slabs, pieces, block):
    rows, width = source.shape
    count, depth = slabs.shape[0], pieces.shape[1]
    half = depth * block
    if block % 128:
        at = pieces_of(slabs, pieces, block).reshape(2, -1)
        return source[:, at[0]], source[:, at[1]]
    part = jax.ShapeDtypeStruct((rows, width // 2), source.dtype)
    return pl.pallas_call(
        functools.partial(pick_kernel, block=block),
        grid_spec=pltpu.PrefetchScalarGridSpec(
            num_scalar_prefetch=2,
            grid=(count,),
            in_specs=[pl.BlockSpec((rows, 2 * half), lambda i, slab, piece: (0, slab[i]))],
            out_specs=[pl.BlockSpec((rows, half), lambda i, slab, piece: (0, i))] * 2,
        ),
        out_shape=[part, part],
        cost_estimate=pl.CostEstimate(
            flops=0, bytes_accessed=4 * rows * width, transcendentals=0
        ),
        name="pick_columns",
    )(slabs, pieces, source)


def grad_columns(grads, slabs):
    rows = grads[0].shape[0]
    shape = [[len(slab) for slab in part] for part in slabs]
    flat = [piece for part in slabs for slab in part for piece in slab]
    plane = sum(piece.shape[0] for piece in slabs[0][0])
    width = plane * len(shape[0])
    return pl.pallas_call(
        functools.partial(grad_kernel, shape=shape, plane=plane),
        in_specs=[VMEM] * (len(grads) + len(flat)),
        out_specs=VMEM,
        out_shape=jax.ShapeDtypeStruct((rows, width), jnp.bfloat16),
        compiler_params=pltpu.CompilerParams(vmem_limit_bytes=20 * 1024 * 1024),
        cost_estimate=pl.CostEstimate(
            flops=2 * rows * sum(piece.size for piece in flat),
            bytes_accessed=2 * sum(piece.size for piece in flat) + 2 * rows * width,
            transcendentals=0,
        ),
        name="grad_columns",
    )(*grads, *flat)


def grad_place(grads, slabs, theirs, places, pieces, block):
    rows, width = theirs.shape[0], 2 * theirs.shape[1]
    shape = [[len(slab) for slab in part] for part in slabs]
    flat = [piece for part in slabs for slab in part for piece in slab]
    plane = sum(piece.shape[0] for piece in slabs[0][0])
    if block % 128:
        at = pieces_of(places, pieces, block).reshape(2, -1)
        target = jnp.zeros((rows, width), theirs.dtype)
        return target.at[:, at[0]].set(grad_columns(grads, slabs)).at[:, at[1]].set(theirs)
    return pl.pallas_call(
        functools.partial(grad_place_kernel, shape=shape, plane=plane, block=block),
        grid_spec=pltpu.PrefetchScalarGridSpec(
            num_scalar_prefetch=2,
            grid=(),
            in_specs=[VMEM] * (len(grads) + len(flat) + 1),
            out_specs=VMEM,
        ),
        out_shape=jax.ShapeDtypeStruct((rows, width), jnp.bfloat16),
        compiler_params=pltpu.CompilerParams(vmem_limit_bytes=20 * 1024 * 1024),
        cost_estimate=pl.CostEstimate(
            flops=2 * rows * sum(piece.size for piece in flat),
            bytes_accessed=2 * sum(piece.size for piece in flat) + 3 * rows * width,
            transcendentals=0,
        ),
        name="grad_place",
    )(places, pieces, *grads, *flat, theirs)


def dot(a, b, left, right):
    return lax.dot_general(
        a, b, (((left,), (right,)), ((), ())), preferred_element_type=jnp.float32
    )


def project_kernel(*refs, counts, more):
    count = 2 * len(counts)
    sources, refs = refs[:count], refs[count:]
    pieces, (own_ref, other_ref) = refs[: sum(counts)], refs[-2:]
    for half, target in ((1, other_ref), (0, own_ref)):
        total = refs[sum(counts) + half][...] if more else None
        left = iter(pieces)
        for i, number in enumerate(counts):
            source, at = sources[2 * i + half], 0
            for _ in range(number):
                piece = next(left)
                end = at + piece.shape[0]
                term = dot(source[:, at:end], piece[...], 1, 0)
                total = term if total is None else total + term
                at = end
        target[...] = total


def project_rows(mine, theirs, slabs, before=()):
    rows = mine.shape[0]
    flat = [piece for slab in slabs.values() for piece in slab]
    columns = flat[0].shape[1]
    operands, in_specs = [], []
    for i, slab in slabs.items():
        plane = sum(piece.shape[0] for piece in slab)
        operands += [mine, theirs]
        in_specs += [pl.BlockSpec((rows, plane), lambda _, i=i: (0, i))] * 2
    whole = [*flat, *before]
    in_specs += [pl.BlockSpec(array.shape, lambda _: (0, 0)) for array in whole]
    area = sum(piece.size for piece in flat)
    return pl.pallas_call(
        functools.partial(
            project_kernel, counts=[len(slab) for slab in slabs.values()], more=bool(before)
        ),
        grid=(1,),
        in_specs=in_specs,
        out_specs=[pl.BlockSpec((rows, columns), lambda _: (0, 0))] * 2,
        out_shape=[jax.ShapeDtypeStruct((rows, columns), jnp.float32)] * 2,
        compiler_params=pltpu.CompilerParams(vmem_limit_bytes=24 * 1024 * 1024),
        cost_estimate=pl.CostEstimate(
            flops=4 * rows * area,
            bytes_accessed=2 * area + 4 * rows * area // columns,
            transcendentals=0,
        ),
        name="project_rows",
    )(*operands, *whole)


def attend_kernel(*refs, group, parts, head_dim, scale, last):
    q_own, q_other, grads, cos_ref, sin_ref, row_pos, key_pos = refs[:7]
    pieces = refs[7 : 7 + parts]
    rest = refs[7 + parts :]
    if last:
        before, rest = rest[0], rest[1:]
    attention_ref, grad_ref = rest[:2]
    terms = rest[2:-1]
    held = rest[-1]
    rows = q_own.shape[0]
    for j in range(parts):
        held[j * rows : (j + 1) * rows, :] = pieces[j][...]
    keys, values = held[:, :head_dim], held[:, head_dim:]
    cos, sin = cos_ref[...], sin_ref[...]
    allowed = key_pos[...] <= row_pos[...]
    key_term = value_term = None
    for h in range(group):
        at = slice(h * head_dim, (h + 1) * head_dim)
        q = q_own[:, at] + q_other[:, at]
        q = (q * cos + pltpu.roll(q, head_dim // 2, 1) * sin).astype(jnp.bfloat16)
        scores = jnp.where(allowed, dot(q, keys, 1, 1) * scale, MASKED)
        weight = jnp.exp(scores - jnp.max(scores, axis=1, keepdims=True))
        inverse = 1.0 / jnp.sum(weight, axis=1, keepdims=True)
        attention = (dot(weight.astype(jnp.bfloat16), values, 1, 0) * inverse).astype(jnp.bfloat16)
        attention_ref[:, at] = attention
        grad = grads[:, at]
        delta = jnp.sum(
            grad.astype(jnp.float32) * attention.astype(jnp.float32), axis=1, keepdims=True
        )
        probs = weight * inverse
        dscore = (probs * (dot(grad, values, 1, 1) - delta)).astype(jnp.bfloat16)
        grad_q = dot(dscore, keys, 1, 0) * scale
        grad_q = grad_q * cos - pltpu.roll(grad_q, head_dim // 2, 1) * sin
        grad_ref[:, at] = grad_q.astype(jnp.bfloat16)
        key_new = dot(dscore, q, 0, 0) * scale
        value_new = dot(probs.astype(jnp.bfloat16), grad, 0, 0)
        key_term = key_new if h == 0 else key_term + key_new
        value_term = value_new if h == 0 else value_term + value_new
    if last:
        key_term = key_term + before[:, :head_dim]
        value_term = value_term + before[:, head_dim:]
        for j in range(parts):
            span = slice(j * rows, (j + 1) * rows)
            terms[j][:, :head_dim] = key_term[span].astype(terms[j].dtype)
            terms[j][:, head_dim:] = value_term[span].astype(terms[j].dtype)
    else:
        terms[0][:, :head_dim] = key_term
        terms[0][:, head_dim:] = value_term


def attend(q_own, q_other, grads, cos, sin, row_pos, key_pos, pieces, before, scale):
    rows, columns = q_own.shape
    head_dim = cos.shape[1]
    parts = len(pieces)
    last = before is not None
    keys = parts * rows
    group = columns // head_dim
    if last:
        terms = [jax.ShapeDtypeStruct((rows, 2 * head_dim), jnp.float32)]
        terms += [jax.ShapeDtypeStruct((rows, 2 * head_dim), jnp.bfloat16)] * (parts - 1)
    else:
        terms = [jax.ShapeDtypeStruct((keys, 2 * head_dim), jnp.float32)]
    out_shape = [jax.ShapeDtypeStruct((rows, columns), jnp.bfloat16)] * 2 + terms
    operands = [q_own, q_other, grads, cos, sin, row_pos, key_pos, *pieces]
    operands += [before] if last else []
    out = pl.pallas_call(
        functools.partial(
            attend_kernel, group=group, parts=parts, head_dim=head_dim, scale=scale, last=last
        ),
        in_specs=[VMEM] * len(operands),
        out_specs=[VMEM] * len(out_shape),
        out_shape=out_shape,
        scratch_shapes=[pltpu.VMEM((keys, 2 * head_dim), jnp.bfloat16)],
        compiler_params=pltpu.CompilerParams(vmem_limit_bytes=20 * 1024 * 1024),
        cost_estimate=pl.CostEstimate(
            flops=14 * rows * keys * columns,
            bytes_accessed=8 * keys * 2 * head_dim,
            transcendentals=rows * keys * group,
        ),
        name="attend",
    )(*operands)
    return out[0], out[1], out[2:]


def finish_kernel(own, other, cos_ref, sin_ref, out):
    head_dim = cos_ref.shape[1]
    total = own[...] + other[...]
    key = total[:, :head_dim]
    key = key * cos_ref[...] + pltpu.roll(key, head_dim // 2, 1) * sin_ref[...]
    out[:, :head_dim] = key.astype(jnp.bfloat16)
    out[:, head_dim:] = total[:, head_dim:].astype(jnp.bfloat16)


def finish_keys(own, other, cos, sin):
    return pl.pallas_call(
        finish_kernel,
        in_specs=[VMEM] * 4,
        out_specs=VMEM,
        out_shape=jax.ShapeDtypeStruct(own.shape, jnp.bfloat16),
        name="finish_keys",
    )(own, other, cos, sin)


def undo_kernel(*refs):
    pieces, (cos_ref, sin_ref, out) = refs[:-3], refs[-3:]
    head_dim = cos_ref.shape[1]
    total = pieces[0][...]
    for piece in pieces[1:]:
        total = total + piece[...].astype(jnp.float32)
    key = total[:, :head_dim]
    key = key * cos_ref[...] - pltpu.roll(key, head_dim // 2, 1) * sin_ref[...]
    out[:, :head_dim] = key.astype(jnp.bfloat16)
    out[:, head_dim:] = total[:, head_dim:].astype(jnp.bfloat16)


def undo_keys(pieces, cos, sin):
    return pl.pallas_call(
        undo_kernel,
        in_specs=[VMEM] * (len(pieces) + 2),
        out_specs=VMEM,
        out_shape=jax.ShapeDtypeStruct(pieces[0].shape, jnp.bfloat16),
        name="undo_keys",
    )(*pieces, cos, sin)


def body(tokens, positions, query_weight, key_weight, value_weight, grad_output):
    token_rows = tokens[0]
    rows, width = token_rows.shape
    head_dim = key_weight.shape[1]
    query_width = query_weight.shape[1]
    heads = query_width // head_dim
    group = heads // 2
    scale = head_dim ** (-0.5)
    size_a, size_b, ctx = lax.axis_size("a"), lax.axis_size("b"), lax.axis_size("ctx")
    at_a, at_b = lax.axis_index("a"), lax.axis_index("b")
    core, place = lax.axis_index("core"), lax.axis_index("ctx")
    block = query_weight.shape[0]
    plane = ctx * block

    kv_local = jnp.concatenate([key_weight, value_weight], axis=1).astype(jnp.bfloat16)
    da, db = jnp.meshgrid(jnp.arange(size_a), jnp.arange(size_b), indexing="ij")
    slabs = ((at_a + size_a - da) % size_a) * size_b + (at_b + size_b - db) % size_b
    slabs = slabs.reshape(-1).astype(jnp.int32)
    line = (place + ctx - jnp.arange(ctx)) % ctx
    pieces = jnp.stack([core * ctx + line, (1 - core) * ctx + line]).astype(jnp.int32)
    mine, theirs = pick_columns(token_rows, slabs, pieces, block)
    half = query_width // 2
    q_local = [query_weight[:, g * half : (g + 1) * half].astype(jnp.bfloat16) for g in range(2)]
    pieces_kv = gather_line(kv_local)
    kv_line = jnp.concatenate([after(pieces_kv[0], mine), *pieces_kv[1:]], axis=0)
    theirs = swap(after(theirs, kv_line))

    q_local = [after(local, theirs) for local in q_local]
    q_line = [jnp.concatenate(gather_line(local), axis=0) for local in q_local]
    kv_sides = along(kv_line, "a"), along(kv_line, "b")
    stage = kv_sides[0] + kv_sides[1] + q_line[:1]
    kv_corners = gather_corners(*kv_sides, "b", *stage)
    q0_a = along(after(q_line[0], *stage), "a")
    stage = q0_a + [piece for corner in kv_corners.values() for piece in corner]
    q1_a = along(after(q_line[1], *stage), "a")
    q0_b = along(after(q_line[0], *stage), "b")
    kv_slabs = in_order(kv_line, *kv_sides, kv_corners)

    positions = after(positions, kv_line)
    own_positions = lax.dynamic_slice_in_dim(positions, place * rows, rows)
    cos_table, sin_table = rope_tables(own_positions, head_dim)
    sin_table = jnp.where(jnp.arange(head_dim) < head_dim // 2, -sin_table, sin_table)
    key_positions = jnp.concatenate(
        [
            lax.dynamic_slice_in_dim(positions, ((place + ctx - k) % ctx) * rows, rows)
            for k in range(ctx)
        ]
    )

    def project(slabs, early_part):
        late = {i: slab for i, slab in enumerate(slabs) if (i // size_b) * (i % size_b) > 0}
        own, other = project_rows(mine, theirs, late, early_part)
        return own, swap(other)

    def project_early(slabs, *deps):
        early = {i: slab for i, slab in enumerate(slabs) if (i // size_b) * (i % size_b) == 0}
        early[0] = after_all(early[0], *deps) if deps else early[0]
        return project_rows(mine, theirs, early)

    columns = jnp.concatenate([after(mine, *q0_a), theirs], axis=0)

    def terms_of(own, other):
        both = jnp.concatenate([own, other], axis=0)

        def make(i, part, extra=()):
            start, stop, _ = part.indices(plane)
            at = slice(i * plane + start, i * plane + stop)
            term = mm(columns[:, at], both, ((0,), (0,)))
            for piece in extra:
                term = term + piece.astype(jnp.float32)
            return term.astype(jnp.bfloat16)

        return make

    own, other = project_rows(mine, theirs, dict(enumerate(kv_slabs)))
    key_value = finish_keys(own, swap(other), cos_table, sin_table)
    stage = q1_a + q0_b + [key_value]
    q0_corners = gather_corners(q0_a, q0_b, "a", *stage)
    q1_b = along(after(q_line[1], *stage), "b")
    part = project_early(in_order(q_line[0], q0_a, q0_b, q0_corners))
    key_values = gather_line(key_value)
    stage = q1_b + key_values + [piece for corner in q0_corners.values() for piece in corner]
    q1_corners = gather_corners(q1_a, q1_b, "both", *stage)
    q_slabs = [
        in_order(q_line[0], q0_a, q0_b, q0_corners),
        in_order(q_line[1], q1_a, q1_b, q1_corners),
    ]
    attentions, gradients, made, came = [], [], [], []
    mid = plane // 2
    term = None
    for g in range(2):
        span = slice(g * group * head_dim, (g + 1) * group * head_dim)
        if g == 1:
            part = project_early(q_slabs[1], term)
        own, other = project(q_slabs[g], part)
        if g == 1:
            own = after(own, *came[0][2])
        attention, grad_q, terms = attend(
            own,
            other,
            grad_output[0][:, span],
            cos_table,
            sin_table,
            own_positions[:, None],
            key_positions[None, :],
            key_values,
            term,
            scale,
        )
        term = terms[0]
        attentions.append(attention)
        grads = (grad_q, swap(grad_q))
        gradients.append(grads)
        made.append(terms_of(*grads))
        came.append(reduce_corners(made[g], "ba"[g], mid))
    summed = [terms[0]] + [shift(terms[k], "ctx", -k) for k in range(1, ctx)]
    first = [*came[0][0].values(), *came[0][1].values()]
    second = [*came[1][0].values(), *came[1][1].values()]
    sides0, went0 = reduce_sides(made[0], came[0], "b", mid, *first, *summed[1:])
    grad_kv = undo_keys(
        [after(summed[0], *first, *second, *went0), *summed[1:]], cos_table, sin_table
    )
    gradients.append((grad_kv, swap(grad_kv)))
    made.append(terms_of(*gradients[2]))
    came.append(reduce_corners(made[2], "both", mid))
    third = [*came[2][0].values(), *came[2][1].values()]
    sides1, went1 = reduce_sides(made[1], came[1], "a", mid, *sides0, *third)
    line0 = after(made[0](0, slice(None), sides0), *went1)
    q_grads = [reduce_line(line0, sides1)]
    line1 = made[1](0, slice(None), sides1)
    kv_sides, _ = reduce_sides(made[2], came[2], "both", mid, *sides1, q_grads[0])
    q_grads.append(reduce_line(line1, kv_sides))

    weights = [*q_slabs, kv_slabs]
    grad_theirs = grad_columns(
        [gradients[0][1], gradients[1][1], after(gradients[2][1], *third)], weights
    )
    grad_theirs = swap(grad_theirs)
    grad_input = grad_place(
        [gradients[0][0], gradients[1][0], gradients[2][0]], weights, grad_theirs, slabs, pieces, block
    )
    kv_line = after(made[2](0, slice(None), kv_sides), q_grads[1])
    kv_wgrad = reduce_line(kv_line, (grad_input,))

    query_grad = jnp.concatenate(q_grads, axis=1)
    key_grad = kv_wgrad[:, :head_dim]
    value_grad = kv_wgrad[:, head_dim:]
    attention_rows = jnp.concatenate(attentions, axis=1)
    return (attention_rows[None], grad_input[None], query_grad, key_grad, value_grad)


def solution(mesh):
    dp, ctx = mesh.devices.shape
    fine = Mesh(mesh.devices.reshape(dp // 4, 2, 2, ctx), ("a", "b", "core", "ctx"))
    batch = P(("a", "b", "core"), "ctx", None)
    master = P(("a", "b", "core", "ctx"), None)
    in_specs = (batch, P(), master, master, master, batch)
    out_specs = (batch, batch, master, master, master)
    return jax.shard_map(body, mesh=fine, in_specs=in_specs, out_specs=out_specs, check_vma=False)
```

```python
import functools

import jax
import jax.numpy as jnp
from jax import lax
from jax.experimental import pallas as pl
from jax.experimental.pallas import tpu as pltpu
from jax.sharding import Mesh, PartitionSpec as P

ROPE_BASE = 1000000.0
MASKED = -1e30


def rope_tables(positions_in, head_dim):
    half_width = head_dim // 2
    exponent = jnp.arange(half_width).astype(jnp.float32) * (2.0 / head_dim)
    frequency = jnp.power(ROPE_BASE, -exponent)
    angles = positions_in.astype(jnp.float32)[:, None] * frequency[None, :]
    angles = jnp.concatenate([angles, angles], axis=1)
    return (jnp.cos(angles), jnp.sin(angles))


def mm(a, b, dims):
    return lax.dot_general(a, b, (dims, ((), ())), preferred_element_type=jnp.float32)


def shift(block, axis, step):
    size = lax.axis_size(axis)
    return lax.ppermute(block, axis, [(i, (i + step) % size) for i in range(size)])


def after(block, *others):
    return lax.optimization_barrier((block, *others))[0]


def after_all(blocks, *others):
    return [after(block, *others) for block in blocks]


def swap(block):
    return shift(block, "core", 1)


def gather_line(block):
    return [block] + [shift(block, "ctx", k) for k in range(1, lax.axis_size("ctx"))]


def along(block, axis):
    return [shift(block, axis, step) for step in range(1, lax.axis_size(axis))]


def gather_corners(sides_a, sides_b, way, *deps):
    corners = {}
    for da, side_a in enumerate(sides_a, 1):
        for db, side_b in enumerate(sides_b, 1):
            mid = side_a.shape[0] // 2
            if way == "b":
                corners[da, db] = [shift(after(side_a, *deps), "b", db)]
            elif way == "a":
                corners[da, db] = [shift(after(side_b, *deps), "a", da)]
            else:
                corners[da, db] = [
                    shift(after(side_a[:mid], *deps), "b", db),
                    shift(after(side_b[mid:], *deps), "a", da),
                ]
    return corners


def in_order(block, sides_a, sides_b, corners):
    slabs = [[block]] + [[side] for side in sides_b]
    for da, side in enumerate(sides_a, 1):
        slabs.append([side])
        slabs += [corners[da, db] for db in range(1, len(sides_b) + 1)]
    return slabs


def reduce_corners(make, way, split):
    size_b = lax.axis_size("b")
    whole, top, low = slice(None), slice(0, split), slice(split, None)
    came_a, came_b, went = {}, {}, []
    for da in range(1, lax.axis_size("a")):
        for db in range(1, size_b):
            i = da * size_b + db
            went += [make(i, rows) for rows in ((top, low) if way == "both" else (whole,))]
            if way != "a":
                came_a[da, db] = shift(went[-2 if way == "both" else -1], "b", -db)
            if way != "b":
                came_b[da, db] = shift(went[-1], "a", -da)
    return came_a, came_b, went


def reduce_sides(make, came, way, split, *deps):
    size_a, size_b = lax.axis_size("a"), lax.axis_size("b")
    whole, top, low = slice(None), slice(0, split), slice(split, None)

    def side(i, extra, part):
        if not extra or way != "both":
            term = make(i, whole, extra)
        else:
            halves = [make(i, rows, extra if rows == part else []) for rows in (top, low)]
            term = jnp.concatenate(halves, axis=0)
        return after(term, *deps) if deps else term

    went, arrived = [], []
    for da in range(1, size_a):
        extra = [piece for (at, _), piece in came[0].items() if at == da]
        went.append(side(da * size_b, extra, top))
        arrived.append(shift(went[-1], "a", -da))
    for db in range(1, size_b):
        extra = [piece for (_, at), piece in came[1].items() if at == db]
        went.append(side(db, extra, low))
        arrived.append(shift(went[-1], "b", -db))
    return arrived, went


def send_line(term):
    size = lax.axis_size("ctx")
    rows = term.shape[0] // size
    return [term[:rows]] + [
        shift(term[k * rows : (k + 1) * rows], "ctx", -k) for k in range(1, size)
    ]


def add_line(pieces, last=()):
    total = after(pieces[0], *last).astype(jnp.float32)
    for piece in pieces[1:]:
        total = total + piece.astype(jnp.float32)
    return total


def pick_kernel(slab_ref, piece_ref, source_ref, mine_ref, theirs_ref, *, block):
    for k in range(mine_ref.shape[1] // block):
        to = slice(k * block, (k + 1) * block)
        start = pl.multiple_of(piece_ref[0, k] * block, block)
        mine_ref[:, to] = source_ref[:, pl.ds(start, block)]
        start = pl.multiple_of(piece_ref[1, k] * block, block)
        theirs_ref[:, to] = source_ref[:, pl.ds(start, block)]


def slab_terms(grads, slabs, i):
    cuts = {0}
    for part in slabs:
        at = 0
        for piece in part[i]:
            at += piece.shape[0]
            cuts.add(at)
    cuts = sorted(cuts)
    for low, high in zip(cuts[:-1], cuts[1:]):
        total = None
        for grad, part in zip(grads, slabs):
            at = 0
            for piece in part[i]:
                if at <= low and high <= at + piece.shape[0]:
                    term = dot(grad, piece[low - at : high - at, :], 1, 1)
                    total = term if total is None else total + term
                at += piece.shape[0]
        yield low, total


def nest(refs, shape):
    refs = iter(refs)
    return [[[next(refs) for _ in range(count)] for count in part] for part in shape]


def grad_kernel(*refs, shape, plane):
    parts = len(shape)
    grads = [ref[...] for ref in refs[:parts]]
    slabs = nest(refs[parts:-1], shape)
    for i in range(len(shape[0])):
        for low, total in slab_terms(grads, slabs, i):
            start = i * plane + low
            refs[-1][:, start : start + total.shape[1]] = total.astype(jnp.bfloat16)


def grad_place_kernel(*refs, shape, plane, block):
    slab_ref, piece_ref, *refs = refs
    parts = len(shape)
    grads = [ref[...] for ref in refs[:parts]]
    slabs = nest(refs[parts:-2], shape)
    theirs_ref, target_ref = refs[-2:]
    for i in range(len(shape[0])):
        base = slab_ref[i] * (2 * plane)
        for k in range(plane // block):
            start = pl.multiple_of(base + piece_ref[1, k] * block, block)
            at = i * plane + k * block
            target_ref[:, pl.ds(start, block)] = theirs_ref[:, at : at + block]
        for low, total in slab_terms(grads, slabs, i):
            total = total.astype(jnp.bfloat16)
            for j in range(total.shape[1] // block):
                k = low // block + j
                start = pl.multiple_of(base + piece_ref[0, k] * block, block)
                target_ref[:, pl.ds(start, block)] = total[:, j * block : (j + 1) * block]


VMEM = pl.BlockSpec(memory_space=pltpu.VMEM)


def pieces_of(slabs, pieces, block):
    at = slabs[None, :, None] * pieces.size + pieces[:, None, :]
    return at[..., None] * block + jnp.arange(block)


def pick_columns(source, slabs, pieces, block):
    rows, width = source.shape
    count, depth = slabs.shape[0], pieces.shape[1]
    half = depth * block
    if block % 128:
        at = pieces_of(slabs, pieces, block).reshape(2, -1)
        return source[:, at[0]], source[:, at[1]]
    part = jax.ShapeDtypeStruct((rows, width // 2), source.dtype)
    return pl.pallas_call(
        functools.partial(pick_kernel, block=block),
        grid_spec=pltpu.PrefetchScalarGridSpec(
            num_scalar_prefetch=2,
            grid=(count,),
            in_specs=[pl.BlockSpec((rows, 2 * half), lambda i, slab, piece: (0, slab[i]))],
            out_specs=[pl.BlockSpec((rows, half), lambda i, slab, piece: (0, i))] * 2,
        ),
        out_shape=[part, part],
        cost_estimate=pl.CostEstimate(
            flops=0, bytes_accessed=4 * rows * width, transcendentals=0
        ),
        name="pick_columns",
    )(slabs, pieces, source)


def grad_columns(grads, slabs):
    rows = grads[0].shape[0]
    shape = [[len(slab) for slab in part] for part in slabs]
    flat = [piece for part in slabs for slab in part for piece in slab]
    plane = sum(piece.shape[0] for piece in slabs[0][0])
    width = plane * len(shape[0])
    return pl.pallas_call(
        functools.partial(grad_kernel, shape=shape, plane=plane),
        in_specs=[VMEM] * (len(grads) + len(flat)),
        out_specs=VMEM,
        out_shape=jax.ShapeDtypeStruct((rows, width), jnp.bfloat16),
        compiler_params=pltpu.CompilerParams(vmem_limit_bytes=20 * 1024 * 1024),
        cost_estimate=pl.CostEstimate(
            flops=2 * rows * sum(piece.size for piece in flat),
            bytes_accessed=2 * sum(piece.size for piece in flat) + 2 * rows * width,
            transcendentals=0,
        ),
        name="grad_columns",
    )(*grads, *flat)


def grad_place(grads, slabs, theirs, places, pieces, block):
    rows, width = theirs.shape[0], 2 * theirs.shape[1]
    shape = [[len(slab) for slab in part] for part in slabs]
    flat = [piece for part in slabs for slab in part for piece in slab]
    plane = sum(piece.shape[0] for piece in slabs[0][0])
    if block % 128:
        at = pieces_of(places, pieces, block).reshape(2, -1)
        target = jnp.zeros((rows, width), theirs.dtype)
        return target.at[:, at[0]].set(grad_columns(grads, slabs)).at[:, at[1]].set(theirs)
    return pl.pallas_call(
        functools.partial(grad_place_kernel, shape=shape, plane=plane, block=block),
        grid_spec=pltpu.PrefetchScalarGridSpec(
            num_scalar_prefetch=2,
            grid=(),
            in_specs=[VMEM] * (len(grads) + len(flat) + 1),
            out_specs=VMEM,
        ),
        out_shape=jax.ShapeDtypeStruct((rows, width), jnp.bfloat16),
        compiler_params=pltpu.CompilerParams(vmem_limit_bytes=20 * 1024 * 1024),
        cost_estimate=pl.CostEstimate(
            flops=2 * rows * sum(piece.size for piece in flat),
            bytes_accessed=2 * sum(piece.size for piece in flat) + 3 * rows * width,
            transcendentals=0,
        ),
        name="grad_place",
    )(places, pieces, *grads, *flat, theirs)


def dot(a, b, left, right):
    return lax.dot_general(
        a, b, (((left,), (right,)), ((), ())), preferred_element_type=jnp.float32
    )


def project_kernel(*refs, counts, more):
    count = 2 * len(counts)
    sources, refs = refs[:count], refs[count:]
    pieces, (own_ref, other_ref) = refs[: sum(counts)], refs[-2:]
    for half, target in ((1, other_ref), (0, own_ref)):
        total = refs[sum(counts) + half][...] if more else None
        left = iter(pieces)
        for i, number in enumerate(counts):
            source, at = sources[2 * i + half], 0
            for _ in range(number):
                piece = next(left)
                end = at + piece.shape[0]
                term = dot(source[:, at:end], piece[...], 1, 0)
                total = term if total is None else total + term
                at = end
        target[...] = total


def project_rows(mine, theirs, slabs, before=()):
    rows = mine.shape[0]
    flat = [piece for slab in slabs.values() for piece in slab]
    columns = flat[0].shape[1]
    operands, in_specs = [], []
    for i, slab in slabs.items():
        plane = sum(piece.shape[0] for piece in slab)
        operands += [mine, theirs]
        in_specs += [pl.BlockSpec((rows, plane), lambda _, i=i: (0, i))] * 2
    whole = [*flat, *before]
    in_specs += [pl.BlockSpec(array.shape, lambda _: (0, 0)) for array in whole]
    area = sum(piece.size for piece in flat)
    return pl.pallas_call(
        functools.partial(
            project_kernel, counts=[len(slab) for slab in slabs.values()], more=bool(before)
        ),
        grid=(1,),
        in_specs=in_specs,
        out_specs=[pl.BlockSpec((rows, columns), lambda _: (0, 0))] * 2,
        out_shape=[jax.ShapeDtypeStruct((rows, columns), jnp.float32)] * 2,
        compiler_params=pltpu.CompilerParams(vmem_limit_bytes=24 * 1024 * 1024),
        cost_estimate=pl.CostEstimate(
            flops=4 * rows * area,
            bytes_accessed=2 * area + 4 * rows * area // columns,
            transcendentals=0,
        ),
        name="project_rows",
    )(*operands, *whole)


def attend_kernel(*refs, group, parts, head_dim, scale, last):
    q_own, q_other, grads, cos_ref, sin_ref, row_pos, key_pos = refs[:7]
    pieces = refs[7 : 7 + parts]
    rest = refs[7 + parts :]
    if last:
        before, rest = rest[0], rest[1:]
    attention_ref, grad_ref = rest[:2]
    terms = rest[2:-1]
    held = rest[-1]
    rows = q_own.shape[0]
    for j in range(parts):
        held[j * rows : (j + 1) * rows, :] = pieces[j][...]
    keys, values = held[:, :head_dim], held[:, head_dim:]
    cos, sin = cos_ref[...], sin_ref[...]
    allowed = key_pos[...] <= row_pos[...]
    key_term = value_term = None
    for h in range(group):
        at = slice(h * head_dim, (h + 1) * head_dim)
        q = q_own[:, at] + q_other[:, at]
        q = (q * cos + pltpu.roll(q, head_dim // 2, 1) * sin).astype(jnp.bfloat16)
        scores = jnp.where(allowed, dot(q, keys, 1, 1) * scale, MASKED)
        weight = jnp.exp(scores - jnp.max(scores, axis=1, keepdims=True))
        inverse = 1.0 / jnp.sum(weight, axis=1, keepdims=True)
        attention = (dot(weight.astype(jnp.bfloat16), values, 1, 0) * inverse).astype(jnp.bfloat16)
        attention_ref[:, at] = attention
        grad = grads[:, at]
        delta = jnp.sum(
            grad.astype(jnp.float32) * attention.astype(jnp.float32), axis=1, keepdims=True
        )
        probs = weight * inverse
        dscore = (probs * (dot(grad, values, 1, 1) - delta)).astype(jnp.bfloat16)
        grad_q = dot(dscore, keys, 1, 0) * scale
        grad_q = grad_q * cos - pltpu.roll(grad_q, head_dim // 2, 1) * sin
        grad_ref[:, at] = grad_q.astype(jnp.bfloat16)
        key_new = dot(dscore, q, 0, 0) * scale
        value_new = dot(probs.astype(jnp.bfloat16), grad, 0, 0)
        key_term = key_new if h == 0 else key_term + key_new
        value_term = value_new if h == 0 else value_term + value_new
    if last:
        key_term = key_term + before[:, :head_dim]
        value_term = value_term + before[:, head_dim:]
        for j in range(parts):
            span = slice(j * rows, (j + 1) * rows)
            terms[j][:, :head_dim] = key_term[span].astype(terms[j].dtype)
            terms[j][:, head_dim:] = value_term[span].astype(terms[j].dtype)
    else:
        terms[0][:, :head_dim] = key_term
        terms[0][:, head_dim:] = value_term


def attend(q_own, q_other, grads, cos, sin, row_pos, key_pos, pieces, before, scale):
    rows, columns = q_own.shape
    head_dim = cos.shape[1]
    parts = len(pieces)
    last = before is not None
    keys = parts * rows
    group = columns // head_dim
    if last:
        terms = [jax.ShapeDtypeStruct((rows, 2 * head_dim), jnp.float32)]
        terms += [jax.ShapeDtypeStruct((rows, 2 * head_dim), jnp.bfloat16)] * (parts - 1)
    else:
        terms = [jax.ShapeDtypeStruct((keys, 2 * head_dim), jnp.float32)]
    out_shape = [jax.ShapeDtypeStruct((rows, columns), jnp.bfloat16)] * 2 + terms
    operands = [q_own, q_other, grads, cos, sin, row_pos, key_pos, *pieces]
    operands += [before] if last else []
    out = pl.pallas_call(
        functools.partial(
            attend_kernel, group=group, parts=parts, head_dim=head_dim, scale=scale, last=last
        ),
        in_specs=[VMEM] * len(operands),
        out_specs=[VMEM] * len(out_shape),
        out_shape=out_shape,
        scratch_shapes=[pltpu.VMEM((keys, 2 * head_dim), jnp.bfloat16)],
        compiler_params=pltpu.CompilerParams(vmem_limit_bytes=20 * 1024 * 1024),
        cost_estimate=pl.CostEstimate(
            flops=14 * rows * keys * columns,
            bytes_accessed=8 * keys * 2 * head_dim,
            transcendentals=rows * keys * group,
        ),
        name="attend",
    )(*operands)
    return out[0], out[1], out[2:]


def finish_kernel(own, other, cos_ref, sin_ref, out):
    head_dim = cos_ref.shape[1]
    total = own[...] + other[...]
    key = total[:, :head_dim]
    key = key * cos_ref[...] + pltpu.roll(key, head_dim // 2, 1) * sin_ref[...]
    out[:, :head_dim] = key.astype(jnp.bfloat16)
    out[:, head_dim:] = total[:, head_dim:].astype(jnp.bfloat16)


def finish_keys(own, other, cos, sin):
    return pl.pallas_call(
        finish_kernel,
        in_specs=[VMEM] * 4,
        out_specs=VMEM,
        out_shape=jax.ShapeDtypeStruct(own.shape, jnp.bfloat16),
        name="finish_keys",
    )(own, other, cos, sin)


def undo_kernel(*refs):
    pieces, (cos_ref, sin_ref, out) = refs[:-3], refs[-3:]
    head_dim = cos_ref.shape[1]
    total = pieces[0][...]
    for piece in pieces[1:]:
        total = total + piece[...].astype(jnp.float32)
    key = total[:, :head_dim]
    key = key * cos_ref[...] - pltpu.roll(key, head_dim // 2, 1) * sin_ref[...]
    out[:, :head_dim] = key.astype(jnp.bfloat16)
    out[:, head_dim:] = total[:, head_dim:].astype(jnp.bfloat16)


def undo_keys(pieces, cos, sin):
    return pl.pallas_call(
        undo_kernel,
        in_specs=[VMEM] * (len(pieces) + 2),
        out_specs=VMEM,
        out_shape=jax.ShapeDtypeStruct(pieces[0].shape, jnp.bfloat16),
        name="undo_keys",
    )(*pieces, cos, sin)


def body(tokens, positions, query_weight, key_weight, value_weight, grad_output):
    token_rows = tokens[0]
    rows, width = token_rows.shape
    head_dim = key_weight.shape[1]
    query_width = query_weight.shape[1]
    heads = query_width // head_dim
    group = heads // 2
    scale = head_dim ** (-0.5)
    size_a, size_b, ctx = lax.axis_size("a"), lax.axis_size("b"), lax.axis_size("ctx")
    at_a, at_b = lax.axis_index("a"), lax.axis_index("b")
    core, place = lax.axis_index("core"), lax.axis_index("ctx")
    block = query_weight.shape[0]
    plane = ctx * block

    kv_local = jnp.concatenate([key_weight, value_weight], axis=1).astype(jnp.bfloat16)
    da, db = jnp.meshgrid(jnp.arange(size_a), jnp.arange(size_b), indexing="ij")
    slabs = ((at_a + size_a - da) % size_a) * size_b + (at_b + size_b - db) % size_b
    slabs = slabs.reshape(-1).astype(jnp.int32)
    line = (place + ctx - jnp.arange(ctx)) % ctx
    pieces = jnp.stack([core * ctx + line, (1 - core) * ctx + line]).astype(jnp.int32)
    mine, theirs = pick_columns(token_rows, slabs, pieces, block)
    half = query_width // 2
    q_local = [query_weight[:, g * half : (g + 1) * half].astype(jnp.bfloat16) for g in range(2)]
    pieces_kv = gather_line(kv_local)
    kv_line = jnp.concatenate([after(pieces_kv[0], mine), *pieces_kv[1:]], axis=0)
    theirs = swap(after(theirs, kv_line))

    q_local = [after(local, theirs) for local in q_local]
    q_line = [jnp.concatenate(gather_line(local), axis=0) for local in q_local]
    positions = after(positions, kv_line)
    own_positions = lax.dynamic_slice_in_dim(positions, place * rows, rows)
    cos_table, sin_table = rope_tables(own_positions, head_dim)
    sin_table = jnp.where(jnp.arange(head_dim) < head_dim // 2, -sin_table, sin_table)
    kv_sides = along(kv_line, "a"), along(kv_line, "b")
    stage = kv_sides[0] + kv_sides[1] + q_line[:1] + [cos_table, sin_table]
    kv_corners = gather_corners(*kv_sides, "b", *stage)
    q0_a = along(after(q_line[0], *stage), "a")
    stage = q0_a + [piece for corner in kv_corners.values() for piece in corner]
    q1_a = along(after(q_line[1], *stage), "a")
    q0_b = along(after(q_line[0], *stage), "b")
    kv_slabs = in_order(kv_line, *kv_sides, kv_corners)

    key_positions = jnp.concatenate(
        [
            lax.dynamic_slice_in_dim(positions, ((place + ctx - k) % ctx) * rows, rows)
            for k in range(ctx)
        ]
    )

    def project(slabs, early_part):
        late = {i: slab for i, slab in enumerate(slabs) if (i // size_b) * (i % size_b) > 0}
        own, other = project_rows(mine, theirs, late, early_part)
        return own, swap(other)

    def project_early(slabs, *deps):
        early = {i: slab for i, slab in enumerate(slabs) if (i // size_b) * (i % size_b) == 0}
        early[0] = after_all(early[0], *deps) if deps else early[0]
        return project_rows(mine, theirs, early)

    columns = jnp.concatenate([after(mine, *q0_a), theirs], axis=0)

    def terms_of(own, other):
        both = jnp.concatenate([own, other], axis=0)

        def make(i, part, extra=()):
            start, stop, _ = part.indices(plane)
            at = slice(i * plane + start, i * plane + stop)
            term = mm(columns[:, at], both, ((0,), (0,)))
            for piece in extra:
                term = term + piece.astype(jnp.float32)
            return term.astype(jnp.bfloat16)

        return make

    own, other = project_rows(mine, theirs, dict(enumerate(kv_slabs)))
    key_value = finish_keys(own, swap(other), cos_table, sin_table)
    stage = q1_a + q0_b + [key_value]
    q0_corners = gather_corners(q0_a, q0_b, "a", *stage)
    q1_b = along(after(q_line[1], *stage), "b")
    part = project_early(in_order(q_line[0], q0_a, q0_b, q0_corners))
    corners = [piece for corner in q0_corners.values() for piece in corner]
    key_values = gather_line(after(key_value, *corners))
    stage = q1_b + [piece for corner in q0_corners.values() for piece in corner]
    q1_corners = gather_corners(q1_a, q1_b, "both", *stage)
    q_slabs = [
        in_order(q_line[0], q0_a, q0_b, q0_corners),
        in_order(q_line[1], q1_a, q1_b, q1_corners),
    ]
    attentions, gradients, made, came = [], [], [], []
    mid = plane // 2
    term = None
    for g in range(2):
        span = slice(g * group * head_dim, (g + 1) * group * head_dim)
        if g == 1:
            part = project_early(q_slabs[1], term)
        own, other = project(q_slabs[g], part)
        if g == 1:
            own = after(own, *came[0][2])
        attention, grad_q, terms = attend(
            own,
            other,
            grad_output[0][:, span],
            cos_table,
            sin_table,
            own_positions[:, None],
            key_positions[None, :],
            key_values,
            term,
            scale,
        )
        term = terms[0]
        attentions.append(attention)
        grads = (grad_q, swap(grad_q))
        gradients.append(grads)
        made.append(terms_of(*grads))
        came.append(reduce_corners(made[g], "ba"[g], mid))
    summed = [terms[0]] + [shift(terms[k], "ctx", -k) for k in range(1, ctx)]
    first = [*came[0][0].values(), *came[0][1].values()]
    second = [*came[1][0].values(), *came[1][1].values()]
    sides0, went0 = reduce_sides(made[0], came[0], "b", mid, *first, *summed[1:])
    grad_kv = undo_keys(
        [after(summed[0], *first, *second, *went0), *summed[1:]], cos_table, sin_table
    )
    gradients.append((grad_kv, swap(grad_kv)))
    made.append(terms_of(*gradients[2]))
    came.append(reduce_corners(made[2], "both", mid))
    third = [*came[2][0].values(), *came[2][1].values()]
    sides1, went1 = reduce_sides(made[1], came[1], "a", mid, *sides0, *third)
    line0 = after(made[0](0, slice(None), sides0), *went1)
    sent0 = send_line(line0)
    q_grads = [add_line(sent0, sides1)]
    line1 = made[1](0, slice(None), sides1)
    kv_sides, _ = reduce_sides(made[2], came[2], "both", mid, *sides1, *sent0[1:-1])
    q_grads.append(add_line(send_line(line1), kv_sides))

    weights = [*q_slabs, kv_slabs]
    grad_theirs = grad_columns(
        [gradients[0][1], gradients[1][1], after(gradients[2][1], *third)], weights
    )
    grad_theirs = swap(grad_theirs)
    grad_input = grad_place(
        [gradients[0][0], gradients[1][0], gradients[2][0]], weights, grad_theirs, slabs, pieces, block
    )
    kv_term = after(made[2](0, slice(None), kv_sides), *q_grads)
    kv_wgrad = add_line(send_line(kv_term), (grad_input,))

    query_grad = jnp.concatenate(q_grads, axis=1)
    key_grad = kv_wgrad[:, :head_dim]
    value_grad = kv_wgrad[:, head_dim:]
    attention_rows = jnp.concatenate(attentions, axis=1)
    return (attention_rows[None], grad_input[None], query_grad, key_grad, value_grad)


def solution(mesh):
    dp, ctx = mesh.devices.shape
    fine = Mesh(mesh.devices.reshape(dp // 4, 2, 2, ctx), ("a", "b", "core", "ctx"))
    batch = P(("a", "b", "core"), "ctx", None)
    master = P(("a", "b", "core", "ctx"), None)
    in_specs = (batch, P(), master, master, master, batch)
    out_specs = (batch, batch, master, master, master)
    return jax.shard_map(body, mesh=fine, in_specs=in_specs, out_specs=out_specs, check_vma=False)
```

```python
import functools

import jax
import jax.numpy as jnp
from jax import lax
from jax.experimental import pallas as pl
from jax.experimental.pallas import tpu as pltpu
from jax.sharding import Mesh, PartitionSpec as P

ROPE_BASE = 1000000.0
MASKED = -1e30


def rope_tables(positions_in, head_dim):
    half_width = head_dim // 2
    exponent = jnp.arange(half_width).astype(jnp.float32) * (2.0 / head_dim)
    frequency = jnp.power(ROPE_BASE, -exponent)
    angles = positions_in.astype(jnp.float32)[:, None] * frequency[None, :]
    angles = jnp.concatenate([angles, angles], axis=1)
    return (jnp.cos(angles), jnp.sin(angles))


def mm(a, b, dims):
    return lax.dot_general(a, b, (dims, ((), ())), preferred_element_type=jnp.float32)


def shift(block, axis, step):
    size = lax.axis_size(axis)
    return lax.ppermute(block, axis, [(i, (i + step) % size) for i in range(size)])


def after(block, *others):
    return lax.optimization_barrier((block, *others))[0]


def after_all(blocks, *others):
    return [after(block, *others) for block in blocks]


def swap(block):
    return shift(block, "core", 1)


def gather_line(block):
    return [block] + [shift(block, "ctx", k) for k in range(1, lax.axis_size("ctx"))]


def along(block, axis):
    return [shift(block, axis, step) for step in range(1, lax.axis_size(axis))]


def gather_corners(sides_a, sides_b, way, *deps):
    corners = {}
    for da, side_a in enumerate(sides_a, 1):
        for db, side_b in enumerate(sides_b, 1):
            mid = side_a.shape[0] // 2
            if way == "b":
                corners[da, db] = [shift(after(side_a, *deps), "b", db)]
            elif way == "a":
                corners[da, db] = [shift(after(side_b, *deps), "a", da)]
            else:
                corners[da, db] = [
                    shift(after(side_a[:mid], *deps), "b", db),
                    shift(after(side_b[mid:], *deps), "a", da),
                ]
    return corners


def in_order(block, sides_a, sides_b, corners):
    slabs = [[block]] + [[side] for side in sides_b]
    for da, side in enumerate(sides_a, 1):
        slabs.append([side])
        slabs += [corners[da, db] for db in range(1, len(sides_b) + 1)]
    return slabs


def reduce_corners(make, way, split):
    size_b = lax.axis_size("b")
    whole, top, low = slice(None), slice(0, split), slice(split, None)
    came_a, came_b, went = {}, {}, []
    for da in range(1, lax.axis_size("a")):
        for db in range(1, size_b):
            i = da * size_b + db
            went += [make(i, rows) for rows in ((top, low) if way == "both" else (whole,))]
            if way != "a":
                came_a[da, db] = shift(went[-2 if way == "both" else -1], "b", -db)
            if way != "b":
                came_b[da, db] = shift(went[-1], "a", -da)
    return came_a, came_b, went


def reduce_sides(make, came, way, split, *deps):
    size_a, size_b = lax.axis_size("a"), lax.axis_size("b")
    whole, top, low = slice(None), slice(0, split), slice(split, None)

    def side(i, extra, part):
        if not extra or way != "both":
            term = make(i, whole, extra)
        else:
            halves = [make(i, rows, extra if rows == part else []) for rows in (top, low)]
            term = jnp.concatenate(halves, axis=0)
        return after(term, *deps) if deps else term

    went, arrived = [], []
    for da in range(1, size_a):
        extra = [piece for (at, _), piece in came[0].items() if at == da]
        went.append(side(da * size_b, extra, top))
        arrived.append(shift(went[-1], "a", -da))
    for db in range(1, size_b):
        extra = [piece for (_, at), piece in came[1].items() if at == db]
        went.append(side(db, extra, low))
        arrived.append(shift(went[-1], "b", -db))
    return arrived, went


def send_line(term):
    size = lax.axis_size("ctx")
    rows = term.shape[0] // size
    return [term[:rows]] + [
        shift(term[k * rows : (k + 1) * rows], "ctx", -k) for k in range(1, size)
    ]


def add_line(pieces, last=()):
    total = after(pieces[0], *last).astype(jnp.float32)
    for piece in pieces[1:]:
        total = total + piece.astype(jnp.float32)
    return total


def pick_kernel(slab_ref, piece_ref, source_ref, mine_ref, theirs_ref, *, block):
    for k in range(mine_ref.shape[1] // block):
        to = slice(k * block, (k + 1) * block)
        start = pl.multiple_of(piece_ref[0, k] * block, block)
        mine_ref[:, to] = source_ref[:, pl.ds(start, block)]
        start = pl.multiple_of(piece_ref[1, k] * block, block)
        theirs_ref[:, to] = source_ref[:, pl.ds(start, block)]


def slab_terms(grads, slabs, i):
    cuts = {0}
    for part in slabs:
        at = 0
        for piece in part[i]:
            at += piece.shape[0]
            cuts.add(at)
    cuts = sorted(cuts)
    for low, high in zip(cuts[:-1], cuts[1:]):
        total = None
        for grad, part in zip(grads, slabs):
            at = 0
            for piece in part[i]:
                if at <= low and high <= at + piece.shape[0]:
                    term = dot(grad, piece[low - at : high - at, :], 1, 1)
                    total = term if total is None else total + term
                at += piece.shape[0]
        yield low, total


def nest(refs, shape):
    refs = iter(refs)
    return [[[next(refs) for _ in range(count)] for count in part] for part in shape]


def grad_kernel(*refs, shape, plane):
    parts = len(shape)
    grads = [ref[...] for ref in refs[:parts]]
    slabs = nest(refs[parts:-1], shape)
    for i in range(len(shape[0])):
        for low, total in slab_terms(grads, slabs, i):
            start = i * plane + low
            refs[-1][:, start : start + total.shape[1]] = total.astype(jnp.bfloat16)


def grad_place_kernel(*refs, shape, plane, block):
    slab_ref, piece_ref, *refs = refs
    parts = len(shape)
    grads = [ref[...] for ref in refs[:parts]]
    slabs = nest(refs[parts:-2], shape)
    theirs_ref, target_ref = refs[-2:]
    for i in range(len(shape[0])):
        base = slab_ref[i] * (2 * plane)
        for k in range(plane // block):
            start = pl.multiple_of(base + piece_ref[1, k] * block, block)
            at = i * plane + k * block
            target_ref[:, pl.ds(start, block)] = theirs_ref[:, at : at + block]
        for low, total in slab_terms(grads, slabs, i):
            total = total.astype(jnp.bfloat16)
            for j in range(total.shape[1] // block):
                k = low // block + j
                start = pl.multiple_of(base + piece_ref[0, k] * block, block)
                target_ref[:, pl.ds(start, block)] = total[:, j * block : (j + 1) * block]


VMEM = pl.BlockSpec(memory_space=pltpu.VMEM)


def pieces_of(slabs, pieces, block):
    at = slabs[None, :, None] * pieces.size + pieces[:, None, :]
    return at[..., None] * block + jnp.arange(block)


def pick_columns(source, slabs, pieces, block):
    rows, width = source.shape
    count, depth = slabs.shape[0], pieces.shape[1]
    half = depth * block
    if block % 128:
        at = pieces_of(slabs, pieces, block).reshape(2, -1)
        return source[:, at[0]], source[:, at[1]]
    part = jax.ShapeDtypeStruct((rows, width // 2), source.dtype)
    return pl.pallas_call(
        functools.partial(pick_kernel, block=block),
        grid_spec=pltpu.PrefetchScalarGridSpec(
            num_scalar_prefetch=2,
            grid=(count,),
            in_specs=[pl.BlockSpec((rows, 2 * half), lambda i, slab, piece: (0, slab[i]))],
            out_specs=[pl.BlockSpec((rows, half), lambda i, slab, piece: (0, i))] * 2,
        ),
        out_shape=[part, part],
        cost_estimate=pl.CostEstimate(
            flops=0, bytes_accessed=4 * rows * width, transcendentals=0
        ),
        name="pick_columns",
    )(slabs, pieces, source)


def grad_columns(grads, slabs):
    rows = grads[0].shape[0]
    shape = [[len(slab) for slab in part] for part in slabs]
    flat = [piece for part in slabs for slab in part for piece in slab]
    plane = sum(piece.shape[0] for piece in slabs[0][0])
    width = plane * len(shape[0])
    return pl.pallas_call(
        functools.partial(grad_kernel, shape=shape, plane=plane),
        in_specs=[VMEM] * (len(grads) + len(flat)),
        out_specs=VMEM,
        out_shape=jax.ShapeDtypeStruct((rows, width), jnp.bfloat16),
        compiler_params=pltpu.CompilerParams(vmem_limit_bytes=20 * 1024 * 1024),
        cost_estimate=pl.CostEstimate(
            flops=2 * rows * sum(piece.size for piece in flat),
            bytes_accessed=2 * sum(piece.size for piece in flat) + 2 * rows * width,
            transcendentals=0,
        ),
        name="grad_columns",
    )(*grads, *flat)


def grad_place(grads, slabs, theirs, places, pieces, block):
    rows, width = theirs.shape[0], 2 * theirs.shape[1]
    shape = [[len(slab) for slab in part] for part in slabs]
    flat = [piece for part in slabs for slab in part for piece in slab]
    plane = sum(piece.shape[0] for piece in slabs[0][0])
    if block % 128:
        at = pieces_of(places, pieces, block).reshape(2, -1)
        target = jnp.zeros((rows, width), theirs.dtype)
        return target.at[:, at[0]].set(grad_columns(grads, slabs)).at[:, at[1]].set(theirs)
    return pl.pallas_call(
        functools.partial(grad_place_kernel, shape=shape, plane=plane, block=block),
        grid_spec=pltpu.PrefetchScalarGridSpec(
            num_scalar_prefetch=2,
            grid=(),
            in_specs=[VMEM] * (len(grads) + len(flat) + 1),
            out_specs=VMEM,
        ),
        out_shape=jax.ShapeDtypeStruct((rows, width), jnp.bfloat16),
        compiler_params=pltpu.CompilerParams(vmem_limit_bytes=20 * 1024 * 1024),
        cost_estimate=pl.CostEstimate(
            flops=2 * rows * sum(piece.size for piece in flat),
            bytes_accessed=2 * sum(piece.size for piece in flat) + 3 * rows * width,
            transcendentals=0,
        ),
        name="grad_place",
    )(places, pieces, *grads, *flat, theirs)


def dot(a, b, left, right):
    return lax.dot_general(
        a, b, (((left,), (right,)), ((), ())), preferred_element_type=jnp.float32
    )


def project_kernel(*refs, counts, more):
    count = 2 * len(counts)
    sources, refs = refs[:count], refs[count:]
    pieces, (own_ref, other_ref) = refs[: sum(counts)], refs[-2:]
    for half, target in ((1, other_ref), (0, own_ref)):
        total = refs[sum(counts) + half][...] if more else None
        left = iter(pieces)
        for i, number in enumerate(counts):
            source, at = sources[2 * i + half], 0
            for _ in range(number):
                piece = next(left)
                end = at + piece.shape[0]
                term = dot(source[:, at:end], piece[...], 1, 0)
                total = term if total is None else total + term
                at = end
        target[...] = total


def project_rows(mine, theirs, slabs, before=()):
    rows = mine.shape[0]
    flat = [piece for slab in slabs.values() for piece in slab]
    columns = flat[0].shape[1]
    operands, in_specs = [], []
    for i, slab in slabs.items():
        plane = sum(piece.shape[0] for piece in slab)
        operands += [mine, theirs]
        in_specs += [pl.BlockSpec((rows, plane), lambda _, i=i: (0, i))] * 2
    whole = [*flat, *before]
    in_specs += [pl.BlockSpec(array.shape, lambda _: (0, 0)) for array in whole]
    area = sum(piece.size for piece in flat)
    return pl.pallas_call(
        functools.partial(
            project_kernel, counts=[len(slab) for slab in slabs.values()], more=bool(before)
        ),
        grid=(1,),
        in_specs=in_specs,
        out_specs=[pl.BlockSpec((rows, columns), lambda _: (0, 0))] * 2,
        out_shape=[jax.ShapeDtypeStruct((rows, columns), jnp.float32)] * 2,
        compiler_params=pltpu.CompilerParams(vmem_limit_bytes=24 * 1024 * 1024),
        cost_estimate=pl.CostEstimate(
            flops=4 * rows * area,
            bytes_accessed=2 * area + 4 * rows * area // columns,
            transcendentals=0,
        ),
        name="project_rows",
    )(*operands, *whole)


def attend_kernel(*refs, group, parts, head_dim, scale, last):
    q_own, q_other, grads, cos_ref, sin_ref, row_pos, key_pos = refs[:7]
    pieces = refs[7 : 7 + parts]
    rest = refs[7 + parts :]
    if last:
        before, rest = rest[0], rest[1:]
    attention_ref, grad_ref = rest[:2]
    terms = rest[2:-1]
    held = rest[-1]
    rows = q_own.shape[0]
    for j in range(parts):
        held[j * rows : (j + 1) * rows, :] = pieces[j][...]
    keys, values = held[:, :head_dim], held[:, head_dim:]
    cos, sin = cos_ref[...], sin_ref[...]
    allowed = key_pos[...] <= row_pos[...]
    key_term = value_term = None
    for h in range(group):
        at = slice(h * head_dim, (h + 1) * head_dim)
        q = q_own[:, at] + q_other[:, at]
        q = (q * cos + pltpu.roll(q, head_dim // 2, 1) * sin).astype(jnp.bfloat16)
        scores = jnp.where(allowed, dot(q, keys, 1, 1) * scale, MASKED)
        weight = jnp.exp(scores - jnp.max(scores, axis=1, keepdims=True))
        inverse = 1.0 / jnp.sum(weight, axis=1, keepdims=True)
        attention = (dot(weight.astype(jnp.bfloat16), values, 1, 0) * inverse).astype(jnp.bfloat16)
        attention_ref[:, at] = attention
        grad = grads[:, at]
        delta = jnp.sum(
            grad.astype(jnp.float32) * attention.astype(jnp.float32), axis=1, keepdims=True
        )
        probs = weight * inverse
        dscore = (probs * (dot(grad, values, 1, 1) - delta)).astype(jnp.bfloat16)
        grad_q = dot(dscore, keys, 1, 0) * scale
        grad_q = grad_q * cos - pltpu.roll(grad_q, head_dim // 2, 1) * sin
        grad_ref[:, at] = grad_q.astype(jnp.bfloat16)
        key_new = dot(dscore, q, 0, 0) * scale
        value_new = dot(probs.astype(jnp.bfloat16), grad, 0, 0)
        key_term = key_new if h == 0 else key_term + key_new
        value_term = value_new if h == 0 else value_term + value_new
    if last:
        key_term = key_term + before[:, :head_dim]
        value_term = value_term + before[:, head_dim:]
        for j in range(parts):
            span = slice(j * rows, (j + 1) * rows)
            terms[j][:, :head_dim] = key_term[span].astype(terms[j].dtype)
            terms[j][:, head_dim:] = value_term[span].astype(terms[j].dtype)
    else:
        terms[0][:, :head_dim] = key_term
        terms[0][:, head_dim:] = value_term


def attend(q_own, q_other, grads, cos, sin, row_pos, key_pos, pieces, before, scale):
    rows, columns = q_own.shape
    head_dim = cos.shape[1]
    parts = len(pieces)
    last = before is not None
    keys = parts * rows
    group = columns // head_dim
    if last:
        terms = [jax.ShapeDtypeStruct((rows, 2 * head_dim), jnp.float32)]
        terms += [jax.ShapeDtypeStruct((rows, 2 * head_dim), jnp.bfloat16)] * (parts - 1)
    else:
        terms = [jax.ShapeDtypeStruct((keys, 2 * head_dim), jnp.float32)]
    out_shape = [jax.ShapeDtypeStruct((rows, columns), jnp.bfloat16)] * 2 + terms
    operands = [q_own, q_other, grads, cos, sin, row_pos, key_pos, *pieces]
    operands += [before] if last else []
    out = pl.pallas_call(
        functools.partial(
            attend_kernel, group=group, parts=parts, head_dim=head_dim, scale=scale, last=last
        ),
        in_specs=[VMEM] * len(operands),
        out_specs=[VMEM] * len(out_shape),
        out_shape=out_shape,
        scratch_shapes=[pltpu.VMEM((keys, 2 * head_dim), jnp.bfloat16)],
        compiler_params=pltpu.CompilerParams(vmem_limit_bytes=20 * 1024 * 1024),
        cost_estimate=pl.CostEstimate(
            flops=14 * rows * keys * columns,
            bytes_accessed=8 * keys * 2 * head_dim,
            transcendentals=rows * keys * group,
        ),
        name="attend",
    )(*operands)
    return out[0], out[1], out[2:]


def finish_kernel(own, other, cos_ref, sin_ref, out):
    head_dim = cos_ref.shape[1]
    total = own[...] + other[...]
    key = total[:, :head_dim]
    key = key * cos_ref[...] + pltpu.roll(key, head_dim // 2, 1) * sin_ref[...]
    out[:, :head_dim] = key.astype(jnp.bfloat16)
    out[:, head_dim:] = total[:, head_dim:].astype(jnp.bfloat16)


def finish_keys(own, other, cos, sin):
    return pl.pallas_call(
        finish_kernel,
        in_specs=[VMEM] * 4,
        out_specs=VMEM,
        out_shape=jax.ShapeDtypeStruct(own.shape, jnp.bfloat16),
        name="finish_keys",
    )(own, other, cos, sin)


def undo_kernel(*refs):
    pieces, (cos_ref, sin_ref, out) = refs[:-3], refs[-3:]
    head_dim = cos_ref.shape[1]
    total = pieces[0][...]
    for piece in pieces[1:]:
        total = total + piece[...].astype(jnp.float32)
    key = total[:, :head_dim]
    key = key * cos_ref[...] - pltpu.roll(key, head_dim // 2, 1) * sin_ref[...]
    out[:, :head_dim] = key.astype(jnp.bfloat16)
    out[:, head_dim:] = total[:, head_dim:].astype(jnp.bfloat16)


def undo_keys(pieces, cos, sin):
    return pl.pallas_call(
        undo_kernel,
        in_specs=[VMEM] * (len(pieces) + 2),
        out_specs=VMEM,
        out_shape=jax.ShapeDtypeStruct(pieces[0].shape, jnp.bfloat16),
        name="undo_keys",
    )(*pieces, cos, sin)


def body(tokens, positions, query_weight, key_weight, value_weight, grad_output):
    token_rows = tokens[0]
    rows, width = token_rows.shape
    head_dim = key_weight.shape[1]
    query_width = query_weight.shape[1]
    heads = query_width // head_dim
    group = heads // 2
    scale = head_dim ** (-0.5)
    size_a, size_b, ctx = lax.axis_size("a"), lax.axis_size("b"), lax.axis_size("ctx")
    at_a, at_b = lax.axis_index("a"), lax.axis_index("b")
    core, place = lax.axis_index("core"), lax.axis_index("ctx")
    block = query_weight.shape[0]
    plane = ctx * block

    kv_local = jnp.concatenate([key_weight, value_weight], axis=1).astype(jnp.bfloat16)
    da, db = jnp.meshgrid(jnp.arange(size_a), jnp.arange(size_b), indexing="ij")
    slabs = ((at_a + size_a - da) % size_a) * size_b + (at_b + size_b - db) % size_b
    slabs = slabs.reshape(-1).astype(jnp.int32)
    line = (place + ctx - jnp.arange(ctx)) % ctx
    pieces = jnp.stack([core * ctx + line, (1 - core) * ctx + line]).astype(jnp.int32)
    mine, theirs = pick_columns(token_rows, slabs, pieces, block)
    half = query_width // 2
    q_local = [query_weight[:, g * half : (g + 1) * half].astype(jnp.bfloat16) for g in range(2)]
    pieces_kv = gather_line(kv_local)
    kv_line = jnp.concatenate([after(pieces_kv[0], mine), *pieces_kv[1:]], axis=0)
    theirs = swap(after(theirs, kv_line))

    q_local = [after(local, theirs) for local in q_local]
    q_line = [jnp.concatenate(gather_line(local), axis=0) for local in q_local]
    positions = after(positions, kv_line)
    own_positions = lax.dynamic_slice_in_dim(positions, place * rows, rows)
    cos_table, sin_table = rope_tables(own_positions, head_dim)
    sin_table = jnp.where(jnp.arange(head_dim) < head_dim // 2, -sin_table, sin_table)
    kv_sides = along(kv_line, "a"), along(kv_line, "b")
    stage = kv_sides[0] + kv_sides[1] + q_line[:1] + [cos_table, sin_table]
    kv_corners = gather_corners(*kv_sides, "b", *stage)
    q0_a = along(after(q_line[0], *stage), "a")
    stage = q0_a + [piece for corner in kv_corners.values() for piece in corner]
    q1_a = along(after(q_line[1], *stage), "a")
    q0_b = along(after(q_line[0], *stage), "b")
    kv_slabs = in_order(kv_line, *kv_sides, kv_corners)

    key_positions = jnp.concatenate(
        [
            lax.dynamic_slice_in_dim(positions, ((place + ctx - k) % ctx) * rows, rows)
            for k in range(ctx)
        ]
    )

    def project(slabs, early_part):
        late = {i: slab for i, slab in enumerate(slabs) if (i // size_b) * (i % size_b) > 0}
        own, other = project_rows(mine, theirs, late, early_part)
        return own, swap(other)

    def project_early(slabs, *deps):
        early = {i: slab for i, slab in enumerate(slabs) if (i // size_b) * (i % size_b) == 0}
        early[0] = after_all(early[0], *deps) if deps else early[0]
        return project_rows(mine, theirs, early)

    columns = jnp.concatenate([after(mine, *q0_a), theirs], axis=0)

    def terms_of(own, other):
        both = jnp.concatenate([own, other], axis=0)

        def make(i, part, extra=()):
            start, stop, _ = part.indices(plane)
            at = slice(i * plane + start, i * plane + stop)
            term = mm(columns[:, at], both, ((0,), (0,)))
            for piece in extra:
                term = term + piece.astype(jnp.float32)
            return term.astype(jnp.bfloat16)

        return make

    own, other = project_rows(mine, theirs, dict(enumerate(kv_slabs)))
    key_value = finish_keys(own, swap(other), cos_table, sin_table)
    stage = q1_a + q0_b + [key_value]
    q0_corners = gather_corners(q0_a, q0_b, "a", *stage)
    q1_b = along(after(q_line[1], *stage), "b")
    part = project_early(in_order(q_line[0], q0_a, q0_b, q0_corners))
    key_values = gather_line(key_value)
    stage = q1_b + key_values + [piece for corner in q0_corners.values() for piece in corner]
    q1_corners = gather_corners(q1_a, q1_b, "both", *stage)
    q_slabs = [
        in_order(q_line[0], q0_a, q0_b, q0_corners),
        in_order(q_line[1], q1_a, q1_b, q1_corners),
    ]
    attentions, gradients, made, came = [], [], [], []
    mid = plane // 2
    term = None
    for g in range(2):
        span = slice(g * group * head_dim, (g + 1) * group * head_dim)
        if g == 1:
            part = project_early(q_slabs[1], term)
        own, other = project(q_slabs[g], part)
        if g == 1:
            own = after(own, *came[0][2])
        attention, grad_q, terms = attend(
            own,
            other,
            grad_output[0][:, span],
            cos_table,
            sin_table,
            own_positions[:, None],
            key_positions[None, :],
            key_values,
            term,
            scale,
        )
        term = terms[0]
        attentions.append(attention)
        grads = (grad_q, swap(grad_q))
        gradients.append(grads)
        made.append(terms_of(*grads))
        came.append(reduce_corners(made[g], "ba"[g], mid))
    summed = [terms[0]] + [shift(terms[k], "ctx", -k) for k in range(1, ctx)]
    first = [*came[0][0].values(), *came[0][1].values()]
    second = [*came[1][0].values(), *came[1][1].values()]
    sides0, went0 = reduce_sides(made[0], came[0], "b", mid, *first, *summed[1:-1])
    grad_kv = undo_keys(
        [after(summed[0], *first, *second, *went0), *summed[1:]], cos_table, sin_table
    )
    gradients.append((grad_kv, swap(grad_kv)))
    made.append(terms_of(*gradients[2]))
    came.append(reduce_corners(made[2], "both", mid))
    third = [*came[2][0].values(), *came[2][1].values()]
    sides1, went1 = reduce_sides(made[1], came[1], "a", mid, *sides0)
    line0 = after(made[0](0, slice(None), sides0), *went1)
    sent0 = send_line(line0)
    q_grads = [add_line(sent0, sides1)]
    line1 = made[1](0, slice(None), sides1)
    kv_sides, _ = reduce_sides(made[2], came[2], "both", mid, *sides1, *sent0[1:-1])
    q_grads.append(add_line(send_line(line1), kv_sides))

    weights = [*q_slabs, kv_slabs]
    grad_theirs = grad_columns(
        [gradients[0][1], gradients[1][1], after(gradients[2][1], *third)], weights
    )
    grad_theirs = swap(grad_theirs)
    grad_input = grad_place(
        [gradients[0][0], gradients[1][0], gradients[2][0]], weights, grad_theirs, slabs, pieces, block
    )
    kv_term = after(made[2](0, slice(None), kv_sides), *q_grads)
    kv_wgrad = add_line(send_line(kv_term), (grad_input,))

    query_grad = jnp.concatenate(q_grads, axis=1)
    key_grad = kv_wgrad[:, :head_dim]
    value_grad = kv_wgrad[:, head_dim:]
    attention_rows = jnp.concatenate(attentions, axis=1)
    return (attention_rows[None], grad_input[None], query_grad, key_grad, value_grad)


def solution(mesh):
    dp, ctx = mesh.devices.shape
    fine = Mesh(mesh.devices.reshape(dp // 4, 2, 2, ctx), ("a", "b", "core", "ctx"))
    batch = P(("a", "b", "core"), "ctx", None)
    master = P(("a", "b", "core", "ctx"), None)
    in_specs = (batch, P(), master, master, master, batch)
    out_specs = (batch, batch, master, master, master)
    return jax.shard_map(body, mesh=fine, in_specs=in_specs, out_specs=out_specs, check_vma=False)
```

```python
import functools

import jax
import jax.numpy as jnp
from jax import lax
from jax.experimental import pallas as pl
from jax.experimental.pallas import tpu as pltpu
from jax.sharding import Mesh, PartitionSpec as P

ROPE_BASE = 1000000.0
MASKED = -1e30


def rope_tables(positions_in, head_dim):
    half_width = head_dim // 2
    exponent = jnp.arange(half_width).astype(jnp.float32) * (2.0 / head_dim)
    frequency = jnp.power(ROPE_BASE, -exponent)
    angles = positions_in.astype(jnp.float32)[:, None] * frequency[None, :]
    angles = jnp.concatenate([angles, angles], axis=1)
    return (jnp.cos(angles), jnp.sin(angles))


def mm(a, b, dims):
    return lax.dot_general(a, b, (dims, ((), ())), preferred_element_type=jnp.float32)


def shift(block, axis, step):
    size = lax.axis_size(axis)
    return lax.ppermute(block, axis, [(i, (i + step) % size) for i in range(size)])


def after(block, *others):
    return lax.optimization_barrier((block, *others))[0]


def after_all(blocks, *others):
    return [after(block, *others) for block in blocks]


def swap(block):
    return shift(block, "core", 1)


def gather_line(block):
    return [block] + [shift(block, "ctx", k) for k in range(1, lax.axis_size("ctx"))]


def along(block, axis):
    return [shift(block, axis, step) for step in range(1, lax.axis_size(axis))]


def gather_corners(sides_a, sides_b, way, *deps):
    corners = {}
    for da, side_a in enumerate(sides_a, 1):
        for db, side_b in enumerate(sides_b, 1):
            mid = side_a.shape[0] // 2
            if way == "b":
                corners[da, db] = [shift(after(side_a, *deps), "b", db)]
            elif way == "a":
                corners[da, db] = [shift(after(side_b, *deps), "a", da)]
            else:
                corners[da, db] = [
                    shift(after(side_a[:mid], *deps), "b", db),
                    shift(after(side_b[mid:], *deps), "a", da),
                ]
    return corners


def in_order(block, sides_a, sides_b, corners):
    slabs = [[block]] + [[side] for side in sides_b]
    for da, side in enumerate(sides_a, 1):
        slabs.append([side])
        slabs += [corners[da, db] for db in range(1, len(sides_b) + 1)]
    return slabs


def reduce_corners(make, way, split):
    size_b = lax.axis_size("b")
    whole, top, low = slice(None), slice(0, split), slice(split, None)
    came_a, came_b, went = {}, {}, []
    for da in range(1, lax.axis_size("a")):
        for db in range(1, size_b):
            i = da * size_b + db
            went += [make(i, rows) for rows in ((top, low) if way == "both" else (whole,))]
            if way != "a":
                came_a[da, db] = shift(went[-2 if way == "both" else -1], "b", -db)
            if way != "b":
                came_b[da, db] = shift(went[-1], "a", -da)
    return came_a, came_b, went


def reduce_sides(make, came, way, split, *deps):
    size_a, size_b = lax.axis_size("a"), lax.axis_size("b")
    whole, top, low = slice(None), slice(0, split), slice(split, None)

    def side(i, extra, part):
        if not extra or way != "both":
            term = make(i, whole, extra)
        else:
            halves = [make(i, rows, extra if rows == part else []) for rows in (top, low)]
            term = jnp.concatenate(halves, axis=0)
        return after(term, *deps) if deps else term

    went, arrived = [], []
    for da in range(1, size_a):
        extra = [piece for (at, _), piece in came[0].items() if at == da]
        went.append(side(da * size_b, extra, top))
        arrived.append(shift(went[-1], "a", -da))
    for db in range(1, size_b):
        extra = [piece for (_, at), piece in came[1].items() if at == db]
        went.append(side(db, extra, low))
        arrived.append(shift(went[-1], "b", -db))
    return arrived, went


def send_line(term):
    size = lax.axis_size("ctx")
    rows = term.shape[0] // size
    return [term[:rows]] + [
        shift(term[k * rows : (k + 1) * rows], "ctx", -k) for k in range(1, size)
    ]


def add_line(pieces, last=()):
    total = after(pieces[0], *last).astype(jnp.float32)
    for piece in pieces[1:]:
        total = total + piece.astype(jnp.float32)
    return total


def pick_kernel(slab_ref, piece_ref, source_ref, mine_ref, theirs_ref, *, block):
    for k in range(mine_ref.shape[1] // block):
        to = slice(k * block, (k + 1) * block)
        start = pl.multiple_of(piece_ref[0, k] * block, block)
        mine_ref[:, to] = source_ref[:, pl.ds(start, block)]
        start = pl.multiple_of(piece_ref[1, k] * block, block)
        theirs_ref[:, to] = source_ref[:, pl.ds(start, block)]


def slab_terms(grads, slabs, i):
    cuts = {0}
    for part in slabs:
        at = 0
        for piece in part[i]:
            at += piece.shape[0]
            cuts.add(at)
    cuts = sorted(cuts)
    for low, high in zip(cuts[:-1], cuts[1:]):
        total = None
        for grad, part in zip(grads, slabs):
            at = 0
            for piece in part[i]:
                if at <= low and high <= at + piece.shape[0]:
                    term = dot(grad, piece[low - at : high - at, :], 1, 1)
                    total = term if total is None else total + term
                at += piece.shape[0]
        yield low, total


def nest(refs, shape):
    refs = iter(refs)
    return [[[next(refs) for _ in range(count)] for count in part] for part in shape]


def grad_kernel(*refs, shape, plane):
    parts = len(shape)
    grads = [ref[...] for ref in refs[:parts]]
    slabs = nest(refs[parts:-1], shape)
    for i in range(len(shape[0])):
        for low, total in slab_terms(grads, slabs, i):
            start = i * plane + low
            refs[-1][:, start : start + total.shape[1]] = total.astype(jnp.bfloat16)


def grad_place_kernel(*refs, shape, plane, block):
    slab_ref, piece_ref, *refs = refs
    parts = len(shape)
    grads = [ref[...] for ref in refs[:parts]]
    slabs = nest(refs[parts:-2], shape)
    theirs_ref, target_ref = refs[-2:]
    for i in range(len(shape[0])):
        base = slab_ref[i] * (2 * plane)
        for k in range(plane // block):
            start = pl.multiple_of(base + piece_ref[1, k] * block, block)
            at = i * plane + k * block
            target_ref[:, pl.ds(start, block)] = theirs_ref[:, at : at + block]
        for low, total in slab_terms(grads, slabs, i):
            total = total.astype(jnp.bfloat16)
            for j in range(total.shape[1] // block):
                k = low // block + j
                start = pl.multiple_of(base + piece_ref[0, k] * block, block)
                target_ref[:, pl.ds(start, block)] = total[:, j * block : (j + 1) * block]


VMEM = pl.BlockSpec(memory_space=pltpu.VMEM)


def pieces_of(slabs, pieces, block):
    at = slabs[None, :, None] * pieces.size + pieces[:, None, :]
    return at[..., None] * block + jnp.arange(block)


def pick_columns(source, slabs, pieces, block):
    rows, width = source.shape
    count, depth = slabs.shape[0], pieces.shape[1]
    half = depth * block
    if block % 128:
        at = pieces_of(slabs, pieces, block).reshape(2, -1)
        return source[:, at[0]], source[:, at[1]]
    part = jax.ShapeDtypeStruct((rows, width // 2), source.dtype)
    return pl.pallas_call(
        functools.partial(pick_kernel, block=block),
        grid_spec=pltpu.PrefetchScalarGridSpec(
            num_scalar_prefetch=2,
            grid=(count,),
            in_specs=[pl.BlockSpec((rows, 2 * half), lambda i, slab, piece: (0, slab[i]))],
            out_specs=[pl.BlockSpec((rows, half), lambda i, slab, piece: (0, i))] * 2,
        ),
        out_shape=[part, part],
        cost_estimate=pl.CostEstimate(
            flops=0, bytes_accessed=4 * rows * width, transcendentals=0
        ),
        name="pick_columns",
    )(slabs, pieces, source)


def grad_columns(grads, slabs):
    rows = grads[0].shape[0]
    shape = [[len(slab) for slab in part] for part in slabs]
    flat = [piece for part in slabs for slab in part for piece in slab]
    plane = sum(piece.shape[0] for piece in slabs[0][0])
    width = plane * len(shape[0])
    return pl.pallas_call(
        functools.partial(grad_kernel, shape=shape, plane=plane),
        in_specs=[VMEM] * (len(grads) + len(flat)),
        out_specs=VMEM,
        out_shape=jax.ShapeDtypeStruct((rows, width), jnp.bfloat16),
        compiler_params=pltpu.CompilerParams(vmem_limit_bytes=20 * 1024 * 1024),
        cost_estimate=pl.CostEstimate(
            flops=2 * rows * sum(piece.size for piece in flat),
            bytes_accessed=2 * sum(piece.size for piece in flat) + 2 * rows * width,
            transcendentals=0,
        ),
        name="grad_columns",
    )(*grads, *flat)


def grad_place(grads, slabs, theirs, places, pieces, block):
    rows, width = theirs.shape[0], 2 * theirs.shape[1]
    shape = [[len(slab) for slab in part] for part in slabs]
    flat = [piece for part in slabs for slab in part for piece in slab]
    plane = sum(piece.shape[0] for piece in slabs[0][0])
    if block % 128:
        at = pieces_of(places, pieces, block).reshape(2, -1)
        target = jnp.zeros((rows, width), theirs.dtype)
        return target.at[:, at[0]].set(grad_columns(grads, slabs)).at[:, at[1]].set(theirs)
    return pl.pallas_call(
        functools.partial(grad_place_kernel, shape=shape, plane=plane, block=block),
        grid_spec=pltpu.PrefetchScalarGridSpec(
            num_scalar_prefetch=2,
            grid=(),
            in_specs=[VMEM] * (len(grads) + len(flat) + 1),
            out_specs=VMEM,
        ),
        out_shape=jax.ShapeDtypeStruct((rows, width), jnp.bfloat16),
        compiler_params=pltpu.CompilerParams(vmem_limit_bytes=20 * 1024 * 1024),
        cost_estimate=pl.CostEstimate(
            flops=2 * rows * sum(piece.size for piece in flat),
            bytes_accessed=2 * sum(piece.size for piece in flat) + 3 * rows * width,
            transcendentals=0,
        ),
        name="grad_place",
    )(places, pieces, *grads, *flat, theirs)


def dot(a, b, left, right):
    return lax.dot_general(
        a, b, (((left,), (right,)), ((), ())), preferred_element_type=jnp.float32
    )


def project_kernel(*refs, counts, more):
    count = 2 * len(counts)
    sources, refs = refs[:count], refs[count:]
    pieces, (own_ref, other_ref) = refs[: sum(counts)], refs[-2:]
    for half, target in ((1, other_ref), (0, own_ref)):
        total = refs[sum(counts) + half][...] if more else None
        left = iter(pieces)
        for i, number in enumerate(counts):
            source, at = sources[2 * i + half], 0
            for _ in range(number):
                piece = next(left)
                end = at + piece.shape[0]
                term = dot(source[:, at:end], piece[...], 1, 0)
                total = term if total is None else total + term
                at = end
        target[...] = total


def project_rows(mine, theirs, slabs, before=()):
    rows = mine.shape[0]
    flat = [piece for slab in slabs.values() for piece in slab]
    columns = flat[0].shape[1]
    operands, in_specs = [], []
    for i, slab in slabs.items():
        plane = sum(piece.shape[0] for piece in slab)
        operands += [mine, theirs]
        in_specs += [pl.BlockSpec((rows, plane), lambda _, i=i: (0, i))] * 2
    whole = [*flat, *before]
    in_specs += [pl.BlockSpec(array.shape, lambda _: (0, 0)) for array in whole]
    area = sum(piece.size for piece in flat)
    return pl.pallas_call(
        functools.partial(
            project_kernel, counts=[len(slab) for slab in slabs.values()], more=bool(before)
        ),
        grid=(1,),
        in_specs=in_specs,
        out_specs=[pl.BlockSpec((rows, columns), lambda _: (0, 0))] * 2,
        out_shape=[jax.ShapeDtypeStruct((rows, columns), jnp.float32)] * 2,
        compiler_params=pltpu.CompilerParams(vmem_limit_bytes=24 * 1024 * 1024),
        cost_estimate=pl.CostEstimate(
            flops=4 * rows * area,
            bytes_accessed=2 * area + 4 * rows * area // columns,
            transcendentals=0,
        ),
        name="project_rows",
    )(*operands, *whole)


def attend_kernel(*refs, group, parts, head_dim, scale, last):
    q_own, q_other, grads, cos_ref, sin_ref, row_pos, key_pos = refs[:7]
    pieces = refs[7 : 7 + parts]
    rest = refs[7 + parts :]
    if last:
        before, rest = rest[0], rest[1:]
    attention_ref, grad_ref = rest[:2]
    terms = rest[2:-1]
    held = rest[-1]
    rows = q_own.shape[0]
    for j in range(parts):
        held[j * rows : (j + 1) * rows, :] = pieces[j][...]
    keys, values = held[:, :head_dim], held[:, head_dim:]
    cos, sin = cos_ref[...], sin_ref[...]
    allowed = key_pos[...] <= row_pos[...]
    key_term = value_term = None
    for h in range(group):
        at = slice(h * head_dim, (h + 1) * head_dim)
        q = q_own[:, at] + q_other[:, at]
        q = (q * cos + pltpu.roll(q, head_dim // 2, 1) * sin).astype(jnp.bfloat16)
        scores = jnp.where(allowed, dot(q, keys, 1, 1) * scale, MASKED)
        weight = jnp.exp(scores - jnp.max(scores, axis=1, keepdims=True))
        inverse = 1.0 / jnp.sum(weight, axis=1, keepdims=True)
        attention = (dot(weight.astype(jnp.bfloat16), values, 1, 0) * inverse).astype(jnp.bfloat16)
        attention_ref[:, at] = attention
        grad = grads[:, at]
        delta = jnp.sum(
            grad.astype(jnp.float32) * attention.astype(jnp.float32), axis=1, keepdims=True
        )
        probs = weight * inverse
        dscore = (probs * (dot(grad, values, 1, 1) - delta)).astype(jnp.bfloat16)
        grad_q = dot(dscore, keys, 1, 0) * scale
        grad_q = grad_q * cos - pltpu.roll(grad_q, head_dim // 2, 1) * sin
        grad_ref[:, at] = grad_q.astype(jnp.bfloat16)
        key_new = dot(dscore, q, 0, 0) * scale
        value_new = dot(probs.astype(jnp.bfloat16), grad, 0, 0)
        key_term = key_new if h == 0 else key_term + key_new
        value_term = value_new if h == 0 else value_term + value_new
    if last:
        key_term = key_term + before[:, :head_dim]
        value_term = value_term + before[:, head_dim:]
        for j in range(parts):
            span = slice(j * rows, (j + 1) * rows)
            terms[j][:, :head_dim] = key_term[span].astype(terms[j].dtype)
            terms[j][:, head_dim:] = value_term[span].astype(terms[j].dtype)
    else:
        terms[0][:, :head_dim] = key_term
        terms[0][:, head_dim:] = value_term


def attend(q_own, q_other, grads, cos, sin, row_pos, key_pos, pieces, before, scale):
    rows, columns = q_own.shape
    head_dim = cos.shape[1]
    parts = len(pieces)
    last = before is not None
    keys = parts * rows
    group = columns // head_dim
    if last:
        terms = [jax.ShapeDtypeStruct((rows, 2 * head_dim), jnp.float32)]
        terms += [jax.ShapeDtypeStruct((rows, 2 * head_dim), jnp.bfloat16)] * (parts - 1)
    else:
        terms = [jax.ShapeDtypeStruct((keys, 2 * head_dim), jnp.float32)]
    out_shape = [jax.ShapeDtypeStruct((rows, columns), jnp.bfloat16)] * 2 + terms
    operands = [q_own, q_other, grads, cos, sin, row_pos, key_pos, *pieces]
    operands += [before] if last else []
    out = pl.pallas_call(
        functools.partial(
            attend_kernel, group=group, parts=parts, head_dim=head_dim, scale=scale, last=last
        ),
        in_specs=[VMEM] * len(operands),
        out_specs=[VMEM] * len(out_shape),
        out_shape=out_shape,
        scratch_shapes=[pltpu.VMEM((keys, 2 * head_dim), jnp.bfloat16)],
        compiler_params=pltpu.CompilerParams(vmem_limit_bytes=20 * 1024 * 1024),
        cost_estimate=pl.CostEstimate(
            flops=14 * rows * keys * columns,
            bytes_accessed=8 * keys * 2 * head_dim,
            transcendentals=rows * keys * group,
        ),
        name="attend",
    )(*operands)
    return out[0], out[1], out[2:]


def finish_kernel(own, other, cos_ref, sin_ref, out):
    head_dim = cos_ref.shape[1]
    total = own[...] + other[...]
    key = total[:, :head_dim]
    key = key * cos_ref[...] + pltpu.roll(key, head_dim // 2, 1) * sin_ref[...]
    out[:, :head_dim] = key.astype(jnp.bfloat16)
    out[:, head_dim:] = total[:, head_dim:].astype(jnp.bfloat16)


def finish_keys(own, other, cos, sin):
    return pl.pallas_call(
        finish_kernel,
        in_specs=[VMEM] * 4,
        out_specs=VMEM,
        out_shape=jax.ShapeDtypeStruct(own.shape, jnp.bfloat16),
        name="finish_keys",
    )(own, other, cos, sin)


def undo_kernel(*refs):
    pieces, (cos_ref, sin_ref, out) = refs[:-3], refs[-3:]
    head_dim = cos_ref.shape[1]
    total = pieces[0][...]
    for piece in pieces[1:]:
        total = total + piece[...].astype(jnp.float32)
    key = total[:, :head_dim]
    key = key * cos_ref[...] - pltpu.roll(key, head_dim // 2, 1) * sin_ref[...]
    out[:, :head_dim] = key.astype(jnp.bfloat16)
    out[:, head_dim:] = total[:, head_dim:].astype(jnp.bfloat16)


def undo_keys(pieces, cos, sin):
    return pl.pallas_call(
        undo_kernel,
        in_specs=[VMEM] * (len(pieces) + 2),
        out_specs=VMEM,
        out_shape=jax.ShapeDtypeStruct(pieces[0].shape, jnp.bfloat16),
        name="undo_keys",
    )(*pieces, cos, sin)


def body(tokens, positions, query_weight, key_weight, value_weight, grad_output):
    token_rows = tokens[0]
    rows, width = token_rows.shape
    head_dim = key_weight.shape[1]
    query_width = query_weight.shape[1]
    heads = query_width // head_dim
    group = heads // 2
    scale = head_dim ** (-0.5)
    size_a, size_b, ctx = lax.axis_size("a"), lax.axis_size("b"), lax.axis_size("ctx")
    at_a, at_b = lax.axis_index("a"), lax.axis_index("b")
    core, place = lax.axis_index("core"), lax.axis_index("ctx")
    block = query_weight.shape[0]
    plane = ctx * block

    kv_local = jnp.concatenate([key_weight, value_weight], axis=1).astype(jnp.bfloat16)
    da, db = jnp.meshgrid(jnp.arange(size_a), jnp.arange(size_b), indexing="ij")
    slabs = ((at_a + size_a - da) % size_a) * size_b + (at_b + size_b - db) % size_b
    slabs = slabs.reshape(-1).astype(jnp.int32)
    line = (place + ctx - jnp.arange(ctx)) % ctx
    pieces = jnp.stack([core * ctx + line, (1 - core) * ctx + line]).astype(jnp.int32)
    mine, theirs = pick_columns(token_rows, slabs, pieces, block)
    half = query_width // 2
    q_local = [query_weight[:, g * half : (g + 1) * half].astype(jnp.bfloat16) for g in range(2)]
    pieces_kv = gather_line(kv_local)
    kv_line = jnp.concatenate([after(pieces_kv[0], mine), *pieces_kv[1:]], axis=0)
    theirs = swap(after(theirs, kv_line))

    q_local = [after(local, theirs) for local in q_local]
    q_line = [jnp.concatenate(gather_line(local), axis=0) for local in q_local]
    positions = after(positions, kv_line)
    own_positions = lax.dynamic_slice_in_dim(positions, place * rows, rows)
    cos_table, sin_table = rope_tables(own_positions, head_dim)
    sin_table = jnp.where(jnp.arange(head_dim) < head_dim // 2, -sin_table, sin_table)
    kv_sides = along(kv_line, "a"), along(kv_line, "b")
    stage = kv_sides[0] + kv_sides[1] + q_line[:1] + [cos_table, sin_table]
    kv_corners = gather_corners(*kv_sides, "b", *stage)
    q0_a = along(after(q_line[0], *stage), "a")
    stage = q0_a + [piece for corner in kv_corners.values() for piece in corner]
    q1_a = along(after(q_line[1], *stage), "a")
    q0_b = along(after(q_line[0], *stage), "b")
    kv_slabs = in_order(kv_line, *kv_sides, kv_corners)

    key_positions = jnp.concatenate(
        [
            lax.dynamic_slice_in_dim(positions, ((place + ctx - k) % ctx) * rows, rows)
            for k in range(ctx)
        ]
    )

    def project(slabs, early_part):
        late = {i: slab for i, slab in enumerate(slabs) if (i // size_b) * (i % size_b) > 0}
        own, other = project_rows(mine, theirs, late, early_part)
        return own, swap(other)

    def project_early(slabs, *deps):
        early = {i: slab for i, slab in enumerate(slabs) if (i // size_b) * (i % size_b) == 0}
        early[0] = after_all(early[0], *deps) if deps else early[0]
        return project_rows(mine, theirs, early)

    columns = jnp.concatenate([after(mine, *q0_a), theirs], axis=0)

    def terms_of(own, other):
        both = jnp.concatenate([own, other], axis=0)

        def make(i, part, extra=()):
            start, stop, _ = part.indices(plane)
            at = slice(i * plane + start, i * plane + stop)
            term = mm(columns[:, at], both, ((0,), (0,)))
            for piece in extra:
                term = term + piece.astype(jnp.float32)
            return term.astype(jnp.bfloat16)

        return make

    own, other = project_rows(mine, theirs, dict(enumerate(kv_slabs)))
    key_value = finish_keys(own, swap(other), cos_table, sin_table)
    stage = q1_a + q0_b + [key_value]
    q0_corners = gather_corners(q0_a, q0_b, "a", *stage)
    q1_b = along(after(q_line[1], *stage), "b")
    part = project_early(in_order(q_line[0], q0_a, q0_b, q0_corners))
    key_values = gather_line(key_value)
    stage = q1_b + key_values + [piece for corner in q0_corners.values() for piece in corner]
    q1_corners = gather_corners(q1_a, q1_b, "both", *stage)
    q_slabs = [
        in_order(q_line[0], q0_a, q0_b, q0_corners),
        in_order(q_line[1], q1_a, q1_b, q1_corners),
    ]
    attentions, gradients, made, came = [], [], [], []
    mid = plane // 2
    term = None
    for g in range(2):
        span = slice(g * group * head_dim, (g + 1) * group * head_dim)
        if g == 1:
            part = project_early(q_slabs[1], term)
        own, other = project(q_slabs[g], part)
        if g == 1:
            own = after(own, *came[0][2])
        attention, grad_q, terms = attend(
            own,
            other,
            grad_output[0][:, span],
            cos_table,
            sin_table,
            own_positions[:, None],
            key_positions[None, :],
            key_values,
            term,
            scale,
        )
        term = terms[0]
        attentions.append(attention)
        grads = (grad_q, swap(grad_q))
        gradients.append(grads)
        made.append(terms_of(*grads))
        came.append(reduce_corners(made[g], "ba"[g], mid))
    summed = [terms[0]] + [shift(terms[k], "ctx", -k) for k in range(1, ctx)]
    first = [*came[0][0].values(), *came[0][1].values()]
    second = [*came[1][0].values(), *came[1][1].values()]
    sides0, went0 = reduce_sides(made[0], came[0], "b", mid, *first, *summed[1:2])
    grad_kv = undo_keys(
        [after(summed[0], *first, *second, *went0), *summed[1:]], cos_table, sin_table
    )
    gradients.append((grad_kv, swap(grad_kv)))
    made.append(terms_of(*gradients[2]))
    came.append(reduce_corners(made[2], "both", mid))
    third = [*came[2][0].values(), *came[2][1].values()]
    sides1, went1 = reduce_sides(made[1], came[1], "a", mid, *sides0)
    line0 = after(made[0](0, slice(None), sides0), *went1)
    sent0 = send_line(line0)
    q_grads = [add_line(sent0, sides1)]
    line1 = made[1](0, slice(None), sides1)
    kv_sides, _ = reduce_sides(made[2], came[2], "both", mid, *sides1, *sent0[1:-1])
    sent1 = send_line(line1)

    weights = [*q_slabs, kv_slabs]
    grad_theirs = grad_columns(
        [gradients[0][1], gradients[1][1], after(gradients[2][1], *third)], weights
    )
    grad_theirs = swap(grad_theirs)
    grad_input = grad_place(
        [gradients[0][0], gradients[1][0], gradients[2][0]], weights, grad_theirs, slabs, pieces, block
    )
    kv_term = after(made[2](0, slice(None), kv_sides), q_grads[0], *sent1[1:-1])
    q_grads.append(add_line(sent1, (grad_input,)))
    kv_wgrad = add_line(send_line(kv_term), (grad_input,))

    query_grad = jnp.concatenate(q_grads, axis=1)
    key_grad = kv_wgrad[:, :head_dim]
    value_grad = kv_wgrad[:, head_dim:]
    attention_rows = jnp.concatenate(attentions, axis=1)
    return (attention_rows[None], grad_input[None], query_grad, key_grad, value_grad)


def solution(mesh):
    dp, ctx = mesh.devices.shape
    fine = Mesh(mesh.devices.reshape(dp // 4, 2, 2, ctx), ("a", "b", "core", "ctx"))
    batch = P(("a", "b", "core"), "ctx", None)
    master = P(("a", "b", "core", "ctx"), None)
    in_specs = (batch, P(), master, master, master, batch)
    out_specs = (batch, batch, master, master, master)
    return jax.shard_map(body, mesh=fine, in_specs=in_specs, out_specs=out_specs, check_vma=False)
```

```python
import functools

import jax
import jax.numpy as jnp
from jax import lax
from jax.experimental import pallas as pl
from jax.experimental.pallas import tpu as pltpu
from jax.sharding import Mesh, PartitionSpec as P

ROPE_BASE = 1000000.0
MASKED = -1e30


def rope_tables(positions_in, head_dim):
    half_width = head_dim // 2
    exponent = jnp.arange(half_width).astype(jnp.float32) * (2.0 / head_dim)
    frequency = jnp.power(ROPE_BASE, -exponent)
    angles = positions_in.astype(jnp.float32)[:, None] * frequency[None, :]
    angles = jnp.concatenate([angles, angles], axis=1)
    return (jnp.cos(angles), jnp.sin(angles))


def mm(a, b, dims):
    return lax.dot_general(a, b, (dims, ((), ())), preferred_element_type=jnp.float32)


def shift(block, axis, step):
    size = lax.axis_size(axis)
    return lax.ppermute(block, axis, [(i, (i + step) % size) for i in range(size)])


def after(block, *others):
    return lax.optimization_barrier((block, *others))[0]


def after_all(blocks, *others):
    return [after(block, *others) for block in blocks]


def swap(block):
    return shift(block, "core", 1)


def gather_line(block):
    return [block] + [shift(block, "ctx", k) for k in range(1, lax.axis_size("ctx"))]


def along(block, axis):
    return [shift(block, axis, step) for step in range(1, lax.axis_size(axis))]


def gather_corners(sides_a, sides_b, way, *deps):
    corners = {}
    for da, side_a in enumerate(sides_a, 1):
        for db, side_b in enumerate(sides_b, 1):
            mid = side_a.shape[0] // 2
            if way == "b":
                corners[da, db] = [shift(after(side_a, *deps), "b", db)]
            elif way == "a":
                corners[da, db] = [shift(after(side_b, *deps), "a", da)]
            else:
                corners[da, db] = [
                    shift(after(side_a[:mid], *deps), "b", db),
                    shift(after(side_b[mid:], *deps), "a", da),
                ]
    return corners


def in_order(block, sides_a, sides_b, corners):
    slabs = [[block]] + [[side] for side in sides_b]
    for da, side in enumerate(sides_a, 1):
        slabs.append([side])
        slabs += [corners[da, db] for db in range(1, len(sides_b) + 1)]
    return slabs


def reduce_corners(make, way, split):
    size_b = lax.axis_size("b")
    whole, top, low = slice(None), slice(0, split), slice(split, None)
    came_a, came_b, went = {}, {}, []
    for da in range(1, lax.axis_size("a")):
        for db in range(1, size_b):
            i = da * size_b + db
            went += [make(i, rows) for rows in ((top, low) if way == "both" else (whole,))]
            if way != "a":
                came_a[da, db] = shift(went[-2 if way == "both" else -1], "b", -db)
            if way != "b":
                came_b[da, db] = shift(went[-1], "a", -da)
    return came_a, came_b, went


def reduce_sides(make, came, way, split, *deps):
    size_a, size_b = lax.axis_size("a"), lax.axis_size("b")
    whole, top, low = slice(None), slice(0, split), slice(split, None)

    def side(i, extra, part):
        if not extra or way != "both":
            term = make(i, whole, extra)
        else:
            halves = [make(i, rows, extra if rows == part else []) for rows in (top, low)]
            term = jnp.concatenate(halves, axis=0)
        return after(term, *deps) if deps else term

    went, arrived = [], []
    for da in range(1, size_a):
        extra = [piece for (at, _), piece in came[0].items() if at == da]
        went.append(side(da * size_b, extra, top))
        arrived.append(shift(went[-1], "a", -da))
    for db in range(1, size_b):
        extra = [piece for (_, at), piece in came[1].items() if at == db]
        went.append(side(db, extra, low))
        arrived.append(shift(went[-1], "b", -db))
    return arrived, went


def send_line(term):
    size = lax.axis_size("ctx")
    rows = term.shape[0] // size
    return [term[:rows]] + [
        shift(term[k * rows : (k + 1) * rows], "ctx", -k) for k in range(1, size)
    ]


def add_line(pieces, last=()):
    total = after(pieces[0], *last).astype(jnp.float32)
    for piece in pieces[1:]:
        total = total + piece.astype(jnp.float32)
    return total


def pick_kernel(slab_ref, piece_ref, source_ref, mine_ref, theirs_ref, *, block):
    for k in range(mine_ref.shape[1] // block):
        to = slice(k * block, (k + 1) * block)
        start = pl.multiple_of(piece_ref[0, k] * block, block)
        mine_ref[:, to] = source_ref[:, pl.ds(start, block)]
        start = pl.multiple_of(piece_ref[1, k] * block, block)
        theirs_ref[:, to] = source_ref[:, pl.ds(start, block)]


def slab_terms(grads, slabs, i):
    cuts = {0}
    for part in slabs:
        at = 0
        for piece in part[i]:
            at += piece.shape[0]
            cuts.add(at)
    cuts = sorted(cuts)
    for low, high in zip(cuts[:-1], cuts[1:]):
        total = None
        for grad, part in zip(grads, slabs):
            at = 0
            for piece in part[i]:
                if at <= low and high <= at + piece.shape[0]:
                    term = dot(grad, piece[low - at : high - at, :], 1, 1)
                    total = term if total is None else total + term
                at += piece.shape[0]
        yield low, total


def nest(refs, shape):
    refs = iter(refs)
    return [[[next(refs) for _ in range(count)] for count in part] for part in shape]


def grad_kernel(*refs, shape, plane):
    parts = len(shape)
    grads = [ref[...] for ref in refs[:parts]]
    slabs = nest(refs[parts:-1], shape)
    for i in range(len(shape[0])):
        for low, total in slab_terms(grads, slabs, i):
            start = i * plane + low
            refs[-1][:, start : start + total.shape[1]] = total.astype(jnp.bfloat16)


def grad_place_kernel(*refs, shape, plane, block):
    slab_ref, piece_ref, *refs = refs
    parts = len(shape)
    grads = [ref[...] for ref in refs[:parts]]
    slabs = nest(refs[parts:-2], shape)
    theirs_ref, target_ref = refs[-2:]
    for i in range(len(shape[0])):
        base = slab_ref[i] * (2 * plane)
        for k in range(plane // block):
            start = pl.multiple_of(base + piece_ref[1, k] * block, block)
            at = i * plane + k * block
            target_ref[:, pl.ds(start, block)] = theirs_ref[:, at : at + block]
        for low, total in slab_terms(grads, slabs, i):
            total = total.astype(jnp.bfloat16)
            for j in range(total.shape[1] // block):
                k = low // block + j
                start = pl.multiple_of(base + piece_ref[0, k] * block, block)
                target_ref[:, pl.ds(start, block)] = total[:, j * block : (j + 1) * block]


VMEM = pl.BlockSpec(memory_space=pltpu.VMEM)


def pieces_of(slabs, pieces, block):
    at = slabs[None, :, None] * pieces.size + pieces[:, None, :]
    return at[..., None] * block + jnp.arange(block)


def pick_columns(source, slabs, pieces, block):
    rows, width = source.shape
    count, depth = slabs.shape[0], pieces.shape[1]
    half = depth * block
    if block % 128:
        at = pieces_of(slabs, pieces, block).reshape(2, -1)
        return source[:, at[0]], source[:, at[1]]
    part = jax.ShapeDtypeStruct((rows, width // 2), source.dtype)
    return pl.pallas_call(
        functools.partial(pick_kernel, block=block),
        grid_spec=pltpu.PrefetchScalarGridSpec(
            num_scalar_prefetch=2,
            grid=(count,),
            in_specs=[pl.BlockSpec((rows, 2 * half), lambda i, slab, piece: (0, slab[i]))],
            out_specs=[pl.BlockSpec((rows, half), lambda i, slab, piece: (0, i))] * 2,
        ),
        out_shape=[part, part],
        cost_estimate=pl.CostEstimate(
            flops=0, bytes_accessed=4 * rows * width, transcendentals=0
        ),
        name="pick_columns",
    )(slabs, pieces, source)


def grad_columns(grads, slabs):
    rows = grads[0].shape[0]
    shape = [[len(slab) for slab in part] for part in slabs]
    flat = [piece for part in slabs for slab in part for piece in slab]
    plane = sum(piece.shape[0] for piece in slabs[0][0])
    width = plane * len(shape[0])
    return pl.pallas_call(
        functools.partial(grad_kernel, shape=shape, plane=plane),
        in_specs=[VMEM] * (len(grads) + len(flat)),
        out_specs=VMEM,
        out_shape=jax.ShapeDtypeStruct((rows, width), jnp.bfloat16),
        compiler_params=pltpu.CompilerParams(vmem_limit_bytes=20 * 1024 * 1024),
        cost_estimate=pl.CostEstimate(
            flops=2 * rows * sum(piece.size for piece in flat),
            bytes_accessed=2 * sum(piece.size for piece in flat) + 2 * rows * width,
            transcendentals=0,
        ),
        name="grad_columns",
    )(*grads, *flat)


def grad_place(grads, slabs, theirs, places, pieces, block):
    rows, width = theirs.shape[0], 2 * theirs.shape[1]
    shape = [[len(slab) for slab in part] for part in slabs]
    flat = [piece for part in slabs for slab in part for piece in slab]
    plane = sum(piece.shape[0] for piece in slabs[0][0])
    if block % 128:
        at = pieces_of(places, pieces, block).reshape(2, -1)
        target = jnp.zeros((rows, width), theirs.dtype)
        return target.at[:, at[0]].set(grad_columns(grads, slabs)).at[:, at[1]].set(theirs)
    return pl.pallas_call(
        functools.partial(grad_place_kernel, shape=shape, plane=plane, block=block),
        grid_spec=pltpu.PrefetchScalarGridSpec(
            num_scalar_prefetch=2,
            grid=(),
            in_specs=[VMEM] * (len(grads) + len(flat) + 1),
            out_specs=VMEM,
        ),
        out_shape=jax.ShapeDtypeStruct((rows, width), jnp.bfloat16),
        compiler_params=pltpu.CompilerParams(vmem_limit_bytes=20 * 1024 * 1024),
        cost_estimate=pl.CostEstimate(
            flops=2 * rows * sum(piece.size for piece in flat),
            bytes_accessed=2 * sum(piece.size for piece in flat) + 3 * rows * width,
            transcendentals=0,
        ),
        name="grad_place",
    )(places, pieces, *grads, *flat, theirs)


def dot(a, b, left, right):
    return lax.dot_general(
        a, b, (((left,), (right,)), ((), ())), preferred_element_type=jnp.float32
    )


def project_kernel(*refs, counts, more):
    count = 2 * len(counts)
    sources, refs = refs[:count], refs[count:]
    pieces, (own_ref, other_ref) = refs[: sum(counts)], refs[-2:]
    for half, target in ((1, other_ref), (0, own_ref)):
        total = refs[sum(counts) + half][...] if more else None
        left = iter(pieces)
        for i, number in enumerate(counts):
            source, at = sources[2 * i + half], 0
            for _ in range(number):
                piece = next(left)
                end = at + piece.shape[0]
                term = dot(source[:, at:end], piece[...], 1, 0)
                total = term if total is None else total + term
                at = end
        target[...] = total


def project_rows(mine, theirs, slabs, before=()):
    rows = mine.shape[0]
    flat = [piece for slab in slabs.values() for piece in slab]
    columns = flat[0].shape[1]
    operands, in_specs = [], []
    for i, slab in slabs.items():
        plane = sum(piece.shape[0] for piece in slab)
        operands += [mine, theirs]
        in_specs += [pl.BlockSpec((rows, plane), lambda _, i=i: (0, i))] * 2
    whole = [*flat, *before]
    in_specs += [pl.BlockSpec(array.shape, lambda _: (0, 0)) for array in whole]
    area = sum(piece.size for piece in flat)
    return pl.pallas_call(
        functools.partial(
            project_kernel, counts=[len(slab) for slab in slabs.values()], more=bool(before)
        ),
        grid=(1,),
        in_specs=in_specs,
        out_specs=[pl.BlockSpec((rows, columns), lambda _: (0, 0))] * 2,
        out_shape=[jax.ShapeDtypeStruct((rows, columns), jnp.float32)] * 2,
        compiler_params=pltpu.CompilerParams(vmem_limit_bytes=24 * 1024 * 1024),
        cost_estimate=pl.CostEstimate(
            flops=4 * rows * area,
            bytes_accessed=2 * area + 4 * rows * area // columns,
            transcendentals=0,
        ),
        name="project_rows",
    )(*operands, *whole)


def attend_kernel(*refs, group, parts, head_dim, scale, last):
    q_own, q_other, grads, cos_ref, sin_ref, row_pos, key_pos = refs[:7]
    pieces = refs[7 : 7 + parts]
    rest = refs[7 + parts :]
    if last:
        before, rest = rest[0], rest[1:]
    attention_ref, grad_ref = rest[:2]
    terms = rest[2:-1]
    held = rest[-1]
    rows = q_own.shape[0]
    for j in range(parts):
        held[j * rows : (j + 1) * rows, :] = pieces[j][...]
    keys, values = held[:, :head_dim], held[:, head_dim:]
    cos, sin = cos_ref[...], sin_ref[...]
    allowed = key_pos[...] <= row_pos[...]
    key_term = value_term = None
    for h in range(group):
        at = slice(h * head_dim, (h + 1) * head_dim)
        q = q_own[:, at] + q_other[:, at]
        q = (q * cos + pltpu.roll(q, head_dim // 2, 1) * sin).astype(jnp.bfloat16)
        scores = jnp.where(allowed, dot(q, keys, 1, 1) * scale, MASKED)
        weight = jnp.exp(scores - jnp.max(scores, axis=1, keepdims=True))
        inverse = 1.0 / jnp.sum(weight, axis=1, keepdims=True)
        attention = (dot(weight.astype(jnp.bfloat16), values, 1, 0) * inverse).astype(jnp.bfloat16)
        attention_ref[:, at] = attention
        grad = grads[:, at]
        delta = jnp.sum(
            grad.astype(jnp.float32) * attention.astype(jnp.float32), axis=1, keepdims=True
        )
        probs = weight * inverse
        dscore = (probs * (dot(grad, values, 1, 1) - delta)).astype(jnp.bfloat16)
        grad_q = dot(dscore, keys, 1, 0) * scale
        grad_q = grad_q * cos - pltpu.roll(grad_q, head_dim // 2, 1) * sin
        grad_ref[:, at] = grad_q.astype(jnp.bfloat16)
        key_new = dot(dscore, q, 0, 0) * scale
        value_new = dot(probs.astype(jnp.bfloat16), grad, 0, 0)
        key_term = key_new if h == 0 else key_term + key_new
        value_term = value_new if h == 0 else value_term + value_new
    if last:
        key_term = key_term + before[:, :head_dim]
        value_term = value_term + before[:, head_dim:]
        for j in range(parts):
            span = slice(j * rows, (j + 1) * rows)
            terms[j][:, :head_dim] = key_term[span].astype(terms[j].dtype)
            terms[j][:, head_dim:] = value_term[span].astype(terms[j].dtype)
    else:
        terms[0][:, :head_dim] = key_term
        terms[0][:, head_dim:] = value_term


def attend(q_own, q_other, grads, cos, sin, row_pos, key_pos, pieces, before, scale):
    rows, columns = q_own.shape
    head_dim = cos.shape[1]
    parts = len(pieces)
    last = before is not None
    keys = parts * rows
    group = columns // head_dim
    if last:
        terms = [jax.ShapeDtypeStruct((rows, 2 * head_dim), jnp.float32)]
        terms += [jax.ShapeDtypeStruct((rows, 2 * head_dim), jnp.bfloat16)] * (parts - 1)
    else:
        terms = [jax.ShapeDtypeStruct((keys, 2 * head_dim), jnp.float32)]
    out_shape = [jax.ShapeDtypeStruct((rows, columns), jnp.bfloat16)] * 2 + terms
    operands = [q_own, q_other, grads, cos, sin, row_pos, key_pos, *pieces]
    operands += [before] if last else []
    out = pl.pallas_call(
        functools.partial(
            attend_kernel, group=group, parts=parts, head_dim=head_dim, scale=scale, last=last
        ),
        in_specs=[VMEM] * len(operands),
        out_specs=[VMEM] * len(out_shape),
        out_shape=out_shape,
        scratch_shapes=[pltpu.VMEM((keys, 2 * head_dim), jnp.bfloat16)],
        compiler_params=pltpu.CompilerParams(vmem_limit_bytes=20 * 1024 * 1024),
        cost_estimate=pl.CostEstimate(
            flops=14 * rows * keys * columns,
            bytes_accessed=8 * keys * 2 * head_dim,
            transcendentals=rows * keys * group,
        ),
        name="attend",
    )(*operands)
    return out[0], out[1], out[2:]


def finish_kernel(own, other, cos_ref, sin_ref, out):
    head_dim = cos_ref.shape[1]
    total = own[...] + other[...]
    key = total[:, :head_dim]
    key = key * cos_ref[...] + pltpu.roll(key, head_dim // 2, 1) * sin_ref[...]
    out[:, :head_dim] = key.astype(jnp.bfloat16)
    out[:, head_dim:] = total[:, head_dim:].astype(jnp.bfloat16)


def finish_keys(own, other, cos, sin):
    return pl.pallas_call(
        finish_kernel,
        in_specs=[VMEM] * 4,
        out_specs=VMEM,
        out_shape=jax.ShapeDtypeStruct(own.shape, jnp.bfloat16),
        name="finish_keys",
    )(own, other, cos, sin)


def undo_kernel(*refs):
    pieces, (cos_ref, sin_ref, out) = refs[:-3], refs[-3:]
    head_dim = cos_ref.shape[1]
    total = pieces[0][...]
    for piece in pieces[1:]:
        total = total + piece[...].astype(jnp.float32)
    key = total[:, :head_dim]
    key = key * cos_ref[...] - pltpu.roll(key, head_dim // 2, 1) * sin_ref[...]
    out[:, :head_dim] = key.astype(jnp.bfloat16)
    out[:, head_dim:] = total[:, head_dim:].astype(jnp.bfloat16)


def undo_keys(pieces, cos, sin):
    return pl.pallas_call(
        undo_kernel,
        in_specs=[VMEM] * (len(pieces) + 2),
        out_specs=VMEM,
        out_shape=jax.ShapeDtypeStruct(pieces[0].shape, jnp.bfloat16),
        name="undo_keys",
    )(*pieces, cos, sin)


def body(tokens, positions, query_weight, key_weight, value_weight, grad_output):
    token_rows = tokens[0]
    rows, width = token_rows.shape
    head_dim = key_weight.shape[1]
    query_width = query_weight.shape[1]
    heads = query_width // head_dim
    group = heads // 2
    scale = head_dim ** (-0.5)
    size_a, size_b, ctx = lax.axis_size("a"), lax.axis_size("b"), lax.axis_size("ctx")
    at_a, at_b = lax.axis_index("a"), lax.axis_index("b")
    core, place = lax.axis_index("core"), lax.axis_index("ctx")
    block = query_weight.shape[0]
    plane = ctx * block

    kv_local = jnp.concatenate([key_weight, value_weight], axis=1).astype(jnp.bfloat16)
    da, db = jnp.meshgrid(jnp.arange(size_a), jnp.arange(size_b), indexing="ij")
    slabs = ((at_a + size_a - da) % size_a) * size_b + (at_b + size_b - db) % size_b
    slabs = slabs.reshape(-1).astype(jnp.int32)
    line = (place + ctx - jnp.arange(ctx)) % ctx
    pieces = jnp.stack([core * ctx + line, (1 - core) * ctx + line]).astype(jnp.int32)
    mine, theirs = pick_columns(token_rows, slabs, pieces, block)
    half = query_width // 2
    q_local = [query_weight[:, g * half : (g + 1) * half].astype(jnp.bfloat16) for g in range(2)]
    pieces_kv = gather_line(kv_local)
    kv_line = jnp.concatenate([after(pieces_kv[0], mine), *pieces_kv[1:]], axis=0)
    theirs = swap(after(theirs, kv_line))

    q_local = [after(local, theirs) for local in q_local]
    q_line = [jnp.concatenate(gather_line(local), axis=0) for local in q_local]
    positions = after(positions, kv_line)
    own_positions = lax.dynamic_slice_in_dim(positions, place * rows, rows)
    cos_table, sin_table = rope_tables(own_positions, head_dim)
    sin_table = jnp.where(jnp.arange(head_dim) < head_dim // 2, -sin_table, sin_table)
    kv_sides = along(kv_line, "a"), along(kv_line, "b")
    stage = kv_sides[0] + kv_sides[1] + q_line[:1] + [cos_table, sin_table]
    kv_corners = gather_corners(*kv_sides, "b", *stage)
    q0_a = along(after(q_line[0], *stage), "a")
    stage = q0_a + [piece for corner in kv_corners.values() for piece in corner]
    q1_a = along(after(q_line[1], *stage), "a")
    q0_b = along(after(q_line[0], *stage), "b")
    kv_slabs = in_order(kv_line, *kv_sides, kv_corners)

    key_positions = jnp.concatenate(
        [
            lax.dynamic_slice_in_dim(positions, ((place + ctx - k) % ctx) * rows, rows)
            for k in range(ctx)
        ]
    )

    def project(slabs, early_part):
        late = {i: slab for i, slab in enumerate(slabs) if (i // size_b) * (i % size_b) > 0}
        own, other = project_rows(mine, theirs, late, early_part)
        return own, swap(other)

    def project_early(slabs, *deps):
        early = {i: slab for i, slab in enumerate(slabs) if (i // size_b) * (i % size_b) == 0}
        early[0] = after_all(early[0], *deps) if deps else early[0]
        return project_rows(mine, theirs, early)

    columns = jnp.concatenate([after(mine, *q0_a), theirs], axis=0)

    def terms_of(own, other):
        both = jnp.concatenate([own, other], axis=0)

        def make(i, part, extra=()):
            start, stop, _ = part.indices(plane)
            at = slice(i * plane + start, i * plane + stop)
            term = mm(columns[:, at], both, ((0,), (0,)))
            for piece in extra:
                term = term + piece.astype(jnp.float32)
            return term.astype(jnp.bfloat16)

        return make

    own, other = project_rows(mine, theirs, dict(enumerate(kv_slabs)))
    key_value = finish_keys(own, swap(other), cos_table, sin_table)
    stage = q1_a + q0_b + [key_value]
    q0_corners = gather_corners(q0_a, q0_b, "a", *stage)
    q1_b = along(after(q_line[1], *stage), "b")
    part = project_early(in_order(q_line[0], q0_a, q0_b, q0_corners))
    key_values = gather_line(key_value)
    stage = q1_b + key_values + [piece for corner in q0_corners.values() for piece in corner]
    q1_corners = gather_corners(q1_a, q1_b, "both", *stage)
    q_slabs = [
        in_order(q_line[0], q0_a, q0_b, q0_corners),
        in_order(q_line[1], q1_a, q1_b, q1_corners),
    ]
    attentions, gradients, made, came = [], [], [], []
    mid = plane // 2
    term = None
    for g in range(2):
        span = slice(g * group * head_dim, (g + 1) * group * head_dim)
        if g == 1:
            part = project_early(q_slabs[1], term)
        own, other = project(q_slabs[g], part)
        if g == 1:
            own = after(own, *came[0][2])
        attention, grad_q, terms = attend(
            own,
            other,
            grad_output[0][:, span],
            cos_table,
            sin_table,
            own_positions[:, None],
            key_positions[None, :],
            key_values,
            term,
            scale,
        )
        term = terms[0]
        attentions.append(attention)
        grads = (grad_q, swap(grad_q))
        gradients.append(grads)
        made.append(terms_of(*grads))
        came.append(reduce_corners(made[g], "ba"[g], mid))
    summed = [terms[0]] + [shift(terms[k], "ctx", -k) for k in range(1, ctx)]
    first = [*came[0][0].values(), *came[0][1].values()]
    second = [*came[1][0].values(), *came[1][1].values()]
    sides0, went0 = reduce_sides(made[0], came[0], "b", mid, *first, *summed[1:-1])
    grad_kv = undo_keys(
        [after(summed[0], *first, *second, *went0), *summed[1:]], cos_table, sin_table
    )
    gradients.append((grad_kv, swap(grad_kv)))
    made.append(terms_of(*gradients[2]))
    came.append(reduce_corners(made[2], "both", mid))
    third = [*came[2][0].values(), *came[2][1].values()]
    sides1, went1 = reduce_sides(made[1], came[1], "a", mid, *sides0)
    line0 = after(made[0](0, slice(None), sides0), *went1)
    sent0 = send_line(line0)
    q_grads = [add_line(sent0, sides1)]
    line1 = made[1](0, slice(None), sides1)
    kv_sides, _ = reduce_sides(made[2], came[2], "both", mid, *sides1, *sent0[1:-1])
    sent1 = send_line(line1)
    q_grads.append(add_line(sent1, kv_sides))

    weights = [*q_slabs, kv_slabs]
    grad_theirs = grad_columns(
        [gradients[0][1], gradients[1][1], after(gradients[2][1], *third)], weights
    )
    grad_theirs = swap(grad_theirs)
    grad_input = grad_place(
        [gradients[0][0], gradients[1][0], gradients[2][0]], weights, grad_theirs, slabs, pieces, block
    )
    kv_term = after(made[2](0, slice(None), kv_sides), q_grads[0], *sent1[1:-1])
    kv_wgrad = add_line(send_line(kv_term), (grad_input,))

    query_grad = jnp.concatenate(q_grads, axis=1)
    key_grad = kv_wgrad[:, :head_dim]
    value_grad = kv_wgrad[:, head_dim:]
    attention_rows = jnp.concatenate(attentions, axis=1)
    return (attention_rows[None], grad_input[None], query_grad, key_grad, value_grad)


def solution(mesh):
    dp, ctx = mesh.devices.shape
    fine = Mesh(mesh.devices.reshape(dp // 4, 2, 2, ctx), ("a", "b", "core", "ctx"))
    batch = P(("a", "b", "core"), "ctx", None)
    master = P(("a", "b", "core", "ctx"), None)
    in_specs = (batch, P(), master, master, master, batch)
    out_specs = (batch, batch, master, master, master)
    return jax.shard_map(body, mesh=fine, in_specs=in_specs, out_specs=out_specs, check_vma=False)
```
